128 devices in a mesh: dp: 16 (over x_lo, z, core), tensor: 8 (over x_hi, y).
Axes of the slice: x: 4 (x_hi: 2, x_lo: 2; x = x_hi * 2 + x_lo), y: 4, z: 4, core: 2. Of those that a mesh axis runs over, the one named last changes fastest.
Arguments:
- tokens: bfloat16 [16384, 1024], P(('dp', 'tensor')), may hold values from -6 to 6
- lengths: int32 [16, 4], P('dp'), may hold values from 1 to 976, as said below
- w_qkv: bfloat16 [2, 1024, 3, 1024], P(None, 'dp', None, 'tensor'), may hold values from -0.1875 to 0.1875
- b_qv: bfloat16 [2, 2, 1024], replicated, may hold values from -3 to 3
- w_out: bfloat16 [2, 1024, 1024], P(None, 'tensor', 'dp'), may hold values from -0.5 to 0.5
- b_out: bfloat16 [2, 1024], replicated, may hold values from -3 to 3
- w_in: bfloat16 [2, 1024, 4096], P(None, 'dp', 'tensor'), may hold values from -0.1875 to 0.1875
- b_in: bfloat16 [2, 4096], replicated, may hold values from -3 to 3
- w_down: bfloat16 [2, 4096, 1024], P(None, 'tensor', 'dp'), may hold values from -0.09375 to 0.09375
- b_down: bfloat16 [2, 1024], replicated, may hold values from -3 to 3
- ln_gain: bfloat16 [2, 2, 1024], replicated, may hold values from 0.5 to 1.5
- ln_bias: bfloat16 [2, 2, 1024], replicated, may hold values from -2 to 2
- cotangent: bfloat16 [16384, 1024], P(('dp', 'tensor')), may hold values from -6 to 6
Outputs:
- encoded: bfloat16 [16384, 1024], P(('dp', 'tensor'))
- g_tokens: bfloat16 [16384, 1024], P(('dp', 'tensor'))
- g_w_qkv: float32 [2, 1024, 3, 1024], P(None, 'dp', None, 'tensor')
- g_b_qv: float32 [2, 2, 1024], replicated
- g_w_out: float32 [2, 1024, 1024], P(None, 'tensor', 'dp')
- g_b_out: float32 [2, 1024], replicated
- g_w_in: float32 [2, 1024, 4096], P(None, 'dp', 'tensor')
- g_b_in: float32 [2, 4096], replicated
- g_w_down: float32 [2, 4096, 1024], P(None, 'tensor', 'dp')
- g_b_down: float32 [2, 1024], replicated
- g_ln_gain: float32 [2, 2, 1024], replicated
- g_ln_bias: float32 [2, 2, 1024], replicated
The draws below stay inside these ranges and needn't reach their ends.
Inputs may be any that keep to these rules, and one draw needn't show every extreme that they name: In each data shard exactly one sequence, at a place drawn from the seed, is long: between 897 and 976 tokens, with exactly 976 in some shard; the others have at most 16 tokens each. A shard's lengths sum to at most 1024.
All inputs are finite; a program needn't handle non-finite values.
Results may differ from the reference program's by a relative error of at most 0.028.
Values may be sent and summed in bfloat16 or wider, within the bound.
A program may use at most 128 MiB of HBM per device.

```python
from functools import partial
import jax
import jax.numpy as jnp
from jax import lax

D = 1024
H = 16
DH = 64
FF = 4096
TOK_DEV = 128
SEQS = 4
LAYERS = 2
ROWS = 1024
TOKENS = 16384
MAXLEN = 976


def draw_lengths(key, part):
    key = jax.random.fold_in(key, 7)
    subkeys = jax.random.split(key, 4)
    shards = TOKENS // ROWS
    short_cap = TOK_DEV // 8
    shorts = jax.random.randint(subkeys[0], (shards, SEQS - 1), 1, short_cap + 1)
    longest = jax.random.randint(subkeys[1], (shards,), ROWS - TOK_DEV + 1, MAXLEN + 1)
    chosen = jax.random.randint(subkeys[2], (), 0, shards)
    longest = jnp.where(jnp.arange(shards) == chosen, MAXLEN, longest)
    long_place = jax.random.randint(subkeys[3], (shards, 1), 0, SEQS)
    columns = jnp.arange(SEQS)[None, :]
    short_index = jnp.clip(columns - (columns > long_place).astype(jnp.int32), 0, SEQS - 2)
    picked = jnp.take_along_axis(shorts, short_index, axis=1)
    return jnp.where(columns == long_place, longest[:, None], picked).astype(jnp.int32)


def shard_levels(own_key, dims, cuts, least, high):
    loudness, own = 1.0, jax.random.fold_in(own_key, 6)
    for position, parts in cuts:
        heights = jnp.exp(jax.random.uniform(jax.random.fold_in(own, position), (parts,), jnp.float32, least / len(cuts), high / len(cuts)))
        loudness = loudness * jnp.repeat(heights, dims[position] // parts).reshape([-1 if axis == position else 1 for axis in range(len(dims))])
    return loudness


def centred(stream_key, shape, scale, bound, pieces=(), kind=jnp.bfloat16):
    values = jax.random.normal(stream_key, shape, jnp.float32) * scale
    if len(pieces) > 0:
        values = shard_levels(stream_key, shape, pieces, -0.22, 0.18) * values
    return jnp.clip(values, min=-bound, max=bound).astype(kind)


def setup_inputs(seed: int = 0) -> dict:
    keys = jax.random.split(jax.random.key(seed), 14)
    tokens = centred(keys[0], (TOKENS, D), 1.0, 6.0, ((0, 128),))
    lengths = draw_lengths(jax.random.fold_in(keys[13], 71), 0)
    w_qkv = centred(keys[2], (LAYERS, D, 3, D), D ** -0.5, 0.1875, ((1, 16), (3, 8)))
    b_qv = centred(keys[3], (LAYERS, 2, D), 0.5, 3.0)
    w_out = centred(keys[4], (LAYERS, D, D), (D // 8) ** -0.5, 0.5, ((1, 8), (2, 16)))
    b_out = centred(keys[5], (LAYERS, D), 0.5, 3.0)
    w_in = centred(keys[6], (LAYERS, D, FF), D ** -0.5, 0.1875, ((1, 16), (2, 8)))
    b_in = centred(keys[7], (LAYERS, FF), 0.5, 3.0)
    w_down = centred(keys[8], (LAYERS, FF, D), FF ** -0.5, 0.09375, ((1, 8), (2, 16)))
    b_down = centred(keys[9], (LAYERS, D), 0.5, 3.0)
    ln_gain = jnp.clip(1.0 + 0.1 * jax.random.normal(keys[10], (LAYERS, 2, D), jnp.float32), 0.5, 1.5).astype(jnp.bfloat16)
    ln_bias = centred(keys[11], (LAYERS, 2, D), 0.3, 2.0)
    cotangent = centred(keys[12], (TOKENS, D), 1.0, 6.0, ((0, 128),))
    return {"tokens": tokens, "lengths": lengths, "w_qkv": w_qkv, "b_qv": b_qv, "w_out": w_out, "b_out": b_out, "w_in": w_in, "b_in": b_in, "w_down": w_down, "b_down": b_down, "ln_gain": ln_gain, "ln_bias": ln_bias, "cotangent": cotangent}


@jax.custom_vjp
def low(v):
    return lax.optimization_barrier(v.astype(jnp.bfloat16)).astype(jnp.float32)

@jax.custom_vjp
def low_back(v):
    return v

def low_keep(v):
    return (low(v), None)

def low_pass(kept, grad):
    return (grad,)

def back_keep(v):
    return (v, None)

def back_low(kept, grad):
    return (low(grad),)
low.defvjp(low_keep, low_pass)
low_back.defvjp(back_keep, back_low)
EPSILON = 1e-06
HIGH = lax.Precision.HIGHEST

def layer_norm(stream, gain_vec, bias_vec):
    row_mean = lax.optimization_barrier(jnp.mean(stream, axis=-1, keepdims=True))
    centered = stream - row_mean
    row_var = lax.optimization_barrier(jnp.mean(centered * centered, axis=-1, keepdims=True))
    return centered * lax.rsqrt(row_var + EPSILON) * gain_vec + bias_vec

def segment_ids(shard_lengths):
    seq_ends = jnp.cumsum(shard_lengths).astype(jnp.int32)
    positions = jnp.arange(ROWS, dtype=jnp.int32)
    segments = lax.optimization_barrier(jnp.sum((positions[:, None] >= seq_ends[None, :]).astype(jnp.int32), axis=1)).astype(jnp.int32)
    return jnp.where(segments == SEQS, SEQS + positions, segments)

def head_attention(queries, keys_in, values_in, allowed):
    scores = low_back(jnp.dot(queries, keys_in.T, precision=HIGH) * DH ** (-0.5))
    scores = jnp.where(allowed, scores, -1e+30)
    row_peak = lax.optimization_barrier(jnp.max(scores, axis=-1, keepdims=True))
    exp_scores = jnp.exp(scores - row_peak)
    attn_probs = low(exp_scores / lax.optimization_barrier(jnp.sum(exp_scores, axis=-1, keepdims=True)))
    return jnp.dot(attn_probs, values_in, precision=HIGH)

def encoder(stream, w_qkv, b_qv, w_out, b_out, w_in, b_in, w_down, b_down, ln_gain, ln_bias, allowed):
    attend = jax.checkpoint(partial(head_attention, allowed=allowed))
    hidden = stream
    for layer_at in range(LAYERS):
        attn_input = low(hidden)
        qkv = jnp.einsum('rd,dcj->rcj', attn_input, w_qkv[layer_at], precision=HIGH)
        bias_all = jnp.stack([b_qv[layer_at, 0], jnp.zeros_like(b_qv[layer_at, 0]), b_qv[layer_at, 1]])
        qkv = low(low_back(qkv + bias_all))
        head_view = qkv.reshape(ROWS, 3, H, DH).transpose(1, 2, 0, 3)
        context = lax.map(lambda triple: attend(triple[0], triple[1], triple[2]), (head_view[0], head_view[1], head_view[2]))
        context = low(low_back(context.transpose(1, 0, 2).reshape(ROWS, D)))
        branch = low_back(jnp.dot(context, w_out[layer_at], precision=HIGH) + b_out[layer_at])
        normed = layer_norm(hidden + branch, ln_gain[layer_at, 0], ln_bias[layer_at, 0])
        mlp_input = low(normed)
        pre_gelu = low_back(jnp.dot(mlp_input, w_in[layer_at], precision=HIGH) + b_in[layer_at])
        activated = low(jax.nn.gelu(pre_gelu, approximate=False))
        branch = low_back(jnp.dot(activated, w_down[layer_at], precision=HIGH) + b_down[layer_at])
        hidden = layer_norm(normed + branch, ln_gain[layer_at, 1], ln_bias[layer_at, 1])
    return hidden

def reference(tokens, lengths, w_qkv, b_qv, w_out, b_out, w_in, b_in, w_down, b_down, ln_gain, ln_bias, cotangent):
    params = tuple((array.astype(jnp.float32) for array in (w_qkv, b_qv, w_out, b_out, w_in, b_in, w_down, b_down, ln_gain, ln_bias)))
    rows_in = tokens.astype(jnp.float32).reshape(-1, ROWS, D)
    rows_grad = cotangent.astype(jnp.float32).reshape(-1, ROWS, D)

    def shard_step(totals, shard_item):
        shard_rows, shard_grad, shard_lengths = shard_item
        segments = segment_ids(shard_lengths)
        allowed = segments[:, None] == segments[None, :]

        def forward(stream, *weights):
            return encoder(stream, *weights, allowed)
        encoded_rows, pullback = jax.vjp(forward, shard_rows, *params)
        gradients = pullback(shard_grad)
        totals = tuple((total + grad_part for total, grad_part in zip(totals, gradients[1:])))
        return (totals, (encoded_rows, gradients[0]))
    zero_grads = tuple((jnp.zeros_like(array) for array in params))
    totals, (encoded_all, input_grads) = lax.scan(shard_step, zero_grads, (rows_in, rows_grad, lengths))
    encoded = encoded_all.reshape(TOKENS, D).astype(jnp.bfloat16)
    g_tokens = input_grads.reshape(TOKENS, D).astype(jnp.bfloat16)
    return (encoded, g_tokens, totals[0], totals[1], totals[2], totals[3], totals[4], totals[5], totals[6], totals[7], totals[8], totals[9])
```

```python
import functools

import jax
import jax.numpy as jnp
from jax import lax
from jax.experimental import pallas as pl
from jax.experimental.pallas import tpu as pltpu
from jax.sharding import PartitionSpec as P

DH = 64
EPSILON = 1e-06
MESH = pl.DeviceIdType.MESH
F32 = jnp.float32
BF16 = jnp.bfloat16


def place():
    dp, tensor = lax.axis_index("dp"), lax.axis_index("tensor")
    core = lax.rem(dp, 2)
    z = lax.rem(lax.div(dp, 2), 4)
    x = lax.rem(lax.div(tensor, 4) * 2 + lax.div(dp, 8), 4)
    y = lax.rem(tensor, 4)
    return x, y, z, core


def device(x, y, z, core):
    x, y, z = lax.rem(x, 4), lax.rem(y, 4), lax.rem(z, 4)
    return (lax.rem(x, 2) * 8 + z * 2 + core, lax.div(x, 2) * 4 + y)


def block_of(x, z):
    x, z = lax.rem(x, 4), lax.rem(z, 4)
    return lax.rem(x, 2) * 8 + z * 2 + lax.div(x, 2)


def greet(devices):
    barrier = pltpu.get_barrier_semaphore()
    for other in devices:
        pl.semaphore_signal(barrier, inc=1, device_id=other, device_id_type=MESH)
    pl.semaphore_wait(barrier, len(devices))


class Copies:
    def __init__(self, send, recv):
        self.send, self.recv, self.started = send, recv, []

    def start(self, src, dst, to):
        at = len(self.started)
        copy = pltpu.make_async_remote_copy(
            src_ref=src,
            dst_ref=dst,
            send_sem=self.send.at[at],
            recv_sem=self.recv.at[at],
            device_id=to,
            device_id_type=MESH,
        )
        copy.start()
        self.started.append(copy)
        return copy

    def wait_sends(self):
        for copy in self.started:
            copy.wait_send()


def group_neighbours():
    x, y, z, core = place()
    return (
        device(x, y, z, 1 - core),
        device(x, y + 1, z, core),
        device(x, y + 3, z, core),
    )


GATHER_COPIES = 12
SCATTER_COPIES = 10


def gather_group(copies, out):
    x, y, z, core = place()
    pair, after, before = group_neighbours()
    half = out.shape[1] // 2
    top, low = pl.ds(0, half), pl.ds(half, half)
    here = core * 4

    def part(step, rows):
        return out.at[here + lax.rem(y + step, 4), rows]

    def send(step, rows, to):
        return copies.start(part(step, rows), part(step, rows), to)

    top_after = send(0, top, after)
    low_before = send(0, low, before)
    low_after = send(0, low, after)
    top_before = send(0, top, before)
    everything = pl.ds(0, 2 * half)
    own_pair = send(0, everything, pair)
    top_after.wait_recv()
    far_top = send(3, top, after)
    low_before.wait_recv()
    far_low = send(1, low, before)
    low_after.wait_recv()
    pair_before = send(3, everything, pair)
    top_before.wait_recv()
    pair_after = send(1, everything, pair)
    far_top.wait_recv()
    pair_top = send(2, top, pair)
    far_low.wait_recv()
    pair_low = send(2, low, pair)
    for copy in (own_pair, pair_before, pair_after, pair_top, pair_low):
        copy.wait_recv()


def scatter_group(copies, part, from_pair, staged, far, near):
    x, y, z, core = place()
    pair, after, before = group_neighbours()
    half = part.shape[1] // 2
    top, low = pl.ds(0, half), pl.ds(half, half)
    here, there = core * 4, (1 - core) * 4
    steps = (2, 1, 3, 0)
    swaps = [
        copies.start(part.at[there + lax.rem(y + step, 4)], from_pair.at[slot], pair)
        for slot, step in enumerate(steps)
    ]

    def chip(slot, rows):
        own = part[here + lax.rem(y + steps[slot], 4), rows].astype(F32)
        return own + from_pair[slot, rows].astype(F32)

    swaps[0].wait_recv()
    staged[0, top] = chip(0, top).astype(BF16)
    far_top = copies.start(staged.at[0, top], far.at[top], after)
    staged[0, low] = chip(0, low).astype(BF16)
    far_low = copies.start(staged.at[0, low], far.at[low], before)
    swaps[1].wait_recv()
    staged[1, low] = chip(1, low).astype(BF16)
    low_after = copies.start(staged.at[1, low], near.at[0, low], after)
    swaps[2].wait_recv()
    staged[2, top] = chip(2, top).astype(BF16)
    top_before = copies.start(staged.at[2, top], near.at[1, top], before)
    far_top.wait_recv()
    staged[1, top] = (chip(1, top) + far[top].astype(F32)).astype(BF16)
    top_after = copies.start(staged.at[1, top], near.at[0, top], after)
    far_low.wait_recv()
    staged[2, low] = (chip(2, low) + far[low].astype(F32)).astype(BF16)
    low_before = copies.start(staged.at[2, low], near.at[1, low], before)
    swaps[3].wait_recv()
    own = chip(3, pl.ds(0, 2 * half))
    for copy in (low_after, top_before, top_after, low_before):
        copy.wait_recv()
    return own + near[0].astype(F32) + near[1].astype(F32)


def scatter_scratch(rows, width):
    return [
        pltpu.VMEM((4, rows, width), BF16),
        pltpu.VMEM((3, rows, width), BF16),
        pltpu.VMEM((rows, width), BF16),
        pltpu.VMEM((2, rows, width), BF16),
    ]


def sems(count):
    return [pltpu.SemaphoreType.DMA((count,)), pltpu.SemaphoreType.DMA((count,))]


def plane_ring(axis):
    x, y, z, core = place()
    if axis == "x":
        return device(x + 1, y, z, core), device(x + 3, y, z, core)
    return device(x, y, z + 1, core), device(x, y, z + 3, core)


def plane_at(first, u, v):
    return block_of(u, v) if first == "x" else block_of(v, u)


PLANE_GATHER_COPIES = 36
PLANE_SCATTER_COPIES = 36


def gather_plane(copies, out):
    x, y, z, core = place()
    quarter = out.shape[1] // 4
    paths = []
    for first, base in (("x", 0), ("z", 2 * quarter)):
        v, u = (x, z) if first == "x" else (z, x)
        other = "z" if first == "x" else "x"
        paths.append(
            dict(
                first=first,
                v=v,
                u=u,
                ring=plane_ring(first),
                cross=plane_ring(other),
                halves=(pl.ds(base, quarter), pl.ds(base + quarter, quarter)),
                whole=pl.ds(base, 2 * quarter),
            )
        )

    def send(path, dv, du, rows, to):
        at = plane_at(path["first"], path["v"] + dv, path["u"] + du)
        return copies.start(out.at[at, rows], out.at[at, rows], to)

    for path in paths:
        after, before = path["ring"]
        top, low = path["halves"]
        path["ta"] = send(path, 0, 0, top, after)
        path["lb"] = send(path, 0, 0, low, before)
        path["la"] = send(path, 0, 0, low, after)
        path["tb"] = send(path, 0, 0, top, before)
        path["c"] = {0: [send(path, 0, 0, path["whole"], to) for to in path["cross"]]}
    for path in paths:
        path["ta"].wait_recv()
        path["ft"] = send(path, 3, 0, path["halves"][0], path["ring"][0])
        path["lb"].wait_recv()
        path["fl"] = send(path, 1, 0, path["halves"][1], path["ring"][1])
    for path in paths:
        path["la"].wait_recv()
        path["c"][3] = [send(path, 3, 0, path["whole"], to) for to in path["cross"]]
        path["tb"].wait_recv()
        path["c"][1] = [send(path, 1, 0, path["whole"], to) for to in path["cross"]]
    last = []
    for path in paths:
        path["c"][0][0].wait_recv()
        last.append(send(path, 0, 3, path["whole"], path["cross"][0]))
    for path in paths:
        path["ft"].wait_recv()
        path["fl"].wait_recv()
        path["c"][2] = [send(path, 2, 0, path["whole"], to) for to in path["cross"]]
    for path in paths:
        path["c"][3][0].wait_recv()
        last.append(send(path, 3, 3, path["whole"], path["cross"][0]))
        path["c"][1][1].wait_recv()
        last.append(send(path, 1, 1, path["whole"], path["cross"][1]))
    for path in paths:
        path["c"][2][1].wait_recv()
        last.append(send(path, 2, 1, path["whole"], path["cross"][1]))
    for path in paths:
        for copy in (path["c"][0][1], path["c"][3][1], path["c"][1][0], path["c"][2][0]):
            copy.wait_recv()
    for copy in last:
        copy.wait_recv()


def scatter_plane_scratch(rows, width):
    half = rows // 2
    return [
        pltpu.VMEM((2, 4, half, width), BF16),
        pltpu.VMEM((2, 2, 4, half, width), BF16),
        pltpu.VMEM((2, 4, half, width), BF16),
        pltpu.VMEM((2, 4, half, width), BF16),
        pltpu.VMEM((2, half, width), BF16),
        pltpu.VMEM((2, 2, half, width), BF16),
        pltpu.VMEM((2, 2, half // 2, width), BF16),
    ]


def scatter_plane(copies, part, out, far, near, passed, summed, far2, near2, passed2):
    x, y, z, core = place()
    half = part.shape[1] // 2
    quarter = half // 2
    paths = []
    for at, (first, base) in enumerate((("x", 0), ("z", half))):
        u, v = (x, z) if first == "x" else (z, x)
        other = "z" if first == "x" else "x"
        paths.append(
            dict(
                at=at,
                first=first,
                u=u,
                v=v,
                ring=plane_ring(first),
                cross=plane_ring(other),
                rows=pl.ds(base, half),
                base=base,
            )
        )

    def source(path, du, v):
        return (plane_at(path["first"], path["u"] + du, v), path["rows"])

    for path in paths:
        at, (after, before) = path["at"], path["ring"]
        path["far"] = [
            copies.start(
                part.at[source(path, 2, v)], far.at[at, v], after if v < 2 else before
            )
            for v in range(4)
        ]
    for path in paths:
        at, (after, before) = path["at"], path["ring"]
        path["near"] = [
            copies.start(part.at[source(path, 1, v)], near.at[at, 0, v], after) for v in (2, 3)
        ] + [
            copies.start(part.at[source(path, 3, v)], near.at[at, 1, v], before) for v in (0, 1)
        ]
    for path in paths:
        at, (after, before) = path["at"], path["ring"]
        for v in (0, 2, 1, 3):
            path["far"][v].wait_recv()
            du, slot, to = (1, 0, after) if v < 2 else (3, 1, before)
            own = part[source(path, du, v)].astype(F32)
            passed[at, v] = (own + far[at, v].astype(F32)).astype(BF16)
            path["near"].append(copies.start(passed.at[at, v], near.at[at, slot, v], to))
    for path in paths:
        at = path["at"]
        for copy in path["near"]:
            copy.wait_recv()
        for v in range(4):
            own = part[source(path, 0, v)].astype(F32)
            summed[at, v] = (
                own + near[at, 0, v].astype(F32) + near[at, 1, v].astype(F32)
            ).astype(BF16)
        v, (after, before) = path["v"], path["cross"]
        top, low = pl.ds(0, quarter), pl.ds(quarter, quarter)
        v1, v2, v3 = lax.rem(v + 1, 4), lax.rem(v + 2, 4), lax.rem(v + 3, 4)
        path["ft"] = copies.start(summed.at[at, v2, top], far2.at[at, top], after)
        path["fl"] = copies.start(summed.at[at, v2, low], far2.at[at, low], before)
        path["last"] = [
            copies.start(summed.at[at, v1, low], near2.at[at, 0, low], after),
            copies.start(summed.at[at, v3, top], near2.at[at, 1, top], before),
        ]
    for path in paths:
        at, v, (after, before) = path["at"], path["v"], path["cross"]
        top, low = pl.ds(0, quarter), pl.ds(quarter, quarter)
        v1, v3 = lax.rem(v + 1, 4), lax.rem(v + 3, 4)
        path["ft"].wait_recv()
        passed2[at, 0] = (summed[at, v1, top].astype(F32) + far2[at, top].astype(F32)).astype(BF16)
        path["last"].append(copies.start(passed2.at[at, 0], near2.at[at, 0, top], after))
        path["fl"].wait_recv()
        passed2[at, 1] = (summed[at, v3, low].astype(F32) + far2[at, low].astype(F32)).astype(BF16)
        path["last"].append(copies.start(passed2.at[at, 1], near2.at[at, 1, low], before))
    for path in paths:
        at, v = path["at"], path["v"]
        for copy in path["last"]:
            copy.wait_recv()
        total = summed[at, v].astype(F32) + near2[at, 0].astype(F32) + near2[at, 1].astype(F32)
        out[path["rows"]] = total


def params(number):
    return pltpu.CompilerParams(
        collective_id=number, has_side_effects=True, vmem_limit_bytes=48 * 2**20
    )


VMEM = pl.BlockSpec(memory_space=pltpu.VMEM)


def start_kernel(tokens, weights, rows_out, weights_out, send, recv, wsend, wrecv):
    x, y, z, core = place()
    greet([*group_neighbours(), *plane_ring("x"), *plane_ring("z")])
    weights_out[block_of(x, z)] = weights[...]
    rows_out[core * 4 + y] = tokens[...]
    plane, group = Copies(wsend, wrecv), Copies(send, recv)
    gather_group(group, rows_out)
    gather_plane(plane, weights_out)
    group.wait_sends()
    plane.wait_sends()


def start(tokens, weights):
    rows, width = tokens.shape
    held, columns = weights.shape
    gathered, full = pl.pallas_call(
        start_kernel,
        out_shape=(
            jax.ShapeDtypeStruct((8, rows, width), BF16),
            jax.ShapeDtypeStruct((16, held, columns), BF16),
        ),
        in_specs=[VMEM] * 2,
        out_specs=(VMEM, VMEM),
        scratch_shapes=sems(GATHER_COPIES) + sems(PLANE_GATHER_COPIES),
        compiler_params=params(0),
        name="start",
    )(tokens, weights)
    return gathered.reshape(8 * rows, width), full.reshape(16 * held, columns)


def normed_parts(stream):
    row_mean = jnp.mean(stream, axis=-1, keepdims=True)
    centered = stream - row_mean
    row_var = jnp.mean(centered * centered, axis=-1, keepdims=True)
    scale = lax.rsqrt(row_var + EPSILON)
    return centered * scale, scale


def norm_pull(unit, scale, gain, grad, sums):
    scaled = grad * gain
    inner = jnp.mean(scaled * unit, axis=-1, keepdims=True)
    pulled = scale * (scaled - jnp.mean(scaled, axis=-1, keepdims=True) - unit * inner)
    low = pulled.astype(BF16)
    sums[0:1] = jnp.sum(grad * unit, axis=0, keepdims=True)
    sums[1:2] = jnp.sum(grad, axis=0, keepdims=True)
    sums[2:3] = jnp.sum(low.astype(F32), axis=0, keepdims=True)
    return pulled, low


def forward_kernel(
    part, held, vectors, stream_out, normed_out, rows_out,
    from_pair, staged, far, near, send, recv, gsend, grecv,
):
    x, y, z, core = place()
    greet(group_neighbours())
    scatter, gather = Copies(send, recv), Copies(gsend, grecv)
    total = scatter_group(scatter, part, from_pair, staged, far, near)
    stream = held[...] + total + vectors[0:1]
    stream_out[...] = stream
    unit, _ = normed_parts(stream)
    normed = unit * vectors[1:2] + vectors[2:3]
    normed_out[...] = normed
    rows_out[core * 4 + y] = normed.astype(BF16)
    gather_group(gather, rows_out)
    scatter.wait_sends()
    gather.wait_sends()


def turn_kernel(
    part, held, vectors, grad, encoded_out, pulled_out, sums_out, rows_out,
    from_pair, staged, far, near, send, recv, gsend, grecv,
):
    x, y, z, core = place()
    greet(group_neighbours())
    scatter, gather = Copies(send, recv), Copies(gsend, grecv)
    total = scatter_group(scatter, part, from_pair, staged, far, near)
    stream = held[...] + total + vectors[0:1]
    unit, scale = normed_parts(stream)
    encoded_out[...] = (unit * vectors[1:2] + vectors[2:3]).astype(BF16)
    pulled, low = norm_pull(unit, scale, vectors[1:2], grad[...].astype(F32), sums_out)
    pulled_out[...] = pulled
    rows_out[core * 4 + y] = low
    gather_group(gather, rows_out)
    scatter.wait_sends()
    gather.wait_sends()


def backward_kernel(
    part, held, vectors, stream, pulled_out, sums_out, rows_out,
    from_pair, staged, far, near, send, recv, gsend, grecv,
):
    x, y, z, core = place()
    greet(group_neighbours())
    scatter, gather = Copies(send, recv), Copies(gsend, grecv)
    total = scatter_group(scatter, part, from_pair, staged, far, near)
    unit, scale = normed_parts(stream[...])
    pulled, low = norm_pull(unit, scale, vectors[1:2], held[...] + total, sums_out)
    pulled_out[...] = pulled
    rows_out[core * 4 + y] = low
    gather_group(gather, rows_out)
    scatter.wait_sends()
    gather.wait_sends()


def group_call(kernel, number, name, operands, outs):
    part = operands[0]
    rows, width = part.shape[0] // 8, part.shape[1]
    shapes = tuple(jax.ShapeDtypeStruct(shape, kind) for shape, kind in outs)
    shapes += (jax.ShapeDtypeStruct((8, rows, width), BF16),)
    results = pl.pallas_call(
        kernel,
        out_shape=shapes,
        in_specs=[VMEM] * len(operands),
        out_specs=(VMEM,) * len(shapes),
        scratch_shapes=scatter_scratch(rows, width)
        + sems(SCATTER_COPIES)
        + sems(GATHER_COPIES),
        compiler_params=params(number),
        name=name,
    )(part.reshape(8, rows, width), *operands[1:])
    return (*results[:-1], results[-1].reshape(8 * rows, width))


def end_kernel(
    part, held, grads, rows_out, grads_out,
    from_pair, staged, far, near, pfar, pnear, passed, summed, far2, near2, passed2,
    send, recv, psend, precv,
):
    greet([*group_neighbours(), *plane_ring("x"), *plane_ring("z")])
    group, plane = Copies(send, recv), Copies(psend, precv)
    total = scatter_group(group, part, from_pair, staged, far, near)
    rows_out[...] = (held[...] + total).astype(BF16)
    scatter_plane(plane, grads, grads_out, pfar, pnear, passed, summed, far2, near2, passed2)
    group.wait_sends()
    plane.wait_sends()


def end(part, held, grads):
    rows, width = held.shape
    kept, columns = grads.shape[0] // 16, grads.shape[1]
    return pl.pallas_call(
        end_kernel,
        out_shape=(
            jax.ShapeDtypeStruct((rows, width), BF16),
            jax.ShapeDtypeStruct((kept, columns), F32),
        ),
        in_specs=[VMEM] * 3,
        out_specs=(VMEM, VMEM),
        scratch_shapes=scatter_scratch(rows, width)
        + scatter_plane_scratch(kept, columns)
        + sems(SCATTER_COPIES)
        + sems(PLANE_SCATTER_COPIES),
        compiler_params=params(4),
        name="end",
    )(part.reshape(8, rows, width), held, grads.reshape(16, kept, columns))


def segment_ids(shard_lengths, total_rows, seq_count):
    seq_ends = jnp.cumsum(shard_lengths)
    positions = jnp.arange(total_rows, dtype=jnp.int32)
    segments = jnp.sum((positions[:, None] >= seq_ends[None, :]).astype(jnp.int32), axis=1)
    return jnp.where(segments == seq_count, seq_count + positions, segments)


def masked_scores(queries, keys_in, allowed, score_scale):
    scores = (
        jnp.einsum("qhd,khd->hqk", queries, keys_in, preferred_element_type=jnp.float32)
        * score_scale
    )
    return jnp.where(allowed[None], scores, -1e30)


def attend_forward(queries, keys_in, values_in, allowed, score_scale):
    scores = masked_scores(queries, keys_in, allowed, score_scale)
    row_peak = jnp.max(scores, axis=-1, keepdims=True)
    exp_scores = jnp.exp(scores - row_peak)
    row_total = jnp.sum(exp_scores, axis=-1, keepdims=True)
    attn_probs = (exp_scores / row_total).astype(jnp.bfloat16)
    context = jnp.einsum("hqk,khd->qhd", attn_probs, values_in, preferred_element_type=jnp.float32)
    return (context, row_peak + jnp.log(row_total))


def attend_backward(queries, keys_in, values_in, allowed, score_scale, log_total, grad_context):
    scores = masked_scores(queries, keys_in, allowed, score_scale)
    attn_probs = jnp.exp(scores - log_total)
    probs_low = attn_probs.astype(jnp.bfloat16)
    grad_probs = jnp.einsum(
        "qhd,khd->hqk", grad_context, values_in, preferred_element_type=jnp.float32
    )
    grad_values = jnp.einsum(
        "hqk,qhd->khd", probs_low, grad_context, preferred_element_type=jnp.float32
    )
    row_inner = jnp.sum(attn_probs * grad_probs, axis=-1, keepdims=True)
    grad_scores = (attn_probs * (grad_probs - row_inner)).astype(jnp.bfloat16)
    grad_queries = (
        jnp.einsum("hqk,khd->qhd", grad_scores, keys_in, preferred_element_type=jnp.float32)
        * score_scale
    )
    grad_keys = (
        jnp.einsum("hqk,qhd->khd", grad_scores, queries, preferred_element_type=jnp.float32)
        * score_scale
    )
    return (grad_queries, grad_keys, grad_values)


def exact_gelu(values):
    return jax.nn.gelu(values, approximate=False)


CONTRACT_LAST = (((1,), (1,)), ((), ()))
CONTRACT_FIRST = (((0,), (0,)), ((), ()))


def flat(x, y, z, core):
    return (x % 2 * 8 + z * 2 + core) * 8 + x // 2 * 4 + y


CHIPS = [(x, y, z, core) for x in range(4) for y in range(4) for z in range(4) for core in (0, 1)]
SWAP = [
    (flat(x, y, z, core), flat(core * 2 + x % 2, y, z, x // 2)) for x, y, z, core in CHIPS
]
PLANES = [
    [flat(xh * 2 + xl, y, z, core) for xl in (0, 1) for z in range(4) for xh in (0, 1)]
    for core in (0, 1)
    for y in range(4)
]
AXES = ("dp", "tensor")


def swap(values):
    return lax.ppermute(values, AXES, SWAP)


def shards(
    tokens,
    lengths,
    w_qkv,
    b_qv,
    w_out,
    b_out,
    w_in,
    b_in,
    w_down,
    b_down,
    ln_gain,
    ln_bias,
    cotangent,
):
    x, y, z, core = place()
    column = core * 4 + y
    own_rows, width = tokens.shape
    total_rows = own_rows * 8
    layers, kept = w_qkv.shape[:2]
    col_width = w_qkv.shape[3]
    hidden_width = w_in.shape[2]
    head_count = col_width // DH
    score_scale = DH ** (-0.5)
    cuts = (0, 3 * col_width, 4 * col_width, 4 * col_width + hidden_width)

    packed = [
        jnp.concatenate(
            [
                w_qkv[at].reshape(kept, 3 * col_width),
                w_out[at].T,
                w_in[at],
                w_down[at].T,
            ],
            axis=1,
        )
        for at in range(layers)
    ]
    first_weights = swap(packed[0])
    tokens = swap(tokens)
    lengths = swap(lengths)
    later_weights = swap(packed[1])
    cotangent = swap(cotangent)
    attn_input, full = start(tokens, first_weights)
    later = lax.all_gather(later_weights, AXES, axis_index_groups=PLANES, axis=0, tiled=True)
    weights = [full, later]

    segments = segment_ids(lengths[0], total_rows, lengths.shape[1])
    allowed = segments[:, None] == segments[None, :]

    def pieces(packed_weights):
        return (
            packed_weights[:, cuts[0] : cuts[1]],
            packed_weights[:, cuts[1] : cuts[2]],
            packed_weights[:, cuts[2] : cuts[3]],
            packed_weights[:, cuts[3] :],
        )

    def vectors(bias, at, which):
        rows = [bias.astype(F32), ln_gain[at, which].astype(F32), ln_bias[at, which].astype(F32)]
        return jnp.stack(rows + [jnp.zeros_like(rows[0])] * 5)

    row_kind = ((own_rows, width), F32)
    sum_kind = ((8, width), F32)
    low_kind = ((own_rows, width), BF16)
    hidden = tokens.astype(F32)
    stored = []
    for at in range(layers):
        full_qkv, full_out, full_in, full_down = pieces(weights[at])
        bias_qv = lax.dynamic_slice_in_dim(
            b_qv[at].astype(F32), column * col_width, col_width, 1
        )
        bias_all = jnp.concatenate([bias_qv[0], jnp.zeros_like(bias_qv[0]), bias_qv[1]])
        qkv = jnp.dot(attn_input, full_qkv, preferred_element_type=F32)
        qkv_low = (qkv + bias_all).astype(BF16)
        head_view = qkv_low.reshape(total_rows, 3, head_count, DH)
        context, log_total = attend_forward(
            head_view[:, 0], head_view[:, 1], head_view[:, 2], allowed, score_scale
        )
        context_low = context.reshape(total_rows, col_width).astype(BF16)
        branch = lax.dot_general(
            context_low, full_out, CONTRACT_LAST, preferred_element_type=F32
        ).astype(BF16)
        first_vectors = vectors(b_out[at], at, 0)
        first_sum, normed, mlp_input = group_call(
            forward_kernel, 1, "forward", (branch, hidden, first_vectors), (row_kind, row_kind)
        )
        bias_in = lax.dynamic_slice_in_dim(
            b_in[at].astype(F32), column * hidden_width, hidden_width, 0
        )
        pre_gelu = jnp.dot(mlp_input, full_in, preferred_element_type=F32) + bias_in
        act_low = exact_gelu(pre_gelu).astype(BF16)
        branch = lax.dot_general(
            act_low, full_down, CONTRACT_LAST, preferred_element_type=F32
        ).astype(BF16)
        second_vectors = vectors(b_down[at], at, 1)
        stored.append(
            [attn_input, qkv_low, log_total, context_low, first_sum, mlp_input, pre_gelu,
             act_low, first_vectors, second_vectors]
        )
        if at < layers - 1:
            second_sum, hidden, attn_input = group_call(
                forward_kernel, 1, "forward", (branch, normed, second_vectors), (row_kind, row_kind)
            )
            stored[at].append(second_sum)
        else:
            encoded, grad_second, sums_two, down_full = group_call(
                turn_kernel,
                2,
                "turn",
                (branch, normed, second_vectors, cotangent),
                (low_kind, row_kind, sum_kind),
            )

    weight_list = [None] * layers
    small_list = [None] * layers
    for at in reversed(range(layers)):
        (
            attn_input, qkv_low, log_total, context_low, first_sum, mlp_input, pre_gelu,
            act_low, first_vectors, second_vectors,
        ) = stored[at][:10]
        full_qkv, full_out, full_in, full_down = pieces(weights[at])
        grad_act = jnp.dot(down_full, full_down, preferred_element_type=F32)
        grad_w_down = lax.dot_general(
            down_full, act_low, CONTRACT_FIRST, preferred_element_type=F32
        )
        pre_low = jax.vjp(exact_gelu, pre_gelu)[1](grad_act)[0].astype(BF16)
        grad_w_in = lax.dot_general(
            mlp_input, pre_low, CONTRACT_FIRST, preferred_element_type=F32
        )
        branch = lax.dot_general(
            pre_low, full_in, CONTRACT_LAST, preferred_element_type=F32
        ).astype(BF16)
        grad_first, sums_one, attn_full = group_call(
            backward_kernel,
            3,
            "backward",
            (branch, grad_second, first_vectors, first_sum),
            (row_kind, sum_kind),
        )
        grad_context = jnp.dot(attn_full, full_out, preferred_element_type=F32)
        grad_context_low = grad_context.astype(BF16).reshape(total_rows, head_count, DH)
        grad_w_out = lax.dot_general(
            attn_full, context_low, CONTRACT_FIRST, preferred_element_type=F32
        )
        head_view = qkv_low.reshape(total_rows, 3, head_count, DH)
        grad_queries, grad_keys, grad_values = attend_backward(
            head_view[:, 0], head_view[:, 1], head_view[:, 2],
            allowed, score_scale, log_total, grad_context_low,
        )
        grad_qkv_low = (
            jnp.stack([grad_queries, grad_keys, grad_values], axis=1)
            .reshape(total_rows, 3 * col_width)
            .astype(BF16)
        )
        grad_w_qkv = lax.dot_general(
            attn_input, grad_qkv_low, CONTRACT_FIRST, preferred_element_type=F32
        )
        branch = lax.dot_general(
            grad_qkv_low, full_qkv, CONTRACT_LAST, preferred_element_type=F32
        ).astype(BF16)
        weight_grads = jnp.concatenate(
            [
                grad_w_qkv.astype(BF16),
                grad_w_out.astype(BF16),
                grad_w_in.astype(BF16),
                grad_w_down.astype(BF16),
            ],
            axis=1,
        )
        qkv_sums = jnp.sum(grad_qkv_low.astype(F32), axis=0).reshape(3, col_width)
        bias_qv_full = lax.dynamic_update_slice_in_dim(
            jnp.zeros((2, b_qv.shape[2]), F32),
            jnp.stack([qkv_sums[0], qkv_sums[2]]),
            column * col_width,
            1,
        )
        bias_in_full = lax.dynamic_update_slice_in_dim(
            jnp.zeros((b_in.shape[1],), F32),
            jnp.sum(pre_low.astype(F32), axis=0),
            column * hidden_width,
            0,
        )
        small_list[at] = jnp.concatenate(
            [
                bias_qv_full,
                bias_in_full.reshape(-1, width),
                sums_one[:3],
                sums_two[:3],
            ]
        )
        if at > 0:
            weight_list[at] = lax.psum_scatter(
                weight_grads, AXES, scatter_dimension=0, axis_index_groups=PLANES, tiled=True
            ).astype(F32)
            grad_second, sums_two, down_full = group_call(
                backward_kernel,
                3,
                "backward",
                (branch, grad_first, stored[at - 1][9], stored[at - 1][10]),
                (row_kind, sum_kind),
            )
        else:
            g_tokens, weight_list[at] = end(branch, grad_first, weight_grads)

    small = lax.psum(jnp.stack(small_list), AXES)
    grads = swap(jnp.stack(weight_list).astype(BF16)).astype(F32)
    g_qkv, g_out, g_in, g_down = (
        grads[:, :, cuts[0] : cuts[1]],
        grads[:, :, cuts[1] : cuts[2]],
        grads[:, :, cuts[2] : cuts[3]],
        grads[:, :, cuts[3] :],
    )
    at_in, at_one = 2, 2 + b_in.shape[1] // width
    at_two = at_one + 3
    return (
        swap(encoded),
        swap(g_tokens),
        g_qkv.reshape(layers, kept, 3, col_width),
        small[:, :at_in],
        g_out.transpose(0, 2, 1),
        small[:, at_one + 2],
        g_in,
        small[:, at_in:at_one].reshape(layers, -1),
        g_down.transpose(0, 2, 1),
        small[:, at_two + 2],
        jnp.stack([small[:, at_one], small[:, at_two]], axis=1),
        jnp.stack([small[:, at_one + 1], small[:, at_two + 1]], axis=1),
    )


def solution(mesh):
    placed = (
        P(("dp", "tensor"), None),
        P("dp", None),
        P(None, "dp", None, "tensor"),
        P(),
        P(None, "tensor", "dp"),
        P(),
        P(None, "dp", "tensor"),
        P(),
        P(None, "tensor", "dp"),
        P(),
        P(),
        P(),
        P(("dp", "tensor"), None),
    )
    return jax.shard_map(
        shards,
        mesh=mesh,
        in_specs=placed,
        out_specs=(
            P(("dp", "tensor"), None),
            P(("dp", "tensor"), None),
            P(None, "dp", None, "tensor"),
            P(),
            P(None, "tensor", "dp"),
            P(),
            P(None, "dp", "tensor"),
            P(),
            P(None, "tensor", "dp"),
            P(),
            P(),
            P(),
        ),
        check_vma=False,
    )
```

```python
import functools

import jax
import jax.numpy as jnp
from jax import lax
from jax.experimental import pallas as pl
from jax.experimental.pallas import tpu as pltpu
from jax.sharding import PartitionSpec as P

DH = 64
EPSILON = 1e-06
MESH = pl.DeviceIdType.MESH
F32 = jnp.float32
BF16 = jnp.bfloat16


def place():
    dp, tensor = lax.axis_index("dp"), lax.axis_index("tensor")
    core = lax.rem(dp, 2)
    z = lax.rem(lax.div(dp, 2), 4)
    x = lax.rem(lax.div(tensor, 4) * 2 + lax.div(dp, 8), 4)
    y = lax.rem(tensor, 4)
    return x, y, z, core


def device(x, y, z, core):
    x, y, z = lax.rem(x, 4), lax.rem(y, 4), lax.rem(z, 4)
    return (lax.rem(x, 2) * 8 + z * 2 + core, lax.div(x, 2) * 4 + y)


def block_of(x, z):
    x, z = lax.rem(x, 4), lax.rem(z, 4)
    return lax.rem(x, 2) * 8 + z * 2 + lax.div(x, 2)


def greet(devices):
    barrier = pltpu.get_barrier_semaphore()
    for other in devices:
        pl.semaphore_signal(barrier, inc=1, device_id=other, device_id_type=MESH)
    pl.semaphore_wait(barrier, len(devices))


class Copies:
    def __init__(self, send, recv):
        self.send, self.recv, self.started = send, recv, []

    def start(self, src, dst, to):
        at = len(self.started)
        copy = pltpu.make_async_remote_copy(
            src_ref=src,
            dst_ref=dst,
            send_sem=self.send.at[at],
            recv_sem=self.recv.at[at],
            device_id=to,
            device_id_type=MESH,
        )
        copy.start()
        self.started.append(copy)
        return copy

    def wait_sends(self):
        for copy in self.started:
            copy.wait_send()


def group_neighbours():
    x, y, z, core = place()
    return (
        device(x, y, z, 1 - core),
        device(x, y + 1, z, core),
        device(x, y + 3, z, core),
    )


GATHER_COPIES = 12
SCATTER_COPIES = 10


def gather_group(copies, out, tick=lambda: None):
    x, y, z, core = place()
    pair, after, before = group_neighbours()
    half = out.shape[1] // 2
    top, low = pl.ds(0, half), pl.ds(half, half)
    here = core * 4

    def part(step, rows):
        return out.at[here + lax.rem(y + step, 4), rows]

    def send(step, rows, to):
        return copies.start(part(step, rows), part(step, rows), to)

    top_after = send(0, top, after)
    low_before = send(0, low, before)
    low_after = send(0, low, after)
    top_before = send(0, top, before)
    everything = pl.ds(0, 2 * half)
    own_pair = send(0, everything, pair)
    tick()
    top_after.wait_recv()
    far_top = send(3, top, after)
    low_before.wait_recv()
    far_low = send(1, low, before)
    tick()
    low_after.wait_recv()
    pair_before = send(3, everything, pair)
    top_before.wait_recv()
    pair_after = send(1, everything, pair)
    tick()
    far_top.wait_recv()
    pair_top = send(2, top, pair)
    far_low.wait_recv()
    pair_low = send(2, low, pair)
    tick()
    for copy in (own_pair, pair_before, pair_after, pair_top, pair_low):
        copy.wait_recv()


def scatter_group(copies, part, from_pair, staged, far, near, tick=lambda: None):
    x, y, z, core = place()
    pair, after, before = group_neighbours()
    half = part.shape[1] // 2
    top, low = pl.ds(0, half), pl.ds(half, half)
    here, there = core * 4, (1 - core) * 4
    steps = (2, 1, 3, 0)
    swaps = [
        copies.start(part.at[there + lax.rem(y + step, 4)], from_pair.at[slot], pair)
        for slot, step in enumerate(steps)
    ]

    def chip(slot, rows):
        own = part[here + lax.rem(y + steps[slot], 4), rows].astype(F32)
        return own + from_pair[slot, rows].astype(F32)

    swaps[0].wait_recv()
    staged[0, top] = chip(0, top).astype(BF16)
    far_top = copies.start(staged.at[0, top], far.at[top], after)
    staged[0, low] = chip(0, low).astype(BF16)
    far_low = copies.start(staged.at[0, low], far.at[low], before)
    swaps[1].wait_recv()
    staged[1, low] = chip(1, low).astype(BF16)
    low_after = copies.start(staged.at[1, low], near.at[0, low], after)
    swaps[2].wait_recv()
    staged[2, top] = chip(2, top).astype(BF16)
    top_before = copies.start(staged.at[2, top], near.at[1, top], before)
    tick()
    far_top.wait_recv()
    staged[1, top] = (chip(1, top) + far[top].astype(F32)).astype(BF16)
    top_after = copies.start(staged.at[1, top], near.at[0, top], after)
    far_low.wait_recv()
    staged[2, low] = (chip(2, low) + far[low].astype(F32)).astype(BF16)
    low_before = copies.start(staged.at[2, low], near.at[1, low], before)
    tick()
    swaps[3].wait_recv()
    own = chip(3, pl.ds(0, 2 * half))
    for copy in (low_after, top_before, top_after, low_before):
        copy.wait_recv()
    return own + near[0].astype(F32) + near[1].astype(F32)


def scatter_scratch(rows, width):
    return [
        pltpu.VMEM((4, rows, width), BF16),
        pltpu.VMEM((3, rows, width), BF16),
        pltpu.VMEM((rows, width), BF16),
        pltpu.VMEM((2, rows, width), BF16),
    ]


def sems(count):
    return [pltpu.SemaphoreType.DMA((count,)), pltpu.SemaphoreType.DMA((count,))]


def plane_ring(axis):
    x, y, z, core = place()
    if axis == "x":
        return device(x + 1, y, z, core), device(x + 3, y, z, core)
    return device(x, y, z + 1, core), device(x, y, z + 3, core)


def plane_at(first, u, v):
    return block_of(u, v) if first == "x" else block_of(v, u)


PLANE_GATHER_COPIES = 36
PLANE_SCATTER_COPIES = 36


def gather_plane(copies, out):
    x, y, z, core = place()
    quarter = out.shape[1] // 4
    paths = []
    for first, base in (("x", 0), ("z", 2 * quarter)):
        v, u = (x, z) if first == "x" else (z, x)
        other = "z" if first == "x" else "x"
        paths.append(
            dict(
                first=first,
                v=v,
                u=u,
                ring=plane_ring(first),
                cross=plane_ring(other),
                halves=(pl.ds(base, quarter), pl.ds(base + quarter, quarter)),
                whole=pl.ds(base, 2 * quarter),
            )
        )

    def send(path, dv, du, rows, to):
        at = plane_at(path["first"], path["v"] + dv, path["u"] + du)
        return copies.start(out.at[at, rows], out.at[at, rows], to)

    for path in paths:
        after, before = path["ring"]
        top, low = path["halves"]
        path["ta"] = send(path, 0, 0, top, after)
        path["lb"] = send(path, 0, 0, low, before)
        path["la"] = send(path, 0, 0, low, after)
        path["tb"] = send(path, 0, 0, top, before)
        path["c"] = {0: [send(path, 0, 0, path["whole"], to) for to in path["cross"]]}
    yield
    for path in paths:
        path["ta"].wait_recv()
        path["ft"] = send(path, 3, 0, path["halves"][0], path["ring"][0])
        path["lb"].wait_recv()
        path["fl"] = send(path, 1, 0, path["halves"][1], path["ring"][1])
    yield
    for path in paths:
        path["la"].wait_recv()
        path["c"][3] = [send(path, 3, 0, path["whole"], to) for to in path["cross"]]
        path["tb"].wait_recv()
        path["c"][1] = [send(path, 1, 0, path["whole"], to) for to in path["cross"]]
    last = []
    for path in paths:
        path["c"][0][0].wait_recv()
        last.append(send(path, 0, 3, path["whole"], path["cross"][0]))
    yield
    for path in paths:
        path["ft"].wait_recv()
        path["fl"].wait_recv()
        path["c"][2] = [send(path, 2, 0, path["whole"], to) for to in path["cross"]]
    yield
    for path in paths:
        path["c"][3][0].wait_recv()
        last.append(send(path, 3, 3, path["whole"], path["cross"][0]))
        path["c"][1][1].wait_recv()
        last.append(send(path, 1, 1, path["whole"], path["cross"][1]))
    yield
    for path in paths:
        path["c"][2][1].wait_recv()
        last.append(send(path, 2, 1, path["whole"], path["cross"][1]))
    yield
    for path in paths:
        for copy in (path["c"][0][1], path["c"][3][1], path["c"][1][0], path["c"][2][0]):
            copy.wait_recv()
    for copy in last:
        copy.wait_recv()


def scatter_plane_scratch(rows, width):
    half = rows // 2
    return [
        pltpu.VMEM((2, 4, half, width), BF16),
        pltpu.VMEM((2, 2, 4, half, width), BF16),
        pltpu.VMEM((2, 4, half, width), BF16),
        pltpu.VMEM((2, 4, half, width), BF16),
        pltpu.VMEM((2, half, width), BF16),
        pltpu.VMEM((2, 2, half, width), BF16),
        pltpu.VMEM((2, 2, half // 2, width), BF16),
    ]


def scatter_plane(copies, part, out, far, near, passed, summed, far2, near2, passed2):
    x, y, z, core = place()
    half = part.shape[1] // 2
    quarter = half // 2
    paths = []
    for at, (first, base) in enumerate((("x", 0), ("z", half))):
        u, v = (x, z) if first == "x" else (z, x)
        other = "z" if first == "x" else "x"
        paths.append(
            dict(
                at=at,
                first=first,
                u=u,
                v=v,
                ring=plane_ring(first),
                cross=plane_ring(other),
                rows=pl.ds(base, half),
                base=base,
            )
        )

    def source(path, du, v):
        return (plane_at(path["first"], path["u"] + du, v), path["rows"])

    for path in paths:
        at, (after, before) = path["at"], path["ring"]
        path["far"] = [
            copies.start(
                part.at[source(path, 2, v)], far.at[at, v], after if v < 2 else before
            )
            for v in range(4)
        ]
    for path in paths:
        at, (after, before) = path["at"], path["ring"]
        path["near"] = [
            copies.start(part.at[source(path, 1, v)], near.at[at, 0, v], after) for v in (2, 3)
        ] + [
            copies.start(part.at[source(path, 3, v)], near.at[at, 1, v], before) for v in (0, 1)
        ]
    yield
    for path in paths:
        at, (after, before) = path["at"], path["ring"]
        for v in (0, 2, 1, 3):
            path["far"][v].wait_recv()
            du, slot, to = (1, 0, after) if v < 2 else (3, 1, before)
            own = part[source(path, du, v)].astype(F32)
            passed[at, v] = (own + far[at, v].astype(F32)).astype(BF16)
            path["near"].append(copies.start(passed.at[at, v], near.at[at, slot, v], to))
    yield
    for path in paths:
        at = path["at"]
        for copy in path["near"]:
            copy.wait_recv()
        for v in range(4):
            own = part[source(path, 0, v)].astype(F32)
            summed[at, v] = (
                own + near[at, 0, v].astype(F32) + near[at, 1, v].astype(F32)
            ).astype(BF16)
        v, (after, before) = path["v"], path["cross"]
        top, low = pl.ds(0, quarter), pl.ds(quarter, quarter)
        v1, v2, v3 = lax.rem(v + 1, 4), lax.rem(v + 2, 4), lax.rem(v + 3, 4)
        path["ft"] = copies.start(summed.at[at, v2, top], far2.at[at, top], after)
        path["fl"] = copies.start(summed.at[at, v2, low], far2.at[at, low], before)
        path["last"] = [
            copies.start(summed.at[at, v1, low], near2.at[at, 0, low], after),
            copies.start(summed.at[at, v3, top], near2.at[at, 1, top], before),
        ]
    yield
    for path in paths:
        at, v, (after, before) = path["at"], path["v"], path["cross"]
        top, low = pl.ds(0, quarter), pl.ds(quarter, quarter)
        v1, v3 = lax.rem(v + 1, 4), lax.rem(v + 3, 4)
        path["ft"].wait_recv()
        passed2[at, 0] = (summed[at, v1, top].astype(F32) + far2[at, top].astype(F32)).astype(BF16)
        path["last"].append(copies.start(passed2.at[at, 0], near2.at[at, 0, top], after))
        path["fl"].wait_recv()
        passed2[at, 1] = (summed[at, v3, low].astype(F32) + far2[at, low].astype(F32)).astype(BF16)
        path["last"].append(copies.start(passed2.at[at, 1], near2.at[at, 1, low], before))
    yield
    for path in paths:
        at, v = path["at"], path["v"]
        for copy in path["last"]:
            copy.wait_recv()
        total = summed[at, v].astype(F32) + near2[at, 0].astype(F32) + near2[at, 1].astype(F32)
        out[path["rows"]] = total.astype(out.dtype)


def params(number):
    return pltpu.CompilerParams(
        collective_id=number, has_side_effects=True, vmem_limit_bytes=48 * 2**20
    )


VMEM = pl.BlockSpec(memory_space=pltpu.VMEM)


def neighbours():
    return [*group_neighbours(), *plane_ring("x"), *plane_ring("z")]


def drain(steps):
    for _ in steps:
        pass


def swap_partner():
    x, y, z, core = place()
    upper = lax.div(x, 2)
    return core != upper, device(core * 2 + lax.rem(x, 2), y, z, upper)


def greet_with_partner(others):
    moves, partner = swap_partner()
    barrier = pltpu.get_barrier_semaphore()
    for other in others:
        pl.semaphore_signal(barrier, inc=1, device_id=other, device_id_type=MESH)

    @pl.when(moves)
    def _():
        pl.semaphore_signal(barrier, inc=1, device_id=partner, device_id_type=MESH)

    pl.semaphore_wait(barrier, len(others) + moves.astype(jnp.int32))


def partner_copy(src, dst, send, recv):
    return pltpu.make_async_remote_copy(
        src_ref=src,
        dst_ref=dst,
        send_sem=send,
        recv_sem=recv,
        device_id=swap_partner()[1],
        device_id_type=MESH,
    )


def start_kernel(tokens, weights, rows_out, weights_out, ssend, srecv, send, recv, wsend, wrecv):
    x, y, z, core = place()
    upper = lax.div(x, 2)
    moves, _ = swap_partner()
    greet_with_partner(neighbours())
    plane, group = Copies(wsend, wrecv), Copies(send, recv)
    there = block_of(core * 2 + lax.rem(x, 2), z)
    weights_move = partner_copy(weights, weights_out.at[there], ssend.at[0], srecv.at[0])
    rows_move = partner_copy(tokens, rows_out.at[upper * 4 + y], ssend.at[1], srecv.at[1])

    @pl.when(moves)
    def _():
        weights_move.start()
        rows_move.start()
        weights_move.wait_recv()

    @pl.when(jnp.logical_not(moves))
    def _():
        weights_out[block_of(x, z)] = weights[...]
        rows_out[core * 4 + y] = tokens[...]

    steps = gather_plane(plane, weights_out)
    next(steps)

    @pl.when(moves)
    def _():
        rows_move.wait_recv()

    gather_group(group, rows_out, lambda: next(steps, None))
    drain(steps)

    @pl.when(moves)
    def _():
        weights_move.wait_send()
        rows_move.wait_send()

    group.wait_sends()
    plane.wait_sends()


def start(tokens, weights):
    rows, width = tokens.shape
    held, columns = weights.shape
    gathered, full = pl.pallas_call(
        start_kernel,
        out_shape=(
            jax.ShapeDtypeStruct((8, rows, width), BF16),
            jax.ShapeDtypeStruct((16, held, columns), BF16),
        ),
        in_specs=[VMEM] * 2,
        out_specs=(VMEM, VMEM),
        scratch_shapes=sems(2) + sems(GATHER_COPIES) + sems(PLANE_GATHER_COPIES),
        compiler_params=params(0),
        name="start",
    )(tokens, weights)
    return gathered.reshape(8 * rows, width), full.reshape(16 * held, columns)


def normed_parts(stream):
    row_mean = jnp.mean(stream, axis=-1, keepdims=True)
    centered = stream - row_mean
    row_var = jnp.mean(centered * centered, axis=-1, keepdims=True)
    scale = lax.rsqrt(row_var + EPSILON)
    return centered * scale, scale


def norm_pull(unit, scale, gain, grad, sums):
    scaled = grad * gain
    inner = jnp.mean(scaled * unit, axis=-1, keepdims=True)
    pulled = scale * (scaled - jnp.mean(scaled, axis=-1, keepdims=True) - unit * inner)
    low = pulled.astype(BF16)
    sums[0:1] = jnp.sum(grad * unit, axis=0, keepdims=True)
    sums[1:2] = jnp.sum(grad, axis=0, keepdims=True)
    sums[2:3] = jnp.sum(low.astype(F32), axis=0, keepdims=True)
    return pulled, low


def group_kernel(mode, plane_mode, count, kept, refs):
    refs = list(refs)
    take = lambda number: [refs.pop(0) for _ in range(number)]
    part, held, vectors, *extra = take(count)
    plane_in = take(1)[0] if plane_mode else None
    outs = take(kept)
    (rows_out,) = take(1)
    plane_out = take(1)[0] if plane_mode else None
    scratch = take(4)
    send, recv, gsend, grecv = take(4)
    x, y, z, core = place()
    greet(neighbours() if plane_mode else group_neighbours())
    scatter, gather = Copies(send, recv), Copies(gsend, grecv)
    steps = iter(())
    if plane_mode == "gather":
        plane = Copies(*take(2))
        plane_out[block_of(x, z)] = plane_in[...]
        steps = gather_plane(plane, plane_out)
    elif plane_mode == "scatter":
        plane = Copies(*take(2))
        steps = scatter_plane(plane, plane_in, plane_out, *refs)
    tick = lambda: next(steps, None)
    tick()
    total = scatter_group(scatter, part, *scratch, tick)
    gain, shift = vectors[1:2], vectors[2:3]
    if mode == "forward":
        stream = held[...] + total + vectors[0:1]
        outs[0][...] = stream
        unit, _ = normed_parts(stream)
        normed = unit * gain + shift
        outs[1][...] = normed
        low = normed.astype(BF16)
    elif mode == "turn":
        unit, scale = normed_parts(held[...] + total + vectors[0:1])
        outs[0][...] = (unit * gain + shift).astype(BF16)
        pulled, low = norm_pull(unit, scale, gain, extra[0][...].astype(F32), outs[2])
        outs[1][...] = pulled
    else:
        unit, scale = normed_parts(extra[0][...])
        pulled, low = norm_pull(unit, scale, gain, held[...] + total, outs[1])
        outs[0][...] = pulled
    rows_out[core * 4 + y] = low
    gather_group(gather, rows_out, tick)
    drain(steps)
    scatter.wait_sends()
    gather.wait_sends()
    if plane_mode:
        plane.wait_sends()


def group_call(mode, number, operands, outs, plane_mode=None, plane_in=None):
    part = operands[0]
    rows, width = part.shape[0] // 8, part.shape[1]
    shapes = tuple(jax.ShapeDtypeStruct(shape, kind) for shape, kind in outs)
    shapes += (jax.ShapeDtypeStruct((8, rows, width), BF16),)
    scratch = scatter_scratch(rows, width) + sems(SCATTER_COPIES) + sems(GATHER_COPIES)
    given = [part.reshape(8, rows, width), *operands[1:]]
    if plane_mode == "gather":
        kept, columns = plane_in.shape
        shapes += (jax.ShapeDtypeStruct((16, kept, columns), BF16),)
        scratch += sems(PLANE_GATHER_COPIES)
        given.append(plane_in)
    elif plane_mode == "scatter":
        kept, columns = plane_in.shape[0] // 16, plane_in.shape[1]
        shapes += (jax.ShapeDtypeStruct((kept, columns), BF16),)
        scratch += sems(PLANE_SCATTER_COPIES) + scatter_plane_scratch(kept, columns)
        given.append(plane_in.reshape(16, kept, columns))

    def kernel(*refs):
        group_kernel(mode, plane_mode, len(operands), len(outs), refs)

    results = pl.pallas_call(
        kernel,
        out_shape=shapes,
        in_specs=[VMEM] * len(given),
        out_specs=(VMEM,) * len(shapes),
        scratch_shapes=scratch,
        compiler_params=params(number),
        name=mode + str(number),
    )(*given)
    results = list(results)
    results[len(outs)] = results[len(outs)].reshape(8 * rows, width)
    if plane_mode == "gather":
        results[-1] = results[-1].reshape(16 * kept, columns)
    return results


def sum_small(copies, small, out, got_x, got_z):
    x, y, z, core = place()
    own = core * 4 + y
    along_x = [device(x + step, y, z, core) for step in (1, 2, 3)]
    along_z = [device(x, y, z + step, core) for step in (1, 2, 3)]
    along_y = [device(x, y + step, z, core) for step in (1, 2, 3)]
    first = [copies.start(small, got_x.at[at], to) for at, to in enumerate(along_x)]
    yield
    for copy in first:
        copy.wait_recv()
    got_z[3] = small[...] + got_x[0] + got_x[1] + got_x[2]
    second = [copies.start(got_z.at[3], got_z.at[at], to) for at, to in enumerate(along_z)]
    yield
    for copy in second:
        copy.wait_recv()
    out[own] = got_z[3] + got_z[0] + got_z[1] + got_z[2]
    third = [copies.start(out.at[own], out.at[own], to) for to in along_y]
    yield
    for copy in third:
        copy.wait_recv()
    held = out.at[pl.ds(core * 4, 4)]
    copies.start(held, held, device(x, y, z, 1 - core)).wait_recv()


def end_kernel(
    part, held, grads, small, rows_out, grads_out, small_out,
    from_pair, staged, far, near, pfar, pnear, passed, summed, far2, near2, passed2,
    rows_stage, grads_stage, got_x, got_z,
    ssend, srecv, send, recv, psend, precv, tsend, trecv,
):
    x, y, z, core = place()
    moves, _ = swap_partner()
    greet_with_partner(
        neighbours()
        + [device(x + 2, y, z, core), device(x, y + 2, z, core), device(x, y, z + 2, core)]
    )
    group, plane, tiny = Copies(send, recv), Copies(psend, precv), Copies(tsend, trecv)
    rows_move = partner_copy(rows_stage, rows_out, ssend.at[0], srecv.at[0])
    grads_move = partner_copy(grads_stage, grads_out, ssend.at[1], srecv.at[1])
    tiny_steps = sum_small(tiny, small, small_out, got_x, got_z)
    plane_steps = scatter_plane(
        plane, grads, grads_stage, pfar, pnear, passed, summed, far2, near2, passed2
    )

    def tick():
        next(plane_steps, None)
        next(tiny_steps, None)

    tick()
    total = scatter_group(group, part, from_pair, staged, far, near, tick)
    low = (held[...] + total).astype(BF16)

    @pl.when(moves)
    def _():
        rows_stage[...] = low
        rows_move.start()

    @pl.when(jnp.logical_not(moves))
    def _():
        rows_out[...] = low

    drain(plane_steps)

    @pl.when(moves)
    def _():
        grads_move.start()

    @pl.when(jnp.logical_not(moves))
    def _():
        grads_out[...] = grads_stage[...]

    drain(tiny_steps)

    @pl.when(moves)
    def _():
        rows_move.wait()
        grads_move.wait()

    group.wait_sends()
    plane.wait_sends()
    tiny.wait_sends()


def end(part, held, grads, small):
    rows, width = held.shape
    kept, columns = grads.shape[0] // 16, grads.shape[1]
    return pl.pallas_call(
        end_kernel,
        out_shape=(
            jax.ShapeDtypeStruct((rows, width), BF16),
            jax.ShapeDtypeStruct((kept, columns), BF16),
            jax.ShapeDtypeStruct((8, *small.shape), F32),
        ),
        in_specs=[VMEM] * 4,
        out_specs=(VMEM,) * 3,
        scratch_shapes=scatter_scratch(rows, width)
        + scatter_plane_scratch(kept, columns)
        + [
            pltpu.VMEM((rows, width), BF16),
            pltpu.VMEM((kept, columns), BF16),
            pltpu.VMEM((3, *small.shape), F32),
            pltpu.VMEM((4, *small.shape), F32),
        ]
        + sems(2)
        + sems(SCATTER_COPIES)
        + sems(PLANE_SCATTER_COPIES)
        + sems(10),
        compiler_params=params(1),
        name="end",
    )(part.reshape(8, rows, width), held, grads.reshape(16, kept, columns), small)


def segment_ids(shard_lengths, total_rows, seq_count):
    seq_ends = jnp.cumsum(shard_lengths)
    positions = jnp.arange(total_rows, dtype=jnp.int32)
    segments = jnp.sum((positions[:, None] >= seq_ends[None, :]).astype(jnp.int32), axis=1)
    return jnp.where(segments == seq_count, seq_count + positions, segments)


def masked_scores(queries, keys_in, allowed, score_scale):
    scores = (
        jnp.einsum("qhd,khd->hqk", queries, keys_in, preferred_element_type=jnp.float32)
        * score_scale
    )
    return jnp.where(allowed[None], scores, -1e30)


def attend_forward(queries, keys_in, values_in, allowed, score_scale):
    scores = masked_scores(queries, keys_in, allowed, score_scale)
    row_peak = jnp.max(scores, axis=-1, keepdims=True)
    exp_scores = jnp.exp(scores - row_peak)
    row_total = jnp.sum(exp_scores, axis=-1, keepdims=True)
    attn_probs = (exp_scores / row_total).astype(jnp.bfloat16)
    context = jnp.einsum("hqk,khd->qhd", attn_probs, values_in, preferred_element_type=jnp.float32)
    return (context, row_peak + jnp.log(row_total))


def attend_backward(queries, keys_in, values_in, allowed, score_scale, log_total, grad_context):
    scores = masked_scores(queries, keys_in, allowed, score_scale)
    attn_probs = jnp.exp(scores - log_total)
    probs_low = attn_probs.astype(jnp.bfloat16)
    grad_probs = jnp.einsum(
        "qhd,khd->hqk", grad_context, values_in, preferred_element_type=jnp.float32
    )
    grad_values = jnp.einsum(
        "hqk,qhd->khd", probs_low, grad_context, preferred_element_type=jnp.float32
    )
    row_inner = jnp.sum(attn_probs * grad_probs, axis=-1, keepdims=True)
    grad_scores = (attn_probs * (grad_probs - row_inner)).astype(jnp.bfloat16)
    grad_queries = (
        jnp.einsum("hqk,khd->qhd", grad_scores, keys_in, preferred_element_type=jnp.float32)
        * score_scale
    )
    grad_keys = (
        jnp.einsum("hqk,qhd->khd", grad_scores, queries, preferred_element_type=jnp.float32)
        * score_scale
    )
    return (grad_queries, grad_keys, grad_values)


def exact_gelu(values):
    return jax.nn.gelu(values, approximate=False)


CONTRACT_LAST = (((1,), (1,)), ((), ()))
CONTRACT_FIRST = (((0,), (0,)), ((), ()))


def flat(x, y, z, core):
    return (x % 2 * 8 + z * 2 + core) * 8 + x // 2 * 4 + y


CHIPS = [(x, y, z, core) for x in range(4) for y in range(4) for z in range(4) for core in (0, 1)]
SWAP = [
    (flat(x, y, z, core), flat(core * 2 + x % 2, y, z, x // 2)) for x, y, z, core in CHIPS
]
PLANES = [
    [flat(xh * 2 + xl, y, z, core) for xl in (0, 1) for z in range(4) for xh in (0, 1)]
    for core in (0, 1)
    for y in range(4)
]
AXES = ("dp", "tensor")


def swap(values):
    return lax.ppermute(values, AXES, SWAP)


def shards(
    tokens,
    lengths,
    w_qkv,
    b_qv,
    w_out,
    b_out,
    w_in,
    b_in,
    w_down,
    b_down,
    ln_gain,
    ln_bias,
    cotangent,
):
    x, y, z, core = place()
    column = core * 4 + y
    own_rows, width = tokens.shape
    total_rows = own_rows * 8
    layers, kept = w_qkv.shape[:2]
    col_width = w_qkv.shape[3]
    hidden_width = w_in.shape[2]
    head_count = col_width // DH
    score_scale = DH ** (-0.5)
    cuts = (0, 3 * col_width, 4 * col_width, 4 * col_width + hidden_width)

    cut_out, cut_down = 3 * col_width, hidden_width
    attention_shards = [
        jnp.concatenate([w_qkv[at].reshape(kept, 3 * col_width), w_out[at].T], axis=1)
        for at in range(layers)
    ]
    hidden_shards = [
        jnp.concatenate([w_in[at], w_down[at].T], axis=1) for at in range(layers)
    ]
    lengths = swap(lengths)
    first_hidden = swap(hidden_shards[0])
    later_shard = swap(jnp.concatenate([attention_shards[1], hidden_shards[1]], axis=1))
    cotangent = swap(cotangent)
    attn_input, attention_full = start(tokens, attention_shards[0])
    hidden = lax.dynamic_slice_in_dim(attn_input, column * own_rows, own_rows, 0).astype(F32)

    segments = segment_ids(lengths[0], total_rows, lengths.shape[1])
    allowed = segments[:, None] == segments[None, :]

    def vectors(bias, at, which):
        rows = [bias.astype(F32), ln_gain[at, which].astype(F32), ln_bias[at, which].astype(F32)]
        return jnp.stack(rows + [jnp.zeros_like(rows[0])] * 5)

    row_kind = ((own_rows, width), F32)
    sum_kind = ((8, width), F32)
    low_kind = ((own_rows, width), BF16)
    stored = []
    for at in range(layers):
        if at > 0:
            attention_full, hidden_full = (
                later_full[:, : cut_out + col_width],
                later_full[:, cut_out + col_width :],
            )
        full_qkv, full_out = attention_full[:, :cut_out], attention_full[:, cut_out:]
        bias_qv = lax.dynamic_slice_in_dim(
            b_qv[at].astype(F32), column * col_width, col_width, 1
        )
        bias_all = jnp.concatenate([bias_qv[0], jnp.zeros_like(bias_qv[0]), bias_qv[1]])
        qkv = jnp.dot(attn_input, full_qkv, preferred_element_type=F32)
        qkv_low = (qkv + bias_all).astype(BF16)
        head_view = qkv_low.reshape(total_rows, 3, head_count, DH)
        context, log_total = attend_forward(
            head_view[:, 0], head_view[:, 1], head_view[:, 2], allowed, score_scale
        )
        context_low = context.reshape(total_rows, col_width).astype(BF16)
        branch = lax.dot_general(
            context_low, full_out, CONTRACT_LAST, preferred_element_type=F32
        ).astype(BF16)
        first_vectors = vectors(b_out[at], at, 0)
        if at == 0:
            first_sum, normed, mlp_input, hidden_full = group_call(
                "forward", 2, (branch, hidden, first_vectors), (row_kind, row_kind),
                "gather", first_hidden,
            )
        else:
            first_sum, normed, mlp_input = group_call(
                "forward", 3, (branch, hidden, first_vectors), (row_kind, row_kind)
            )
        full_in, full_down = hidden_full[:, :cut_down], hidden_full[:, cut_down:]
        bias_in = lax.dynamic_slice_in_dim(
            b_in[at].astype(F32), column * hidden_width, hidden_width, 0
        )
        pre_gelu = jnp.dot(mlp_input, full_in, preferred_element_type=F32) + bias_in
        act_low = exact_gelu(pre_gelu).astype(BF16)
        branch = lax.dot_general(
            act_low, full_down, CONTRACT_LAST, preferred_element_type=F32
        ).astype(BF16)
        second_vectors = vectors(b_down[at], at, 1)
        stored.append(
            [attn_input, qkv_low, log_total, context_low, first_sum, mlp_input, pre_gelu,
             act_low, first_vectors, second_vectors, full_qkv, full_out, full_in, full_down]
        )
        if at == 0:
            second_sum, hidden, attn_input, later_full = group_call(
                "forward", 4, (branch, normed, second_vectors), (row_kind, row_kind),
                "gather", later_shard,
            )
            stored[at].append(second_sum)
        else:
            encoded, grad_second, sums_two, down_full = group_call(
                "turn",
                5,
                (branch, normed, second_vectors, cotangent),
                (low_kind, row_kind, sum_kind),
            )

    attention_grads, hidden_grads = [None] * layers, [None] * layers
    small_list = [None] * layers
    for at in reversed(range(layers)):
        (
            attn_input, qkv_low, log_total, context_low, first_sum, mlp_input, pre_gelu,
            act_low, first_vectors, second_vectors, full_qkv, full_out, full_in, full_down,
        ) = stored[at][:14]
        grad_act = jnp.dot(down_full, full_down, preferred_element_type=F32)
        grad_w_down = lax.dot_general(
            down_full, act_low, CONTRACT_FIRST, preferred_element_type=F32
        )
        pre_low = jax.vjp(exact_gelu, pre_gelu)[1](grad_act)[0].astype(BF16)
        grad_w_in = lax.dot_general(
            mlp_input, pre_low, CONTRACT_FIRST, preferred_element_type=F32
        )
        branch = lax.dot_general(
            pre_low, full_in, CONTRACT_LAST, preferred_element_type=F32
        ).astype(BF16)
        own_grads = jnp.concatenate([grad_w_in.astype(BF16), grad_w_down.astype(BF16)], axis=1)
        grad_first, sums_one, attn_full, hidden_grads[at] = group_call(
            "backward", 6 + 2 * at, (branch, grad_second, first_vectors, first_sum),
            (row_kind, sum_kind), "scatter", own_grads,
        )
        hidden_grads[at] = swap(hidden_grads[at])
        grad_context = jnp.dot(attn_full, full_out, preferred_element_type=F32)
        grad_context_low = grad_context.astype(BF16).reshape(total_rows, head_count, DH)
        grad_w_out = lax.dot_general(
            attn_full, context_low, CONTRACT_FIRST, preferred_element_type=F32
        )
        head_view = qkv_low.reshape(total_rows, 3, head_count, DH)
        grad_queries, grad_keys, grad_values = attend_backward(
            head_view[:, 0], head_view[:, 1], head_view[:, 2],
            allowed, score_scale, log_total, grad_context_low,
        )
        grad_qkv_low = (
            jnp.stack([grad_queries, grad_keys, grad_values], axis=1)
            .reshape(total_rows, 3 * col_width)
            .astype(BF16)
        )
        grad_w_qkv = lax.dot_general(
            attn_input, grad_qkv_low, CONTRACT_FIRST, preferred_element_type=F32
        )
        branch = lax.dot_general(
            grad_qkv_low, full_qkv, CONTRACT_LAST, preferred_element_type=F32
        ).astype(BF16)
        own_grads = jnp.concatenate([grad_w_qkv.astype(BF16), grad_w_out.astype(BF16)], axis=1)
        qkv_sums = jnp.sum(grad_qkv_low.astype(F32), axis=0).reshape(3, col_width)
        own_sums = jnp.concatenate(
            [
                qkv_sums[0],
                qkv_sums[2],
                jnp.sum(pre_low.astype(F32), axis=0),
                jnp.zeros((width - 2 * col_width - hidden_width,), F32),
            ]
        )
        small_list[at] = jnp.concatenate(
            [sums_one[:3], sums_two[:3], own_sums[None], jnp.zeros((1, width), F32)]
        )
        if at > 0:
            grad_second, sums_two, down_full, attention_grads[at] = group_call(
                "backward", 7, (branch, grad_first, stored[at - 1][9], stored[at - 1][14]),
                (row_kind, sum_kind), "scatter", own_grads,
            )
            attention_grads[at] = swap(attention_grads[at])
        else:
            g_tokens, attention_grads[at], small = end(
                branch, grad_first, own_grads, jnp.concatenate(small_list)
            )

    attention_grads = jnp.stack(attention_grads).astype(F32)
    hidden_grads = jnp.stack(hidden_grads).astype(F32)
    small = small.reshape(8, layers, 8, width)
    sums = jnp.sum(small[:, :, :6], axis=0)
    own_sums = small[:, :, 6].transpose(1, 0, 2)
    g_b_qv = jnp.stack(
        [own_sums[:, :, :col_width], own_sums[:, :, col_width : 2 * col_width]], axis=1
    )
    g_b_in = own_sums[:, :, 2 * col_width : 2 * col_width + hidden_width]
    return (
        swap(encoded),
        g_tokens,
        attention_grads[:, :, :cut_out].reshape(layers, kept, 3, col_width),
        g_b_qv.reshape(layers, 2, width),
        attention_grads[:, :, cut_out:].transpose(0, 2, 1),
        sums[:, 2],
        hidden_grads[:, :, :cut_down],
        g_b_in.reshape(layers, -1),
        hidden_grads[:, :, cut_down:].transpose(0, 2, 1),
        sums[:, 5],
        jnp.stack([sums[:, 0], sums[:, 3]], axis=1),
        jnp.stack([sums[:, 1], sums[:, 4]], axis=1),
    )


def solution(mesh):
    placed = (
        P(("dp", "tensor"), None),
        P("dp", None),
        P(None, "dp", None, "tensor"),
        P(),
        P(None, "tensor", "dp"),
        P(),
        P(None, "dp", "tensor"),
        P(),
        P(None, "tensor", "dp"),
        P(),
        P(),
        P(),
        P(("dp", "tensor"), None),
    )
    return jax.shard_map(
        shards,
        mesh=mesh,
        in_specs=placed,
        out_specs=(
            P(("dp", "tensor"), None),
            P(("dp", "tensor"), None),
            P(None, "dp", None, "tensor"),
            P(),
            P(None, "tensor", "dp"),
            P(),
            P(None, "dp", "tensor"),
            P(),
            P(None, "tensor", "dp"),
            P(),
            P(),
            P(),
        ),
        check_vma=False,
    )
```

```python
import functools

import jax
import jax.numpy as jnp
from jax import lax
from jax.experimental import pallas as pl
from jax.experimental.pallas import tpu as pltpu
from jax.sharding import PartitionSpec as P

DH = 64
EPSILON = 1e-06
MESH = pl.DeviceIdType.MESH
F32 = jnp.float32
BF16 = jnp.bfloat16


def place():
    dp, tensor = lax.axis_index("dp"), lax.axis_index("tensor")
    core = lax.rem(dp, 2)
    z = lax.rem(lax.div(dp, 2), 4)
    x = lax.rem(lax.div(tensor, 4) * 2 + lax.div(dp, 8), 4)
    y = lax.rem(tensor, 4)
    return x, y, z, core


def device(x, y, z, core):
    x, y, z = lax.rem(x, 4), lax.rem(y, 4), lax.rem(z, 4)
    return (lax.rem(x, 2) * 8 + z * 2 + core, lax.div(x, 2) * 4 + y)


def block_of(x, z):
    x, z = lax.rem(x, 4), lax.rem(z, 4)
    return lax.rem(x, 2) * 8 + z * 2 + lax.div(x, 2)


def greet(devices):
    barrier = pltpu.get_barrier_semaphore()
    for other in devices:
        pl.semaphore_signal(barrier, inc=1, device_id=other, device_id_type=MESH)
    pl.semaphore_wait(barrier, len(devices))


class Copies:
    def __init__(self, send, recv):
        self.send, self.recv, self.started = send, recv, []

    def start(self, src, dst, to):
        at = len(self.started)
        copy = pltpu.make_async_remote_copy(
            src_ref=src,
            dst_ref=dst,
            send_sem=self.send.at[at],
            recv_sem=self.recv.at[at],
            device_id=to,
            device_id_type=MESH,
        )
        copy.start()
        self.started.append(copy)
        return copy

    def wait_sends(self):
        for copy in self.started:
            copy.wait_send()


def group_neighbours():
    x, y, z, core = place()
    return (
        device(x, y, z, 1 - core),
        device(x, y + 1, z, core),
        device(x, y + 3, z, core),
    )


GATHER_COPIES = 24
SCATTER_COPIES = 20


def gather_steps(copies, out, base, count):
    x, y, z, core = place()
    pair, after, before = group_neighbours()
    half = count // 2
    top, low, both = pl.ds(base, half), pl.ds(base + half, half), pl.ds(base, count)

    def send(step, rows, to):
        ref = out.at[core * 4 + lax.rem(y + step, 4), rows]
        return copies.start(ref, ref, to)

    top_after = send(0, top, after)
    low_before = send(0, low, before)
    low_after = send(0, low, after)
    top_before = send(0, top, before)
    own_pair = send(0, both, pair)
    yield
    top_after.wait_recv()
    far_top = send(3, top, after)
    low_before.wait_recv()
    far_low = send(1, low, before)
    yield
    low_after.wait_recv()
    pair_before = send(3, both, pair)
    top_before.wait_recv()
    pair_after = send(1, both, pair)
    yield
    far_top.wait_recv()
    pair_top = send(2, top, pair)
    far_low.wait_recv()
    pair_low = send(2, low, pair)
    yield
    for copy in (own_pair, pair_before, pair_after, pair_top, pair_low):
        copy.wait_recv()
    yield


def scatter_steps(copies, part, from_pair, staged, far, near, base, count, result):
    x, y, z, core = place()
    pair, after, before = group_neighbours()
    half = count // 2
    top, low, both = pl.ds(base, half), pl.ds(base + half, half), pl.ds(base, count)
    here, there = core * 4, (1 - core) * 4
    steps = (2, 1, 3, 0)
    swaps = [
        copies.start(
            part.at[there + lax.rem(y + step, 4), both], from_pair.at[slot, both], pair
        )
        for slot, step in enumerate(steps)
    ]

    def chip(slot, rows):
        own = part[here + lax.rem(y + steps[slot], 4), rows].astype(F32)
        return own + from_pair[slot, rows].astype(F32)

    yield
    swaps[0].wait_recv()
    staged[0, top] = chip(0, top).astype(BF16)
    far_top = copies.start(staged.at[0, top], far.at[top], after)
    staged[0, low] = chip(0, low).astype(BF16)
    far_low = copies.start(staged.at[0, low], far.at[low], before)
    yield
    swaps[1].wait_recv()
    staged[1, low] = chip(1, low).astype(BF16)
    low_after = copies.start(staged.at[1, low], near.at[0, low], after)
    swaps[2].wait_recv()
    staged[2, top] = chip(2, top).astype(BF16)
    top_before = copies.start(staged.at[2, top], near.at[1, top], before)
    yield
    far_top.wait_recv()
    staged[1, top] = (chip(1, top) + far[top].astype(F32)).astype(BF16)
    top_after = copies.start(staged.at[1, top], near.at[0, top], after)
    far_low.wait_recv()
    staged[2, low] = (chip(2, low) + far[low].astype(F32)).astype(BF16)
    low_before = copies.start(staged.at[2, low], near.at[1, low], before)
    yield
    swaps[3].wait_recv()
    own = chip(3, both)
    for copy in (low_after, top_before, top_after, low_before):
        copy.wait_recv()
    result.append(own + near[0, both].astype(F32) + near[1, both].astype(F32))
    yield


def scatter_gather(scatter, gather, part, bufs, rows_out, between, tick):
    x, y, z, core = place()
    count = part.shape[1] // 2
    results = [], []
    first, second = [
        scatter_steps(scatter, part, *bufs, at * count, count, results[at]) for at in (0, 1)
    ]

    def send(at):
        rows = pl.ds(at * count, count)
        rows_out[core * 4 + y, rows] = between(results[at][0], at, rows)
        steps = gather_steps(gather, rows_out, at * count, count)
        next(steps)
        return steps

    next(first)
    next(second)
    tick()
    next(first)
    next(first)
    next(second)
    next(first)
    next(second)
    tick()
    next(second)
    next(first)
    first = send(0)
    tick()
    next(second)
    second = send(1)
    next(first)
    tick()
    next(first)
    next(second)
    next(first)
    tick()
    next(second)
    next(first)
    next(second)
    tick()
    next(second)


def gather_all(gather, rows_out, tick):
    count = rows_out.shape[1] // 2
    first, second = [gather_steps(gather, rows_out, at * count, count) for at in (0, 1)]
    for _ in range(5):
        next(first)
        next(second)
        tick()


def scatter_all(scatter, part, bufs, tick):
    count = part.shape[1] // 2
    results = [], []
    first, second = [
        scatter_steps(scatter, part, *bufs, at * count, count, results[at]) for at in (0, 1)
    ]
    for _ in range(5):
        next(first)
        next(second)
        tick()
    return results[0][0], results[1][0]


def scatter_scratch(rows, width):
    return [
        pltpu.VMEM((4, rows, width), BF16),
        pltpu.VMEM((3, rows, width), BF16),
        pltpu.VMEM((rows, width), BF16),
        pltpu.VMEM((2, rows, width), BF16),
    ]


def sems(count):
    return [pltpu.SemaphoreType.DMA((count,)), pltpu.SemaphoreType.DMA((count,))]


def plane_ring(axis):
    x, y, z, core = place()
    if axis == "x":
        return device(x + 1, y, z, core), device(x + 3, y, z, core)
    return device(x, y, z + 1, core), device(x, y, z + 3, core)


def plane_at(first, u, v):
    return block_of(u, v) if first == "x" else block_of(v, u)


PLANE_GATHER_COPIES = 36
PLANE_SCATTER_COPIES = 36


def gather_plane(copies, out):
    x, y, z, core = place()
    quarter = out.shape[1] // 4
    paths = []
    for first, base in (("x", 0), ("z", 2 * quarter)):
        v, u = (x, z) if first == "x" else (z, x)
        other = "z" if first == "x" else "x"
        paths.append(
            dict(
                first=first,
                v=v,
                u=u,
                ring=plane_ring(first),
                cross=plane_ring(other),
                halves=(pl.ds(base, quarter), pl.ds(base + quarter, quarter)),
                whole=pl.ds(base, 2 * quarter),
            )
        )

    def send(path, dv, du, rows, to):
        at = plane_at(path["first"], path["v"] + dv, path["u"] + du)
        return copies.start(out.at[at, rows], out.at[at, rows], to)

    for path in paths:
        after, before = path["ring"]
        top, low = path["halves"]
        path["ta"] = send(path, 0, 0, top, after)
        path["lb"] = send(path, 0, 0, low, before)
        path["la"] = send(path, 0, 0, low, after)
        path["tb"] = send(path, 0, 0, top, before)
        path["c"] = {0: [send(path, 0, 0, path["whole"], to) for to in path["cross"]]}
    yield
    for path in paths:
        path["ta"].wait_recv()
        path["ft"] = send(path, 3, 0, path["halves"][0], path["ring"][0])
        path["lb"].wait_recv()
        path["fl"] = send(path, 1, 0, path["halves"][1], path["ring"][1])
    yield
    for path in paths:
        path["la"].wait_recv()
        path["c"][3] = [send(path, 3, 0, path["whole"], to) for to in path["cross"]]
        path["tb"].wait_recv()
        path["c"][1] = [send(path, 1, 0, path["whole"], to) for to in path["cross"]]
    last = []
    for path in paths:
        path["c"][0][0].wait_recv()
        last.append(send(path, 0, 3, path["whole"], path["cross"][0]))
    yield
    for path in paths:
        path["ft"].wait_recv()
        path["fl"].wait_recv()
        path["c"][2] = [send(path, 2, 0, path["whole"], to) for to in path["cross"]]
    yield
    for path in paths:
        path["c"][3][0].wait_recv()
        last.append(send(path, 3, 3, path["whole"], path["cross"][0]))
        path["c"][1][1].wait_recv()
        last.append(send(path, 1, 1, path["whole"], path["cross"][1]))
    yield
    for path in paths:
        path["c"][2][1].wait_recv()
        last.append(send(path, 2, 1, path["whole"], path["cross"][1]))
    yield
    for path in paths:
        for copy in (path["c"][0][1], path["c"][3][1], path["c"][1][0], path["c"][2][0]):
            copy.wait_recv()
    for copy in last:
        copy.wait_recv()


def scatter_plane_scratch(rows, width):
    half = rows // 2
    return [
        pltpu.VMEM((2, 4, half, width), BF16),
        pltpu.VMEM((2, 2, 4, half, width), BF16),
        pltpu.VMEM((2, 4, half, width), BF16),
        pltpu.VMEM((2, 4, half, width), BF16),
        pltpu.VMEM((2, half, width), BF16),
        pltpu.VMEM((2, 2, half, width), BF16),
        pltpu.VMEM((2, 2, half // 2, width), BF16),
    ]


def scatter_plane(copies, part, out, far, near, passed, summed, far2, near2, passed2):
    x, y, z, core = place()
    half = part.shape[1] // 2
    quarter = half // 2
    paths = []
    for at, (first, base) in enumerate((("x", 0), ("z", half))):
        u, v = (x, z) if first == "x" else (z, x)
        other = "z" if first == "x" else "x"
        paths.append(
            dict(
                at=at,
                first=first,
                u=u,
                v=v,
                ring=plane_ring(first),
                cross=plane_ring(other),
                rows=pl.ds(base, half),
                base=base,
            )
        )

    def source(path, du, v):
        return (plane_at(path["first"], path["u"] + du, v), path["rows"])

    for path in paths:
        at, (after, before) = path["at"], path["ring"]
        path["far"] = [
            copies.start(
                part.at[source(path, 2, v)], far.at[at, v], after if v < 2 else before
            )
            for v in range(4)
        ]
    for path in paths:
        at, (after, before) = path["at"], path["ring"]
        path["near"] = [
            copies.start(part.at[source(path, 1, v)], near.at[at, 0, v], after) for v in (2, 3)
        ] + [
            copies.start(part.at[source(path, 3, v)], near.at[at, 1, v], before) for v in (0, 1)
        ]
    yield
    for path in paths:
        at, (after, before) = path["at"], path["ring"]
        for v in (0, 2, 1, 3):
            path["far"][v].wait_recv()
            du, slot, to = (1, 0, after) if v < 2 else (3, 1, before)
            own = part[source(path, du, v)].astype(F32)
            passed[at, v] = (own + far[at, v].astype(F32)).astype(BF16)
            path["near"].append(copies.start(passed.at[at, v], near.at[at, slot, v], to))
    yield
    for path in paths:
        at = path["at"]
        for copy in path["near"]:
            copy.wait_recv()
        for v in range(4):
            own = part[source(path, 0, v)].astype(F32)
            summed[at, v] = (
                own + near[at, 0, v].astype(F32) + near[at, 1, v].astype(F32)
            ).astype(BF16)
        v, (after, before) = path["v"], path["cross"]
        top, low = pl.ds(0, quarter), pl.ds(quarter, quarter)
        v1, v2, v3 = lax.rem(v + 1, 4), lax.rem(v + 2, 4), lax.rem(v + 3, 4)
        path["ft"] = copies.start(summed.at[at, v2, top], far2.at[at, top], after)
        path["fl"] = copies.start(summed.at[at, v2, low], far2.at[at, low], before)
        path["last"] = [
            copies.start(summed.at[at, v1, low], near2.at[at, 0, low], after),
            copies.start(summed.at[at, v3, top], near2.at[at, 1, top], before),
        ]
    yield
    for path in paths:
        at, v, (after, before) = path["at"], path["v"], path["cross"]
        top, low = pl.ds(0, quarter), pl.ds(quarter, quarter)
        v1, v3 = lax.rem(v + 1, 4), lax.rem(v + 3, 4)
        path["ft"].wait_recv()
        passed2[at, 0] = (summed[at, v1, top].astype(F32) + far2[at, top].astype(F32)).astype(BF16)
        path["last"].append(copies.start(passed2.at[at, 0], near2.at[at, 0, top], after))
        path["fl"].wait_recv()
        passed2[at, 1] = (summed[at, v3, low].astype(F32) + far2[at, low].astype(F32)).astype(BF16)
        path["last"].append(copies.start(passed2.at[at, 1], near2.at[at, 1, low], before))
    yield
    for path in paths:
        at, v = path["at"], path["v"]
        for copy in path["last"]:
            copy.wait_recv()
        total = summed[at, v].astype(F32) + near2[at, 0].astype(F32) + near2[at, 1].astype(F32)
        out[path["rows"]] = total.astype(out.dtype)


def params(number):
    return pltpu.CompilerParams(
        collective_id=number, has_side_effects=True, vmem_limit_bytes=48 * 2**20
    )


VMEM = pl.BlockSpec(memory_space=pltpu.VMEM)


def neighbours():
    return [*group_neighbours(), *plane_ring("x"), *plane_ring("z")]


def drain(steps):
    for _ in steps:
        pass


def swap_partner():
    x, y, z, core = place()
    upper = lax.div(x, 2)
    return core != upper, device(core * 2 + lax.rem(x, 2), y, z, upper)


def greet_with_partner(others):
    moves, partner = swap_partner()
    barrier = pltpu.get_barrier_semaphore()
    for other in others:
        pl.semaphore_signal(barrier, inc=1, device_id=other, device_id_type=MESH)

    @pl.when(moves)
    def _():
        pl.semaphore_signal(barrier, inc=1, device_id=partner, device_id_type=MESH)

    pl.semaphore_wait(barrier, len(others) + moves.astype(jnp.int32))


def partner_copy(src, dst, send, recv):
    return pltpu.make_async_remote_copy(
        src_ref=src,
        dst_ref=dst,
        send_sem=send,
        recv_sem=recv,
        device_id=swap_partner()[1],
        device_id_type=MESH,
    )


class Swaps:
    def __init__(self, send, recv):
        self.send, self.recv, self.moves = send, recv, []

    def copy(self, src, dst, own_dst=None):
        at = len(self.moves)
        copy = partner_copy(src, dst, self.send.at[at], self.recv.at[at])
        self.moves.append(copy)
        moves, _ = swap_partner()

        @pl.when(moves)
        def _():
            copy.start()

        @pl.when(jnp.logical_not(moves))
        def _():
            target = dst if own_dst is None else own_dst
            target[...] = src[...]

        return copy

    def arrive(self, copy):
        @pl.when(swap_partner()[0])
        def _():
            copy.wait_recv()

    def finish(self, *arrived):
        @pl.when(swap_partner()[0])
        def _():
            for copy in self.moves:
                copy.wait_send()
                if not any(copy is other for other in arrived):
                    copy.wait_recv()


def start_kernel(
    tokens, weights, lengths, later, rows_out, weights_out, lengths_out, later_out,
    ssend, srecv, send, recv, wsend, wrecv,
):
    x, y, z, core = place()
    greet_with_partner(neighbours())
    plane, group, swaps = Copies(wsend, wrecv), Copies(send, recv), Swaps(ssend, srecv)
    there = block_of(core * 2 + lax.rem(x, 2), z)
    own = weights_out.at[block_of(x, z)]
    weights_move = swaps.copy(weights, weights_out.at[there], own)
    own = rows_out.at[core * 4 + y]
    rows_move = swaps.copy(tokens, rows_out.at[lax.div(x, 2) * 4 + y], own)
    swaps.copy(lengths, lengths_out)
    swaps.copy(later, later_out)
    swaps.arrive(weights_move)
    steps = gather_plane(plane, weights_out)
    next(steps)
    swaps.arrive(rows_move)
    gather_all(group, rows_out, lambda: next(steps, None))
    drain(steps)
    swaps.finish(weights_move, rows_move)
    group.wait_sends()
    plane.wait_sends()


def start(tokens, weights, lengths, later):
    rows, width = tokens.shape
    held, columns = weights.shape
    gathered, full, lengths, later = pl.pallas_call(
        start_kernel,
        out_shape=(
            jax.ShapeDtypeStruct((8, rows, width), BF16),
            jax.ShapeDtypeStruct((16, held, columns), BF16),
            jax.ShapeDtypeStruct(lengths.shape, lengths.dtype),
            jax.ShapeDtypeStruct(later.shape, BF16),
        ),
        in_specs=[VMEM] * 4,
        out_specs=(VMEM,) * 4,
        scratch_shapes=sems(4) + sems(GATHER_COPIES) + sems(PLANE_GATHER_COPIES),
        compiler_params=params(0),
        name="start",
    )(tokens, weights, lengths, later)
    return gathered.reshape(8 * rows, width), full.reshape(16 * held, columns), lengths, later


def normed_parts(stream):
    row_mean = jnp.mean(stream, axis=-1, keepdims=True)
    centered = stream - row_mean
    row_var = jnp.mean(centered * centered, axis=-1, keepdims=True)
    scale = lax.rsqrt(row_var + EPSILON)
    return centered * scale, scale


def norm_pull(unit, scale, gain, grad, sums):
    scaled = grad * gain
    inner = jnp.mean(scaled * unit, axis=-1, keepdims=True)
    pulled = scale * (scaled - jnp.mean(scaled, axis=-1, keepdims=True) - unit * inner)
    low = pulled.astype(BF16)
    sums[0:1] += jnp.sum(grad * unit, axis=0, keepdims=True)
    sums[1:2] += jnp.sum(grad, axis=0, keepdims=True)
    sums[2:3] += jnp.sum(low.astype(F32), axis=0, keepdims=True)
    return pulled, low


def group_kernel(mode, plane_mode, swapped, count, kept, refs):
    refs = list(refs)
    take = lambda number: [refs.pop(0) for _ in range(number)]
    part, held, vectors, *extra = take(count)
    plane_in = take(1)[0] if plane_mode else None
    swaps_in = take(swapped)
    outs = take(kept)
    (rows_out,) = take(1)
    plane_out = take(1)[0] if plane_mode else None
    swaps_out = take(swapped)
    bufs = take(4)
    scatter, gather = Copies(*take(2)), Copies(*take(2))
    x, y, z, core = place()
    others = neighbours() if plane_mode else group_neighbours()
    if swapped:
        swaps = Swaps(*take(2))
        greet_with_partner(others)
    else:
        greet(others)
    steps = iter(())
    if plane_mode == "gather":
        plane = Copies(*take(2))
        plane_out[block_of(x, z)] = plane_in[...]
        steps = gather_plane(plane, plane_out)
    elif plane_mode == "scatter":
        plane = Copies(*take(2))
        steps = scatter_plane(plane, plane_in, plane_out, *refs)

    def tick():
        next(steps, None)

    gain, shift = vectors[1:2], vectors[2:3]
    if mode != "forward":
        sums = outs[-1]
        sums[...] = jnp.zeros_like(sums)

    def between(total, at, rows):
        if mode == "forward":
            stream = held[rows] + total + vectors[0:1]
            outs[0][rows] = stream
            unit, _ = normed_parts(stream)
            normed = unit * gain + shift
            outs[1][rows] = normed
            return normed.astype(BF16)
        if mode == "turn":
            unit, scale = normed_parts(held[rows] + total + vectors[0:1])
            outs[0][rows] = (unit * gain + shift).astype(BF16)
            pulled, low = norm_pull(unit, scale, gain, extra[0][rows].astype(F32), sums)
            outs[1][rows] = pulled
            return low
        unit, scale = normed_parts(extra[0][rows])
        pulled, low = norm_pull(unit, scale, gain, held[rows] + total, sums)
        outs[0][rows] = pulled
        return low

    def first_tick():
        if not started:
            started.append(True)
            for src, dst in zip(swaps_in, swaps_out):
                swaps.copy(src, dst)
        tick()

    started = []
    scatter_gather(scatter, gather, part, bufs, rows_out, between, first_tick)
    drain(steps)
    scatter.wait_sends()
    gather.wait_sends()
    if plane_mode:
        plane.wait_sends()
    if swapped:
        swaps.finish()


def group_call(mode, number, operands, outs, plane_mode=None, plane_in=None, swapped=()):
    part = operands[0]
    rows, width = part.shape[0] // 8, part.shape[1]
    shapes = tuple(jax.ShapeDtypeStruct(shape, kind) for shape, kind in outs)
    shapes += (jax.ShapeDtypeStruct((8, rows, width), BF16),)
    scratch = scatter_scratch(rows, width) + sems(SCATTER_COPIES) + sems(GATHER_COPIES)
    given = [part.reshape(8, rows, width), *operands[1:]]
    if swapped:
        scratch += sems(len(swapped))
    if plane_mode == "gather":
        kept, columns = plane_in.shape
        shapes += (jax.ShapeDtypeStruct((16, kept, columns), BF16),)
        scratch += sems(PLANE_GATHER_COPIES)
        given.append(plane_in)
    elif plane_mode == "scatter":
        kept, columns = plane_in.shape[0] // 16, plane_in.shape[1]
        shapes += (jax.ShapeDtypeStruct((kept, columns), BF16),)
        scratch += sems(PLANE_SCATTER_COPIES) + scatter_plane_scratch(kept, columns)
        given.append(plane_in.reshape(16, kept, columns))
    shapes += tuple(jax.ShapeDtypeStruct(array.shape, array.dtype) for array in swapped)
    given += swapped

    def kernel(*refs):
        group_kernel(mode, plane_mode, len(swapped), len(operands), len(outs), refs)

    results = pl.pallas_call(
        kernel,
        out_shape=shapes,
        in_specs=[VMEM] * len(given),
        out_specs=(VMEM,) * len(shapes),
        scratch_shapes=scratch,
        compiler_params=params(number),
        name=mode + str(number),
    )(*given)
    results = list(results)
    at = len(outs)
    results[at] = results[at].reshape(8 * rows, width)
    if plane_mode == "gather":
        results[at + 1] = results[at + 1].reshape(16 * kept, columns)
    return results


def sum_small(copies, small, out, got_x, got_z):
    x, y, z, core = place()
    own = core * 4 + y
    along_x = [device(x + step, y, z, core) for step in (1, 2, 3)]
    along_z = [device(x, y, z + step, core) for step in (1, 2, 3)]
    along_y = [device(x, y + step, z, core) for step in (1, 2, 3)]
    first = [copies.start(small, got_x.at[at], to) for at, to in enumerate(along_x)]
    yield
    for copy in first:
        copy.wait_recv()
    got_z[3] = small[...] + got_x[0] + got_x[1] + got_x[2]
    second = [copies.start(got_z.at[3], got_z.at[at], to) for at, to in enumerate(along_z)]
    yield
    for copy in second:
        copy.wait_recv()
    out[own] = got_z[3] + got_z[0] + got_z[1] + got_z[2]
    third = [copies.start(out.at[own], out.at[own], to) for to in along_y]
    yield
    for copy in third:
        copy.wait_recv()
    held = out.at[pl.ds(core * 4, 4)]
    copies.start(held, held, device(x, y, z, 1 - core)).wait_recv()


def end_kernel(
    part, held, grads, small, later, rows_out, grads_out, small_out, later_out,
    from_pair, staged, far, near, pfar, pnear, passed, summed, far2, near2, passed2,
    rows_stage, grads_stage, got_x, got_z,
    ssend, srecv, send, recv, psend, precv, tsend, trecv,
):
    x, y, z, core = place()
    greet_with_partner(
        neighbours()
        + [device(x + 2, y, z, core), device(x, y + 2, z, core), device(x, y, z + 2, core)]
    )
    group, plane, tiny = Copies(send, recv), Copies(psend, precv), Copies(tsend, trecv)
    swaps = Swaps(ssend, srecv)
    tiny_steps = sum_small(tiny, small, small_out, got_x, got_z)
    plane_steps = scatter_plane(
        plane, grads, grads_stage, pfar, pnear, passed, summed, far2, near2, passed2
    )
    started = []

    def tick():
        next(plane_steps, None)
        next(tiny_steps, None)
        if not started:
            started.append(swaps.copy(later, later_out))

    totals = scatter_all(group, part, (from_pair, staged, far, near), tick)
    count = rows_stage.shape[0] // 2
    for at in (0, 1):
        rows = pl.ds(at * count, count)
        rows_stage[rows] = (held[rows] + totals[at]).astype(BF16)
    swaps.copy(rows_stage, rows_out)
    drain(plane_steps)
    swaps.copy(grads_stage, grads_out)
    drain(tiny_steps)
    swaps.finish()
    group.wait_sends()
    plane.wait_sends()
    tiny.wait_sends()


def end(part, held, grads, small, later):
    rows, width = held.shape
    kept, columns = grads.shape[0] // 16, grads.shape[1]
    return pl.pallas_call(
        end_kernel,
        out_shape=(
            jax.ShapeDtypeStruct((rows, width), BF16),
            jax.ShapeDtypeStruct((kept, columns), BF16),
            jax.ShapeDtypeStruct((8, *small.shape), F32),
            jax.ShapeDtypeStruct(later.shape, BF16),
        ),
        in_specs=[VMEM] * 5,
        out_specs=(VMEM,) * 4,
        scratch_shapes=scatter_scratch(rows, width)
        + scatter_plane_scratch(kept, columns)
        + [
            pltpu.VMEM((rows, width), BF16),
            pltpu.VMEM((kept, columns), BF16),
            pltpu.VMEM((3, *small.shape), F32),
            pltpu.VMEM((4, *small.shape), F32),
        ]
        + sems(3)
        + sems(SCATTER_COPIES)
        + sems(PLANE_SCATTER_COPIES)
        + sems(10),
        compiler_params=params(1),
        name="end",
    )(part.reshape(8, rows, width), held, grads.reshape(16, kept, columns), small, later)


def segment_ids(shard_lengths, total_rows, seq_count):
    seq_ends = jnp.cumsum(shard_lengths)
    positions = jnp.arange(total_rows, dtype=jnp.int32)
    segments = jnp.sum((positions[:, None] >= seq_ends[None, :]).astype(jnp.int32), axis=1)
    return jnp.where(segments == seq_count, seq_count + positions, segments)


def masked_scores(queries, keys_in, allowed, score_scale):
    scores = (
        jnp.einsum("qhd,khd->hqk", queries, keys_in, preferred_element_type=jnp.float32)
        * score_scale
    )
    return jnp.where(allowed[None], scores, -1e30)


def attend_forward(queries, keys_in, values_in, allowed, score_scale):
    scores = masked_scores(queries, keys_in, allowed, score_scale)
    row_peak = jnp.max(scores, axis=-1, keepdims=True)
    exp_scores = jnp.exp(scores - row_peak)
    row_total = jnp.sum(exp_scores, axis=-1, keepdims=True)
    attn_probs = (exp_scores / row_total).astype(jnp.bfloat16)
    context = jnp.einsum("hqk,khd->qhd", attn_probs, values_in, preferred_element_type=jnp.float32)
    return (context, row_peak + jnp.log(row_total))


def attend_backward(queries, keys_in, values_in, allowed, score_scale, log_total, grad_context):
    scores = masked_scores(queries, keys_in, allowed, score_scale)
    attn_probs = jnp.exp(scores - log_total)
    probs_low = attn_probs.astype(jnp.bfloat16)
    grad_probs = jnp.einsum(
        "qhd,khd->hqk", grad_context, values_in, preferred_element_type=jnp.float32
    )
    grad_values = jnp.einsum(
        "hqk,qhd->khd", probs_low, grad_context, preferred_element_type=jnp.float32
    )
    row_inner = jnp.sum(attn_probs * grad_probs, axis=-1, keepdims=True)
    grad_scores = (attn_probs * (grad_probs - row_inner)).astype(jnp.bfloat16)
    grad_queries = (
        jnp.einsum("hqk,khd->qhd", grad_scores, keys_in, preferred_element_type=jnp.float32)
        * score_scale
    )
    grad_keys = (
        jnp.einsum("hqk,qhd->khd", grad_scores, queries, preferred_element_type=jnp.float32)
        * score_scale
    )
    return (grad_queries, grad_keys, grad_values)


def exact_gelu(values):
    return jax.nn.gelu(values, approximate=False)


CONTRACT_LAST = (((1,), (1,)), ((), ()))
CONTRACT_FIRST = (((0,), (0,)), ((), ()))


def shards(
    tokens,
    lengths,
    w_qkv,
    b_qv,
    w_out,
    b_out,
    w_in,
    b_in,
    w_down,
    b_down,
    ln_gain,
    ln_bias,
    cotangent,
):
    x, y, z, core = place()
    column = core * 4 + y
    own_rows, width = tokens.shape
    total_rows = own_rows * 8
    layers, kept = w_qkv.shape[:2]
    col_width = w_qkv.shape[3]
    hidden_width = w_in.shape[2]
    head_count = col_width // DH
    score_scale = DH ** (-0.5)
    cuts = (0, 3 * col_width, 4 * col_width, 4 * col_width + hidden_width)

    cut_out, cut_down = 3 * col_width, hidden_width
    attention_shards = [
        jnp.concatenate([w_qkv[at].reshape(kept, 3 * col_width), w_out[at].T], axis=1)
        for at in range(layers)
    ]
    hidden_shards = [
        jnp.concatenate([w_in[at], w_down[at].T], axis=1) for at in range(layers)
    ]
    later_shard = jnp.concatenate([attention_shards[1], hidden_shards[1]], axis=1)
    seq_count = lengths.shape[1]
    lengths = jnp.pad(lengths, ((0, 7), (0, 128 - seq_count)))
    attn_input, attention_full, lengths, first_hidden = start(
        tokens, attention_shards[0], lengths, hidden_shards[0]
    )
    hidden = lax.dynamic_slice_in_dim(attn_input, column * own_rows, own_rows, 0).astype(F32)

    segments = segment_ids(lengths[0, :seq_count], total_rows, seq_count)
    allowed = segments[:, None] == segments[None, :]

    def vectors(bias, at, which):
        rows = [bias.astype(F32), ln_gain[at, which].astype(F32), ln_bias[at, which].astype(F32)]
        return jnp.stack(rows + [jnp.zeros_like(rows[0])] * 5)

    row_kind = ((own_rows, width), F32)
    sum_kind = ((8, width), F32)
    low_kind = ((own_rows, width), BF16)
    stored = []
    for at in range(layers):
        if at > 0:
            attention_full, hidden_full = (
                later_full[:, : cut_out + col_width],
                later_full[:, cut_out + col_width :],
            )
        full_qkv, full_out = attention_full[:, :cut_out], attention_full[:, cut_out:]
        bias_qv = lax.dynamic_slice_in_dim(
            b_qv[at].astype(F32), column * col_width, col_width, 1
        )
        bias_all = jnp.concatenate([bias_qv[0], jnp.zeros_like(bias_qv[0]), bias_qv[1]])
        qkv = jnp.dot(attn_input, full_qkv, preferred_element_type=F32)
        qkv_low = (qkv + bias_all).astype(BF16)
        head_view = qkv_low.reshape(total_rows, 3, head_count, DH)
        context, log_total = attend_forward(
            head_view[:, 0], head_view[:, 1], head_view[:, 2], allowed, score_scale
        )
        context_low = context.reshape(total_rows, col_width).astype(BF16)
        branch = lax.dot_general(
            context_low, full_out, CONTRACT_LAST, preferred_element_type=F32
        ).astype(BF16)
        first_vectors = vectors(b_out[at], at, 0)
        if at == 0:
            first_sum, normed, mlp_input, hidden_full, later_shard, cotangent = group_call(
                "forward", 2, (branch, hidden, first_vectors), (row_kind, row_kind),
                "gather", first_hidden, (later_shard, cotangent),
            )
        else:
            first_sum, normed, mlp_input = group_call(
                "forward", 3, (branch, hidden, first_vectors), (row_kind, row_kind)
            )
        full_in, full_down = hidden_full[:, :cut_down], hidden_full[:, cut_down:]
        bias_in = lax.dynamic_slice_in_dim(
            b_in[at].astype(F32), column * hidden_width, hidden_width, 0
        )
        pre_gelu = jnp.dot(mlp_input, full_in, preferred_element_type=F32) + bias_in
        act_low = exact_gelu(pre_gelu).astype(BF16)
        branch = lax.dot_general(
            act_low, full_down, CONTRACT_LAST, preferred_element_type=F32
        ).astype(BF16)
        second_vectors = vectors(b_down[at], at, 1)
        stored.append(
            [attn_input, qkv_low, log_total, context_low, first_sum, mlp_input, pre_gelu,
             act_low, first_vectors, second_vectors, full_qkv, full_out, full_in, full_down]
        )
        if at == 0:
            second_sum, hidden, attn_input, later_full = group_call(
                "forward", 4, (branch, normed, second_vectors), (row_kind, row_kind),
                "gather", later_shard,
            )
            stored[at].append(second_sum)
        else:
            encoded, grad_second, sums_two, down_full = group_call(
                "turn",
                5,
                (branch, normed, second_vectors, cotangent),
                (low_kind, row_kind, sum_kind),
            )

    attention_grads, hidden_grads = [None] * layers, [None] * layers
    small_list = [None] * layers
    for at in reversed(range(layers)):
        (
            attn_input, qkv_low, log_total, context_low, first_sum, mlp_input, pre_gelu,
            act_low, first_vectors, second_vectors, full_qkv, full_out, full_in, full_down,
        ) = stored[at][:14]
        grad_act = jnp.dot(down_full, full_down, preferred_element_type=F32)
        grad_w_down = lax.dot_general(
            down_full, act_low, CONTRACT_FIRST, preferred_element_type=F32
        )
        pre_low = jax.vjp(exact_gelu, pre_gelu)[1](grad_act)[0].astype(BF16)
        grad_w_in = lax.dot_general(
            mlp_input, pre_low, CONTRACT_FIRST, preferred_element_type=F32
        )
        branch = lax.dot_general(
            pre_low, full_in, CONTRACT_LAST, preferred_element_type=F32
        ).astype(BF16)
        own_grads = jnp.concatenate([grad_w_in.astype(BF16), grad_w_down.astype(BF16)], axis=1)
        held_back = (encoded,) if at > 0 else (attention_grads[1],)
        grad_first, sums_one, attn_full, hidden_grads[at], *swapped = group_call(
            "backward", 6 + 2 * at, (branch, grad_second, first_vectors, first_sum),
            (row_kind, sum_kind), "scatter", own_grads, held_back,
        )
        if at > 0:
            (encoded,) = swapped
        else:
            (attention_grads[1],) = swapped
        grad_context = jnp.dot(attn_full, full_out, preferred_element_type=F32)
        grad_context_low = grad_context.astype(BF16).reshape(total_rows, head_count, DH)
        grad_w_out = lax.dot_general(
            attn_full, context_low, CONTRACT_FIRST, preferred_element_type=F32
        )
        head_view = qkv_low.reshape(total_rows, 3, head_count, DH)
        grad_queries, grad_keys, grad_values = attend_backward(
            head_view[:, 0], head_view[:, 1], head_view[:, 2],
            allowed, score_scale, log_total, grad_context_low,
        )
        grad_qkv_low = (
            jnp.stack([grad_queries, grad_keys, grad_values], axis=1)
            .reshape(total_rows, 3 * col_width)
            .astype(BF16)
        )
        grad_w_qkv = lax.dot_general(
            attn_input, grad_qkv_low, CONTRACT_FIRST, preferred_element_type=F32
        )
        branch = lax.dot_general(
            grad_qkv_low, full_qkv, CONTRACT_LAST, preferred_element_type=F32
        ).astype(BF16)
        own_grads = jnp.concatenate([grad_w_qkv.astype(BF16), grad_w_out.astype(BF16)], axis=1)
        qkv_sums = jnp.sum(grad_qkv_low.astype(F32), axis=0).reshape(3, col_width)
        own_sums = jnp.concatenate(
            [
                qkv_sums[0],
                qkv_sums[2],
                jnp.sum(pre_low.astype(F32), axis=0),
                jnp.zeros((width - 2 * col_width - hidden_width,), F32),
            ]
        )
        small_list[at] = jnp.concatenate(
            [sums_one[:3], sums_two[:3], own_sums[None], jnp.zeros((1, width), F32)]
        )
        if at > 0:
            grad_second, sums_two, down_full, attention_grads[at], hidden_grads[at] = group_call(
                "backward", 7, (branch, grad_first, stored[at - 1][9], stored[at - 1][14]),
                (row_kind, sum_kind), "scatter", own_grads, (hidden_grads[at],),
            )
        else:
            g_tokens, attention_grads[at], small, hidden_grads[at] = end(
                branch, grad_first, own_grads, jnp.concatenate(small_list), hidden_grads[at]
            )

    attention_grads = jnp.stack(attention_grads).astype(F32)
    hidden_grads = jnp.stack(hidden_grads).astype(F32)
    small = small.reshape(8, layers, 8, width)
    sums = jnp.sum(small[:, :, :6], axis=0)
    own_sums = small[:, :, 6].transpose(1, 0, 2)
    g_b_qv = jnp.stack(
        [own_sums[:, :, :col_width], own_sums[:, :, col_width : 2 * col_width]], axis=1
    )
    g_b_in = own_sums[:, :, 2 * col_width : 2 * col_width + hidden_width]
    return (
        encoded,
        g_tokens,
        attention_grads[:, :, :cut_out].reshape(layers, kept, 3, col_width),
        g_b_qv.reshape(layers, 2, width),
        attention_grads[:, :, cut_out:].transpose(0, 2, 1),
        sums[:, 2],
        hidden_grads[:, :, :cut_down],
        g_b_in.reshape(layers, -1),
        hidden_grads[:, :, cut_down:].transpose(0, 2, 1),
        sums[:, 5],
        jnp.stack([sums[:, 0], sums[:, 3]], axis=1),
        jnp.stack([sums[:, 1], sums[:, 4]], axis=1),
    )


def solution(mesh):
    placed = (
        P(("dp", "tensor"), None),
        P("dp", None),
        P(None, "dp", None, "tensor"),
        P(),
        P(None, "tensor", "dp"),
        P(),
        P(None, "dp", "tensor"),
        P(),
        P(None, "tensor", "dp"),
        P(),
        P(),
        P(),
        P(("dp", "tensor"), None),
    )
    return jax.shard_map(
        shards,
        mesh=mesh,
        in_specs=placed,
        out_specs=(
            P(("dp", "tensor"), None),
            P(("dp", "tensor"), None),
            P(None, "dp", None, "tensor"),
            P(),
            P(None, "tensor", "dp"),
            P(),
            P(None, "dp", "tensor"),
            P(),
            P(None, "tensor", "dp"),
            P(),
            P(),
            P(),
        ),
        check_vma=False,
    )
```

```python
import functools
import types

import jax
import jax.numpy as jnp
from jax import lax
from jax.experimental import pallas as pl
from jax.experimental.pallas import tpu as pltpu
from jax.sharding import PartitionSpec as P

DH = 64
EPSILON = 1e-06
MESH = pl.DeviceIdType.MESH
F32 = jnp.float32
BF16 = jnp.bfloat16


def place():
    dp, tensor = lax.axis_index("dp"), lax.axis_index("tensor")
    core = lax.rem(dp, 2)
    z = lax.rem(lax.div(dp, 2), 4)
    x = lax.rem(lax.div(tensor, 4) * 2 + lax.div(dp, 8), 4)
    y = lax.rem(tensor, 4)
    return x, y, z, core


def device(x, y, z, core):
    x, y, z = lax.rem(x, 4), lax.rem(y, 4), lax.rem(z, 4)
    return (lax.rem(x, 2) * 8 + z * 2 + core, lax.div(x, 2) * 4 + y)


def block_of(x, z):
    x, z = lax.rem(x, 4), lax.rem(z, 4)
    return lax.rem(x, 2) * 8 + z * 2 + lax.div(x, 2)


def greet(devices):
    barrier = pltpu.get_barrier_semaphore()
    for other in devices:
        pl.semaphore_signal(barrier, inc=1, device_id=other, device_id_type=MESH)
    pl.semaphore_wait(barrier, len(devices))


class Copies:
    def __init__(self, send, recv):
        self.send, self.recv, self.started = send, recv, []

    def start(self, src, dst, to):
        at = len(self.started)
        copy = pltpu.make_async_remote_copy(
            src_ref=src,
            dst_ref=dst,
            send_sem=self.send.at[at],
            recv_sem=self.recv.at[at],
            device_id=to,
            device_id_type=MESH,
        )
        copy.start()
        self.started.append(copy)
        return copy

    def wait_sends(self):
        for copy in self.started:
            copy.wait_send()


def group_neighbours():
    x, y, z, core = place()
    return (
        device(x, y, z, 1 - core),
        device(x, y + 1, z, core),
        device(x, y + 3, z, core),
    )


GATHER_COPIES = 24
SCATTER_COPIES = 20


class Gather:
    def __init__(self, copies, out, base, count):
        self.x, self.y, self.z, self.core = place()
        self.pair, self.after, self.before = group_neighbours()
        half = count // 2
        self.top, self.low = pl.ds(base, half), pl.ds(base + half, half)
        self.both = pl.ds(base, count)
        self.copies, self.out = copies, out

    def send(self, step, rows, to):
        ref = self.out.at[self.core * 4 + lax.rem(self.y + step, 4), rows]
        return self.copies.start(ref, ref, to)

    def f(self, low=None):
        if low is not None:
            self.out[self.core * 4 + self.y, self.both] = low
        self.top_after = self.send(0, self.top, self.after)
        self.low_before = self.send(0, self.low, self.before)

    def f2(self):
        self.low_after = self.send(0, self.low, self.after)
        self.top_before = self.send(0, self.top, self.before)

    def f3(self):
        self.paired = [self.send(0, self.both, self.pair)]

    def g(self):
        self.top_after.wait_recv()
        self.far_top = self.send(3, self.top, self.after)
        self.low_before.wait_recv()
        self.far_low = self.send(1, self.low, self.before)

    def h(self):
        self.low_after.wait_recv()
        self.paired.append(self.send(3, self.both, self.pair))
        self.top_before.wait_recv()
        self.paired.append(self.send(1, self.both, self.pair))

    def i(self):
        self.far_top.wait_recv()
        self.paired.append(self.send(2, self.top, self.pair))
        self.far_low.wait_recv()
        self.paired.append(self.send(2, self.low, self.pair))

    def j(self):
        for copy in self.paired:
            copy.wait_recv()


class Scatter:
    def __init__(self, copies, part, bufs, base, count):
        self.x, self.y, self.z, self.core = place()
        self.pair, self.after, self.before = group_neighbours()
        half = count // 2
        self.top, self.low = pl.ds(base, half), pl.ds(base + half, half)
        self.both = pl.ds(base, count)
        self.copies, self.part = copies, part
        self.from_pair, self.staged, self.far, self.near = bufs
        self.swaps = []

    STEPS = (2, 1, 3, 0)

    def swap(self, slot):
        at = (1 - self.core) * 4 + lax.rem(self.y + self.STEPS[slot], 4)
        src, dst = self.part.at[at, self.both], self.from_pair.at[slot, self.both]
        self.swaps.append(self.copies.start(src, dst, self.pair))

    def chip(self, slot, rows):
        own = self.part[self.core * 4 + lax.rem(self.y + self.STEPS[slot], 4), rows]
        return own.astype(F32) + self.from_pair[slot, rows].astype(F32)

    def pass_on(self, slot, rows, value, dst, to):
        self.staged[slot, rows] = value.astype(BF16)
        return self.copies.start(self.staged.at[slot, rows], dst, to)

    def a0(self):
        self.swap(0)

    def a1(self):
        for slot in (1, 2, 3):
            self.swap(slot)

    def b(self):
        self.swaps[0].wait_recv()
        top, low = self.top, self.low
        self.far_top = self.pass_on(0, top, self.chip(0, top), self.far.at[top], self.after)
        self.far_low = self.pass_on(0, low, self.chip(0, low), self.far.at[low], self.before)

    def c(self):
        top, low = self.top, self.low
        self.swaps[1].wait_recv()
        low_after = self.pass_on(1, low, self.chip(1, low), self.near.at[0, low], self.after)
        self.swaps[2].wait_recv()
        top_before = self.pass_on(2, top, self.chip(2, top), self.near.at[1, top], self.before)
        self.last = [low_after, top_before]

    def d(self):
        top, low = self.top, self.low
        self.far_top.wait_recv()
        value = self.chip(1, top) + self.far[top].astype(F32)
        self.last.append(self.pass_on(1, top, value, self.near.at[0, top], self.after))
        self.far_low.wait_recv()
        value = self.chip(2, low) + self.far[low].astype(F32)
        self.last.append(self.pass_on(2, low, value, self.near.at[1, low], self.before))

    def e(self):
        self.swaps[3].wait_recv()
        own = self.chip(3, self.both)
        for copy in self.last:
            copy.wait_recv()
        return own + self.near[0, self.both].astype(F32) + self.near[1, self.both].astype(F32)


OPENING = (
    "Aa0", "Ab", "Ba0", "Aa1", "Bb", "t", "Ac", "Ad", "t", "Ba1",
    "Bc", "Bd", "t",
)
MIDDLE = (
    "x", "x", "Ae", "Af", "Af2", "x", "x", "Be", "Bf", "Bf3",
    "Af3", "t", "Bf2", "x", "x", "Ag", "t", "Bg", "Bh", "x",
    "x", "t", "Ah", "Ai", "Aj",
)
TURN_ONE = (
    "Aw0", "+Aa0", "Bi", "+Aa1", "Aw1", "t", "+Ab", "Bj", "Bw0", "+Ba0",
)
TURN_TWO = (
    "t", "+Ac", "Bw1", "+Bb", "t", "+Ad", "+Ba1", "+Bc", "+Bd", "t",
)
CLOSING = (
    "Bi", "t", "Bj",
)


def run_chain(scatter, gather, stages, tick, before_work, after_work=None):
    x, y, z, core = place()
    count = stages[0]["part"].shape[1] // 2

    def steps_of(stage):
        return {
            half: (
                Scatter(scatter, stage["part"], stage["bufs"], at * count, count),
                Gather(gather, stage["rows"], at * count, count),
            )
            for at, half in enumerate("AB")
        }

    def run(order, stage, now, then=None):
        for name in order:
            if name == "t":
                tick()
                continue
            if name == "x":
                if stage.get("side"):
                    stage["side"].pop(0)()
                continue
            if name[0] == "+":
                steps, name = then, name[1:]
            else:
                steps = now
            half, name = name[0], name[1:]
            rows = pl.ds("AB".index(half) * count, count)
            own_scatter, own_gather = steps[half]
            if name == "e":
                stage[half] = own_scatter.e()
            elif name == "f":
                own_gather.f(stage["between"](stage[half], rows))
            elif name in ("w0", "w1"):
                blocks = pl.ds((core if name == "w1" else 1 - core) * 4, 4)
                stage["work"](blocks, rows)
            elif hasattr(own_scatter, name):
                getattr(own_scatter, name)()
            else:
                getattr(own_gather, name)()

    now = steps_of(stages[0])
    run(OPENING, stages[0], now)
    for at, stage in enumerate(stages):
        run(MIDDLE, stage, now)
        if at == len(stages) - 1:
            run(CLOSING, stage, now)
            break
        if at == 0:
            before_work()
        then = steps_of(stages[at + 1])
        run(TURN_ONE, stage, now, then)
        run(TURN_TWO, stage, now, then)
        if after_work is not None:
            after_work(at)
        now = then


def gather_all(gather, rows_out, tick, arrivals):
    count = rows_out.shape[1] // 2
    halves = [Gather(gather, rows_out, at * count, count) for at in (0, 1)]
    for half, arrive in zip(halves, arrivals):
        arrive()
        for name in ("f", "f2", "f3"):
            getattr(half, name)()
    for name in ("g", "h", "i", "j"):
        tick()
        for half in halves:
            getattr(half, name)()
        tick()


def scatter_all(scatter, part, bufs, tick):
    count = part.shape[1] // 2
    first, second = [Scatter(scatter, part, bufs, at * count, count) for at in (0, 1)]
    for name in OPENING:
        if name == "t":
            tick()
        else:
            getattr(first if name[0] == "A" else second, name[1:])()
    return first.e(), second.e()


def scatter_scratch(rows, width):
    return [
        pltpu.VMEM((4, rows, width), BF16),
        pltpu.VMEM((3, rows, width), BF16),
        pltpu.VMEM((rows, width), BF16),
        pltpu.VMEM((2, rows, width), BF16),
    ]


def sems(count):
    return [pltpu.SemaphoreType.DMA((count,)), pltpu.SemaphoreType.DMA((count,))]


def plane_ring(axis):
    x, y, z, core = place()
    if axis == "x":
        return device(x + 1, y, z, core), device(x + 3, y, z, core)
    return device(x, y, z + 1, core), device(x, y, z + 3, core)


def plane_at(first, u, v):
    return block_of(u, v) if first == "x" else block_of(v, u)


PLANE_GATHER_COPIES = 36
PLANE_SCATTER_COPIES = 36


def gather_plane(copies, out):
    x, y, z, core = place()
    quarter = out.shape[1] // 4
    paths = []
    for first, base in (("x", 0), ("z", 2 * quarter)):
        v, u = (x, z) if first == "x" else (z, x)
        other = "z" if first == "x" else "x"
        paths.append(
            types.SimpleNamespace(
                first=first,
                v=v,
                u=u,
                ring=plane_ring(first),
                cross=plane_ring(other),
                halves=(pl.ds(base, quarter), pl.ds(base + quarter, quarter)),
                whole=pl.ds(base, 2 * quarter),
            )
        )

    def send(path, dv, du, rows, to):
        at = plane_at(path.first, path.v + dv, path.u + du)
        return copies.start(out.at[at, rows], out.at[at, rows], to)

    for path in paths:
        after, before = path.ring
        top, low = path.halves
        path.ta = send(path, 0, 0, top, after)
        path.lb = send(path, 0, 0, low, before)
        path.la = send(path, 0, 0, low, after)
        path.tb = send(path, 0, 0, top, before)
        path.c = {0: [send(path, 0, 0, path.whole, to) for to in path.cross]}
    yield
    for path in paths:
        path.ta.wait_recv()
        path.ft = send(path, 3, 0, path.halves[0], path.ring[0])
        path.lb.wait_recv()
        path.fl = send(path, 1, 0, path.halves[1], path.ring[1])
    yield
    for path in paths:
        path.la.wait_recv()
        path.c[3] = [send(path, 3, 0, path.whole, to) for to in path.cross]
        path.tb.wait_recv()
        path.c[1] = [send(path, 1, 0, path.whole, to) for to in path.cross]
    last = []
    for path in paths:
        path.c[0][0].wait_recv()
        last.append(send(path, 0, 3, path.whole, path.cross[0]))
    yield
    for path in paths:
        path.ft.wait_recv()
        path.fl.wait_recv()
        path.c[2] = [send(path, 2, 0, path.whole, to) for to in path.cross]
    yield
    for path in paths:
        path.c[3][0].wait_recv()
        last.append(send(path, 3, 3, path.whole, path.cross[0]))
        path.c[1][1].wait_recv()
        last.append(send(path, 1, 1, path.whole, path.cross[1]))
    yield
    for path in paths:
        path.c[2][1].wait_recv()
        last.append(send(path, 2, 1, path.whole, path.cross[1]))
    yield
    for path in paths:
        for copy in (path.c[0][1], path.c[3][1], path.c[1][0], path.c[2][0]):
            copy.wait_recv()
    for copy in last:
        copy.wait_recv()


def scatter_plane_scratch(rows, width):
    half = rows // 2
    return [
        pltpu.VMEM((2, 4, half, width), BF16),
        pltpu.VMEM((2, 2, 4, half, width), BF16),
        pltpu.VMEM((2, 4, half, width), BF16),
        pltpu.VMEM((2, 4, half, width), BF16),
        pltpu.VMEM((2, half, width), BF16),
        pltpu.VMEM((2, 2, half, width), BF16),
        pltpu.VMEM((2, 2, half // 2, width), BF16),
    ]


def scatter_plane(copies, part, out, far, near, passed, summed, far2, near2, passed2):
    x, y, z, core = place()
    half = part.shape[1] // 2
    quarter = half // 2
    paths = []
    for at, (first, base) in enumerate((("x", 0), ("z", half))):
        u, v = (x, z) if first == "x" else (z, x)
        other = "z" if first == "x" else "x"
        paths.append(
            types.SimpleNamespace(
                at=at,
                first=first,
                u=u,
                v=v,
                ring=plane_ring(first),
                cross=plane_ring(other),
                rows=pl.ds(base, half),
                base=base,
            )
        )

    def source(path, du, v):
        return (plane_at(path.first, path.u + du, v), path.rows)

    for path in paths:
        at, (after, before) = path.at, path.ring
        path.far = [
            copies.start(
                part.at[source(path, 2, v)], far.at[at, v], after if v < 2 else before
            )
            for v in range(4)
        ]
    for path in paths:
        at, (after, before) = path.at, path.ring
        path.near = [
            copies.start(part.at[source(path, 1, v)], near.at[at, 0, v], after) for v in (2, 3)
        ] + [
            copies.start(part.at[source(path, 3, v)], near.at[at, 1, v], before) for v in (0, 1)
        ]
    yield
    for path in paths:
        at, (after, before) = path.at, path.ring
        for v in (0, 2, 1, 3):
            path.far[v].wait_recv()
            du, slot, to = (1, 0, after) if v < 2 else (3, 1, before)
            own = part[source(path, du, v)].astype(F32)
            passed[at, v] = (own + far[at, v].astype(F32)).astype(BF16)
            path.near.append(copies.start(passed.at[at, v], near.at[at, slot, v], to))
    yield
    for path in paths:
        at = path.at
        for copy in path.near:
            copy.wait_recv()
        for v in range(4):
            own = part[source(path, 0, v)].astype(F32)
            summed[at, v] = (
                own + near[at, 0, v].astype(F32) + near[at, 1, v].astype(F32)
            ).astype(BF16)
        v, (after, before) = path.v, path.cross
        top, low = pl.ds(0, quarter), pl.ds(quarter, quarter)
        v1, v2, v3 = lax.rem(v + 1, 4), lax.rem(v + 2, 4), lax.rem(v + 3, 4)
        path.ft = copies.start(summed.at[at, v2, top], far2.at[at, top], after)
        path.fl = copies.start(summed.at[at, v2, low], far2.at[at, low], before)
        path.last = [
            copies.start(summed.at[at, v1, low], near2.at[at, 0, low], after),
            copies.start(summed.at[at, v3, top], near2.at[at, 1, top], before),
        ]
    yield
    for path in paths:
        at, v, (after, before) = path.at, path.v, path.cross
        top, low = pl.ds(0, quarter), pl.ds(quarter, quarter)
        v1, v3 = lax.rem(v + 1, 4), lax.rem(v + 3, 4)
        path.ft.wait_recv()
        passed2[at, 0] = (summed[at, v1, top].astype(F32) + far2[at, top].astype(F32)).astype(BF16)
        path.last.append(copies.start(passed2.at[at, 0], near2.at[at, 0, top], after))
        path.fl.wait_recv()
        passed2[at, 1] = (summed[at, v3, low].astype(F32) + far2[at, low].astype(F32)).astype(BF16)
        path.last.append(copies.start(passed2.at[at, 1], near2.at[at, 1, low], before))
    yield
    for path in paths:
        at, v = path.at, path.v
        for copy in path.last:
            copy.wait_recv()
        total = summed[at, v].astype(F32) + near2[at, 0].astype(F32) + near2[at, 1].astype(F32)
        out[path.rows] = total.astype(out.dtype)


def params(number):
    return pltpu.CompilerParams(
        collective_id=number, has_side_effects=True, vmem_limit_bytes=56 * 2**20
    )


VMEM = pl.BlockSpec(memory_space=pltpu.VMEM)
HBM = pl.BlockSpec(memory_space=pl.ANY)


def neighbours():
    return [*group_neighbours(), *plane_ring("x"), *plane_ring("z")]


def drain(steps):
    for _ in steps:
        pass


def swap_partner():
    x, y, z, core = place()
    upper = lax.div(x, 2)
    return core != upper, device(core * 2 + lax.rem(x, 2), y, z, upper)


def greet_with_partner(others):
    moves, partner = swap_partner()
    barrier = pltpu.get_barrier_semaphore()
    for other in others:
        pl.semaphore_signal(barrier, inc=1, device_id=other, device_id_type=MESH)

    @pl.when(moves)
    def _():
        pl.semaphore_signal(barrier, inc=1, device_id=partner, device_id_type=MESH)

    pl.semaphore_wait(barrier, len(others) + moves.astype(jnp.int32))


def partner_copy(src, dst, send, recv):
    return pltpu.make_async_remote_copy(
        src_ref=src,
        dst_ref=dst,
        send_sem=send,
        recv_sem=recv,
        device_id=swap_partner()[1],
        device_id_type=MESH,
    )


class Swaps:
    def __init__(self, send, recv):
        self.send, self.recv, self.moves = send, recv, []

    def copy(self, src, dst, own_dst=None):
        at = len(self.moves)
        copy = partner_copy(src, dst, self.send.at[at], self.recv.at[at])
        self.moves.append(copy)
        moves, _ = swap_partner()

        @pl.when(moves)
        def _():
            copy.start()

        @pl.when(jnp.logical_not(moves))
        def _():
            target = dst if own_dst is None else own_dst
            target[...] = src[...]

        return copy

    def arrive(self, copy):
        @pl.when(swap_partner()[0])
        def _():
            copy.wait_recv()

    def finish(self, *arrived):
        @pl.when(swap_partner()[0])
        def _():
            for copy in self.moves:
                copy.wait_send()
                if not any(copy is other for other in arrived):
                    copy.wait_recv()


def start_kernel(
    tokens, attention, hidden, lengths, rows_out, weights_out, attention_out, hidden_out, lengths_out,
    ssend, srecv, send, recv, wsend, wrecv,
):
    x, y, z, core = place()
    greet_with_partner(neighbours())
    plane, group, swaps = Copies(wsend, wrecv), Copies(send, recv), Swaps(ssend, srecv)
    there = block_of(core * 2 + lax.rem(x, 2), z)
    own = weights_out.at[block_of(x, z)]
    weights_move = swaps.copy(attention.at[0], weights_out.at[there], own)
    count = tokens.shape[0] // 2
    rows_moves = []
    for half in (pl.ds(0, count), pl.ds(count, count)):
        own = rows_out.at[core * 4 + y, half]
        target = rows_out.at[lax.div(x, 2) * 4 + y, half]
        rows_moves.append(swaps.copy(tokens.at[half], target, own))
    swaps.copy(lengths, lengths_out)
    swaps.arrive(weights_move)
    steps = gather_plane(plane, weights_out)
    next(steps)
    arrivals = [functools.partial(swaps.arrive, move) for move in rows_moves]
    ticks = []

    def tick():
        ticks.append(None)
        next(steps, None)
        if len(ticks) == 3:
            swaps.copy(hidden, hidden_out)
            swaps.copy(attention.at[1], attention_out)

    gather_all(group, rows_out, tick, arrivals)
    drain(steps)
    swaps.finish(weights_move, *rows_moves)
    group.wait_sends()
    plane.wait_sends()


def start(tokens, attention, hidden, lengths):
    rows, width = tokens.shape
    _, held, columns = attention.shape
    shape = jax.ShapeDtypeStruct
    return pl.pallas_call(
        start_kernel,
        out_shape=(
            shape((8, rows, width), BF16),
            shape((16, held, columns), BF16),
            shape((held, columns), BF16),
            shape(hidden.shape, BF16),
            shape(lengths.shape, lengths.dtype),
        ),
        in_specs=[VMEM] * 4,
        out_specs=(VMEM,) * 5,
        scratch_shapes=sems(6) + sems(GATHER_COPIES) + sems(PLANE_GATHER_COPIES),
        compiler_params=params(0),
        name="start",
    )(tokens, attention, hidden, lengths)


def normed_parts(stream):
    row_mean = jnp.mean(stream, axis=-1, keepdims=True)
    centered = stream - row_mean
    row_var = jnp.mean(centered * centered, axis=-1, keepdims=True)
    scale = lax.rsqrt(row_var + EPSILON)
    return centered * scale, scale


def norm_pull(unit, scale, gain, grad, sums):
    scaled = grad * gain
    inner = jnp.mean(scaled * unit, axis=-1, keepdims=True)
    pulled = scale * (scaled - jnp.mean(scaled, axis=-1, keepdims=True) - unit * inner)
    low = pulled.astype(BF16)
    sums[0:1] += jnp.sum(grad * unit, axis=0, keepdims=True)
    sums[1:2] += jnp.sum(grad, axis=0, keepdims=True)
    sums[2:3] += jnp.sum(low.astype(F32), axis=0, keepdims=True)
    return pulled, low


INV_SQRT2 = 0.7071067811865476
INV_SQRT_2PI = 0.3989422804014327
CONTRACT_LAST = (((1,), (1,)), ((), ()))
CONTRACT_FIRST = (((0,), (0,)), ((), ()))


def normal_cdf(values):
    return 0.5 * (1.0 + lax.erf(values * INV_SQRT2))


def flatten(block):
    return block.reshape(block.shape[0] * block.shape[1], block.shape[2])


def hidden_forward(ref, hidden_width):
    def work(blocks, rows):
        full_in = flatten(ref.hidden_full[:, :, :hidden_width])
        full_down = flatten(ref.hidden_full[:, :, hidden_width:])
        values = flatten(ref.mlp_input[blocks, rows])
        pre_gelu = jnp.dot(values, full_in, preferred_element_type=F32) + ref.bias_in[ref.layer : ref.layer + 1]
        act = (pre_gelu * normal_cdf(pre_gelu)).astype(BF16)
        branch = lax.dot_general(act, full_down, CONTRACT_LAST, preferred_element_type=F32)
        shape = ref.mlp_input[blocks, rows].shape
        ref.pre_gelu[blocks, rows] = pre_gelu.reshape(*shape[:2], -1)
        ref.act[blocks, rows] = act.reshape(*shape[:2], -1)
        ref.branch_two[blocks, rows] = branch.astype(BF16).reshape(shape)

    return work


def hidden_backward(ref, hidden_width):
    def work(blocks, rows):
        full_in = flatten(ref.hidden_full[:, :, :hidden_width])
        full_down = flatten(ref.hidden_full[:, :, hidden_width:])
        values = flatten(ref.down_full[blocks, rows])
        grad_act = jnp.dot(values, full_down, preferred_element_type=F32)
        pre_gelu = flatten(ref.pre_gelu[blocks, rows])
        slope = normal_cdf(pre_gelu) + pre_gelu * (
            jnp.exp(pre_gelu * pre_gelu * -0.5) * INV_SQRT_2PI
        )
        low = (slope * grad_act).astype(BF16)
        branch = lax.dot_general(low, full_in, CONTRACT_LAST, preferred_element_type=F32)
        shape = ref.down_full[blocks, rows].shape
        ref.pre_low[blocks, rows] = low.reshape(*shape[:2], -1)
        ref.in_sums[0:1] += jnp.sum(low.astype(F32), axis=0, keepdims=True)
        ref.branch_three[blocks, rows] = branch.astype(BF16).reshape(shape)

    return work


def hidden_grads(ref, out):
    pieces = []
    into = out
    hidden_width = into.shape[2] // 2

    def piece(quarter, left, right, base):
        def work():
            values = flatten(left[:, :, quarter * 256 : (quarter + 1) * 256])
            grad = lax.dot_general(
                values, flatten(right[...]), CONTRACT_FIRST, preferred_element_type=F32
            )
            into[quarter * 4 : (quarter + 1) * 4, :, base : base + hidden_width] = grad.astype(
                BF16
            ).reshape(4, 64, hidden_width)

        return work

    for quarter in range(4):
        pieces.append(piece(quarter, ref.down_full, ref.act, hidden_width))
    for quarter in range(4):
        pieces.append(piece(quarter, ref.mlp_input, ref.pre_low, 0))
    return dict(side=pieces)


def param_rows(ref, at, which):
    rows = (2 * which + at, 4 + 2 * at + which, 8 + 2 * at + which)
    return [ref.params[row : row + 1] for row in rows]


def forward_norm(ref, held, at, which, stream_out, normed_out):
    def between(total, rows):
        bias, gain, shift = param_rows(ref, at, which)
        stream = held[rows].astype(F32) + total + bias
        stream_out[rows] = stream
        unit, _ = normed_parts(stream)
        normed = unit * gain + shift
        normed_out[rows] = normed
        return normed.astype(BF16)

    return between


def turn_norm(ref, held, at, which, pulled_out, sums):
    def between(total, rows):
        bias, gain, shift = param_rows(ref, at, which)
        unit, scale = normed_parts(held[rows] + total + bias)
        ref.encoded[rows] = (unit * gain + shift).astype(BF16)
        grad = ref.cotangent[rows].astype(F32)
        pulled, low = norm_pull(unit, scale, gain, grad, sums)
        pulled_out[rows] = pulled
        return low

    return between


def backward_norm(ref, held, at, which, stream, pulled_out, sums):
    def between(total, rows):
        unit, scale = normed_parts(stream[rows])
        grad = held[rows] + total
        pulled, low = norm_pull(unit, scale, param_rows(ref, at, which)[1], grad, sums)
        pulled_out[rows] = pulled
        return low

    return between


def zeroed(ref):
    if not hasattr(ref, "in_sums"):
        return ()
    return (ref.sums_one, ref.sums_two, ref.in_sums)


def chain_call(
    number, name, inputs, outputs, scratch, stages_of,
    gathers=(), scatters=(), swapped=(), late=(), early=(), pace=1, swapped_after=(),
):
    rows, width = 128, 1024
    names_in, names_out, names_scratch = list(inputs), list(outputs), list(scratch)
    stage_count = stages_of({}, True)
    shapes = []
    for key in names_out:
        shape, kind = outputs[key]
        shapes.append(jax.ShapeDtypeStruct(shape, kind))
    scratch_shapes = [pltpu.VMEM(shape, kind) for shape, kind in scratch.values()]
    for _ in range(stage_count):
        scratch_shapes += scatter_scratch(rows, width)
    scratch_shapes += sems(SCATTER_COPIES * stage_count) + sems(GATHER_COPIES * stage_count)
    pieces = [key for sources, _ in scatters for key in sources]
    stored = [key for keys, _ in early for key in keys]
    scratch_shapes += [pltpu.VMEM(inputs[key].shape, inputs[key].dtype) for key in late]
    scratch_shapes += [pltpu.VMEM(*outputs[key]) for key in stored]
    scratch_shapes += [pltpu.SemaphoreType.DMA((len(late) + len(stored) + len(pieces) + 1,))]
    for _ in gathers:
        scratch_shapes += sems(PLANE_GATHER_COPIES)
    for sources, out in scatters:
        kept, columns = {**outputs, **scratch}[out][0]
        scratch_shapes += [pltpu.VMEM((16, kept, columns), BF16)]
        scratch_shapes += sems(PLANE_SCATTER_COPIES) + scatter_plane_scratch(kept, columns)
    if swapped:
        scratch_shapes += sems(len(swapped) + len(swapped_after))

    def kernel(*refs):
        refs = list(refs)
        take = lambda count: [refs.pop(0) for _ in range(count)]
        ref = types.SimpleNamespace()
        held = vars(ref)
        for names in (names_in, names_out, names_scratch):
            held.update(zip(names, take(len(names))))
        bufs = [take(4) for _ in range(stage_count)]
        scatter, gather = Copies(*take(2)), Copies(*take(2))
        far_refs = {key: held[key] for key in (*late, *stored)}
        held.update(zip((*late, *stored), take(len(late) + len(stored))))
        (local,) = take(1)
        fetches, stores, count = [], [], []

        def local_copy(src, dst, kept):
            copy = pltpu.make_async_copy(src, dst, local.at[len(count)])
            copy.start()
            count.append(None)
            kept.append(copy)
            return copy

        for key in late:
            local_copy(far_refs[key], held[key], fetches)

        def after_work(at):
            for keys, stage in early:
                if stage == at:
                    for key in keys:
                        local_copy(held[key], far_refs[key], stores)

        x, y, z, core = place()
        others = neighbours() if gathers or scatters else group_neighbours()
        planes, queue = [], []
        for source, out in gathers:
            plane = Copies(*take(2))
            planes.append(plane)
            queue.append((gather_plane(plane, held[out]), (), True))
        for sources, out in scatters:
            (assembled,) = take(1)
            plane = Copies(*take(2))
            planes.append(plane)
            at, parts = 0, []
            for source in sources:
                columns = pl.ds(at, held[source].shape[-1])
                local_copy(held[source], assembled.at[:, :, columns], parts)
                at += held[source].shape[-1]
            steps = scatter_plane(plane, assembled, held[out], *take(7))
            queue.append((steps, parts, sources))
        stages = stages_of(ref, False)
        for stage, own in zip(stages, bufs):
            stage["bufs"] = own
        if swapped:
            swaps = Swaps(*take(2))
            greet_with_partner(others)
        else:
            greet(others)
        for sums in zeroed(ref):
            sums[...] = jnp.zeros_like(sums)
        for source, out in gathers:
            held[out][block_of(x, z)] = held[source][...]
        started, ended, ticks = [], [], [None] * (pace - 1)

        def tick():
            if not started:
                started.append(True)
                for _, parts, _ in queue:
                    for part in parts:
                        part.wait()
                for source, out in swapped:
                    swaps.copy(held[source], held[out])
            ticks.append(None)
            if len(ticks) % pace:
                return
            advance_planes()

        def advance_planes():
            while queue:
                try:
                    next(queue[0][0])
                    return
                except StopIteration:
                    queue.pop(0)
            if not ended:
                ended.append(True)
                for source, out in swapped_after:
                    swaps.copy(held[source], held[out])

        def before_work():
            if gathers and len(queue) == len(gathers) + len(scatters):
                drain(queue.pop(0)[0])
            for copy in fetches:
                copy.wait()
            fetches.clear()

        run_chain(scatter, gather, stages, tick, before_work, after_work)
        for steps, *_ in queue:
            drain(steps)
        queue.clear()
        advance_planes()
        for copies in (scatter, gather, *planes):
            copies.wait_sends()
        for copy in stores:
            copy.wait()
        if swapped:
            swaps.finish()

    results = pl.pallas_call(
        kernel,
        out_shape=tuple(shapes),
        in_specs=[HBM if key in (*late, *pieces) else VMEM for key in names_in],
        out_specs=tuple(HBM if key in stored else VMEM for key in names_out),
        scratch_shapes=scratch_shapes,
        compiler_params=params(number),
        name=name,
    )(*inputs.values())
    return dict(zip(names_out, results))


def sum_small(copies, small, out, got_x, got_z):
    x, y, z, core = place()
    own = core * 4 + y
    along_x = [device(x + step, y, z, core) for step in (1, 2, 3)]
    along_z = [device(x, y, z + step, core) for step in (1, 2, 3)]
    along_y = [device(x, y + step, z, core) for step in (1, 2, 3)]
    first = [copies.start(small, got_x.at[at], to) for at, to in enumerate(along_x)]
    yield
    for copy in first:
        copy.wait_recv()
    got_z[3] = small[...] + got_x[0] + got_x[1] + got_x[2]
    second = [copies.start(got_z.at[3], got_z.at[at], to) for at, to in enumerate(along_z)]
    yield
    for copy in second:
        copy.wait_recv()
    out[own] = got_z[3] + got_z[0] + got_z[1] + got_z[2]
    third = [copies.start(out.at[own], out.at[own], to) for to in along_y]
    yield
    for copy in third:
        copy.wait_recv()
    held = out.at[pl.ds(core * 4, 4)]
    copies.start(held, held, device(x, y, z, 1 - core)).wait_recv()


def end_kernel(*refs):
    refs = list(refs)
    take = lambda count: [refs.pop(0) for _ in range(count)]
    part, held, *pieces = take(5)
    layer_sums = [take(4), take(4)]
    rows_out, grads_out, small_out = take(3)
    grads, local = take(2)
    bufs, plane_bufs = take(4), take(7)
    rows_stage, grads_stage, small, got_x, got_z = take(5)
    swaps, group, plane, tiny = Swaps(*take(2)), Copies(*take(2)), Copies(*take(2)), Copies(*take(2))
    x, y, z, core = place()
    at, fetches = 0, []
    for number, piece in enumerate(pieces):
        columns = pl.ds(at, piece.shape[2])
        fetches.append(pltpu.make_async_copy(piece, grads.at[:, :, columns], local.at[number]))
        fetches[-1].start()
        at += piece.shape[2]
    small[...] = jnp.zeros_like(small)
    for base, (sums_one, sums_two, qkv_sums, in_sums) in zip((0, 8), layer_sums):
        third, hidden_width = qkv_sums.shape[1] // 3, in_sums.shape[1]
        small[base : base + 3] = sums_one[0:3]
        small[base + 3 : base + 6] = sums_two[0:3]
        small[base + 6 : base + 7, :third] = qkv_sums[0:1, :third]
        small[base + 6 : base + 7, third : 2 * third] = qkv_sums[0:1, 2 * third :]
        small[base + 6 : base + 7, 2 * third : 2 * third + hidden_width] = in_sums[0:1]
    greet_with_partner(
        neighbours()
        + [device(x + 2, y, z, core), device(x, y + 2, z, core), device(x, y, z + 2, core)]
    )
    tiny_steps = sum_small(tiny, small, small_out, got_x, got_z)
    plane_steps = scatter_plane(plane, grads, grads_stage, *plane_bufs)
    ticks = []

    def tick():
        ticks.append(None)
        if len(ticks) == 1:
            next(tiny_steps)
            for copy in fetches:
                copy.wait()
            next(plane_steps)
        elif len(ticks) == 2:
            next(tiny_steps)
        elif len(ticks) == 3:
            next(plane_steps)

    totals = scatter_all(group, part, bufs, tick)
    count = rows_stage.shape[0] // 2
    for at in (0, 1):
        rows = pl.ds(at * count, count)
        rows_stage[rows] = (held[rows] + totals[at]).astype(BF16)
    swaps.copy(rows_stage, rows_out)
    next(plane_steps)
    next(tiny_steps)
    next(plane_steps)
    drain(tiny_steps)
    drain(plane_steps)
    swaps.copy(grads_stage, grads_out)
    swaps.finish()
    group.wait_sends()
    plane.wait_sends()
    tiny.wait_sends()


def end(part, held, pieces, layer_sums):
    rows, width = held.shape
    kept, columns = pieces[0].shape[1], sum(piece.shape[2] for piece in pieces)
    shape = jax.ShapeDtypeStruct
    return pl.pallas_call(
        end_kernel,
        out_shape=(
            shape((rows, width), BF16),
            shape((kept, columns), BF16),
            shape((8, 16, width), F32),
        ),
        in_specs=[VMEM] * 2 + [HBM] * 3 + [VMEM] * 8,
        out_specs=(VMEM,) * 3,
        scratch_shapes=[pltpu.VMEM((16, kept, columns), BF16), pltpu.SemaphoreType.DMA((3,))]
        + scatter_scratch(rows, width)
        + scatter_plane_scratch(kept, columns)
        + [
            pltpu.VMEM((rows, width), BF16),
            pltpu.VMEM((kept, columns), BF16),
            pltpu.VMEM((16, width), F32),
            pltpu.VMEM((3, 16, width), F32),
            pltpu.VMEM((4, 16, width), F32),
        ]
        + sems(2)
        + sems(SCATTER_COPIES)
        + sems(PLANE_SCATTER_COPIES)
        + sems(10),
        compiler_params=params(1),
        name="end",
    )(part, held, *pieces, *layer_sums[0], *layer_sums[1])


def finish_kernel(
    small, zero, one,
    g_qkv, g_b_qv, g_out, g_b_out, g_in, g_b_in, g_down, g_b_down, g_gain, g_shift,
):
    third, hidden_width = g_out.shape[1], g_in.shape[2]
    cut = 4 * third
    for at, grads in enumerate((zero, one)):
        for which in range(3):
            columns = slice(which * third, (which + 1) * third)
            g_qkv[at, :, which] = grads[:, columns].astype(F32)
        g_out[at] = grads[:, 3 * third : cut].astype(F32).T
        g_in[at] = grads[:, cut : cut + hidden_width].astype(F32)
        g_down[at] = grads[:, cut + hidden_width :].astype(F32).T
        rows = jnp.sum(small[:, at * 8 : at * 8 + 8], axis=0)
        g_gain[at, 0:1], g_shift[at, 0:1], g_b_out[at : at + 1] = rows[0:1], rows[1:2], rows[2:3]
        g_gain[at, 1:2], g_shift[at, 1:2], g_b_down[at : at + 1] = rows[3:4], rows[4:5], rows[5:6]
        for block in range(8):
            row = small[block, at * 8 + 6 : at * 8 + 7]
            columns = slice(block * third, (block + 1) * third)
            g_b_qv[at, 0:1, columns] = row[:, :third]
            g_b_qv[at, 1:2, columns] = row[:, third : 2 * third]
            columns = slice(block * hidden_width, (block + 1) * hidden_width)
            g_b_in[at : at + 1, columns] = row[:, 2 * third : 2 * third + hidden_width]


def finish(small, zero, one, third):
    kept, hidden_width = zero.shape[0], (zero.shape[1] - 4 * third) // 2
    width = small.shape[2]
    shapes = (
        (2, kept, 3, third),
        (2, 2, width),
        (2, third, kept),
        (2, width),
        (2, kept, hidden_width),
        (2, 8 * hidden_width),
        (2, hidden_width, kept),
        (2, width),
        (2, 2, width),
        (2, 2, width),
    )
    return pl.pallas_call(
        finish_kernel,
        out_shape=tuple(jax.ShapeDtypeStruct(shape, F32) for shape in shapes),
        in_specs=[VMEM] * 3,
        out_specs=(VMEM,) * len(shapes),
        compiler_params=pltpu.CompilerParams(vmem_limit_bytes=48 * 2**20),
        name="finish",
    )(small, zero, one)


HEAD_SCALE = DH ** (-0.5)


def segment_parts(lengths, rows):
    def of(shape, dim):
        positions = lax.broadcasted_iota(jnp.int32, shape, dim)
        end, segments = 0, jnp.zeros(shape, jnp.int32)
        for at in range(4):
            end = end + lengths[0, at]
            segments += (positions >= end).astype(jnp.int32)
        return jnp.where(segments == 4, 4 + positions, segments)

    return of((rows, 1), 0), of((1, rows), 1)


def head_lanes(values, head):
    lanes = lax.broadcasted_iota(jnp.int32, values.shape, 1)
    return jnp.where((lanes >= head * DH) & (lanes < (head + 1) * DH), values, 0)


def pick_heads(parts):
    features = lax.broadcasted_iota(jnp.int32, parts[0].shape, 0)
    return jnp.where(features < DH, parts[0], parts[1])


CHUNK = 512


def attend_kernel(lengths, rows, weights, bias, qkv_out, context_out, lse_out, branch_out, v_turned, seg_row):
    total, width = rows.shape[0], context_out.shape[1]
    column, row = segment_parts(lengths, total)
    seg_row[...] = jnp.broadcast_to(row, seg_row.shape)

    def chunk(at):
        return pl.ds(pl.multiple_of(at * CHUNK, CHUNK), CHUNK)

    @pl.loop(0, total // CHUNK)
    def _(at):
        r = chunk(at)
        qkv = jnp.dot(rows[r], weights[:, : 3 * width], preferred_element_type=F32)
        qkv_out[r] = (qkv + bias[0:1]).astype(BF16)

    keys = qkv_out[:, width : 2 * width]
    v_turned[...] = qkv_out[:, 2 * width :].astype(F32).T.astype(BF16)

    @pl.loop(0, total // CHUNK)
    def _(at):
        r = chunk(at)
        queries = qkv_out[r, :width].astype(F32) * HEAD_SCALE
        allowed = column == seg_row[0:1, r]
        parts = []
        for head in range(2):
            own = head_lanes(queries, head).astype(BF16)
            scores = lax.dot_general(keys, own, CONTRACT_LAST, preferred_element_type=F32)
            scores = jnp.where(allowed, scores, -1e30)
            peak = jnp.max(scores, axis=0, keepdims=True)
            raised = jnp.exp(scores - peak)
            total_row = jnp.sum(raised, axis=0, keepdims=True)
            probs = (raised * (1.0 / total_row)).astype(BF16)
            parts.append(jnp.dot(v_turned[...], probs, preferred_element_type=F32))
            lse_out[head : head + 1, r] = peak + jnp.log(total_row)
        context = pick_heads(parts).T.astype(BF16)
        context_out[r] = context
        branch = lax.dot_general(
            context, weights[:, 3 * width :], CONTRACT_LAST, preferred_element_type=F32
        )
        branch_out[r] = branch.astype(BF16)


def attend(lengths, rows, weights, bias):
    total, width = rows.shape[0], weights.shape[1] // 4
    shape = jax.ShapeDtypeStruct
    return pl.pallas_call(
        attend_kernel,
        out_shape=(
            shape((total, 3 * width), BF16),
            shape((total, width), BF16),
            shape((8, total), F32),
            shape((total, rows.shape[1]), BF16),
        ),
        in_specs=[pl.BlockSpec(memory_space=pltpu.SMEM)] + [VMEM] * 3,
        out_specs=(VMEM,) * 4,
        scratch_shapes=[pltpu.VMEM((width, total), BF16), pltpu.VMEM((8, total), jnp.int32)],
        compiler_params=pltpu.CompilerParams(vmem_limit_bytes=48 * 2**20),
        name="attend",
    )(lengths, rows, weights, bias)


def attend_back_kernel(
    lengths, grad_rows, rows, weights, qkv, context, lse,
    g_qkv, g_out, branch_out, sums_out,
    grad_context, grad_qkv, k_turned, k_sum, v_sum, seg_row,
):
    total, width = rows.shape[0], context.shape[1]
    column, row = segment_parts(lengths, total)
    seg_row[...] = jnp.broadcast_to(row, seg_row.shape)

    def chunk(at):
        return pl.ds(pl.multiple_of(at * CHUNK, CHUNK), CHUNK)

    @pl.loop(0, total // CHUNK)
    def _(at):
        r = chunk(at)
        grad_context[r] = jnp.dot(
            grad_rows[r], weights[:, 3 * width :], preferred_element_type=F32
        ).astype(BF16)

    keys, values = qkv[:, width : 2 * width], qkv[:, 2 * width :]
    k_turned[...] = keys.astype(F32).T.astype(BF16)
    k_sum[...] = jnp.zeros_like(k_sum)
    v_sum[...] = jnp.zeros_like(v_sum)

    @pl.loop(0, total // CHUNK)
    def _(at):
        r = chunk(at)
        queries = qkv[r, :width].astype(F32) * HEAD_SCALE
        grads = grad_context[r].astype(F32)
        allowed = column == seg_row[0:1, r]
        parts = []
        for head in range(2):
            own = head_lanes(queries, head).astype(BF16)
            own_grads = head_lanes(grads, head).astype(BF16)
            scores = lax.dot_general(keys, own, CONTRACT_LAST, preferred_element_type=F32)
            scores = jnp.where(allowed, scores, -1e30)
            probs = jnp.exp(scores - lse[head : head + 1, r])
            grad_probs = lax.dot_general(
                values, own_grads, CONTRACT_LAST, preferred_element_type=F32
            )
            v_sum[...] += jnp.dot(probs.astype(BF16), own_grads, preferred_element_type=F32)
            inner = jnp.sum(probs * grad_probs, axis=0, keepdims=True)
            grad_scores = (probs * (grad_probs - inner)).astype(BF16)
            k_sum[...] += jnp.dot(grad_scores, own, preferred_element_type=F32)
            parts.append(jnp.dot(k_turned[...], grad_scores, preferred_element_type=F32))
        grad_qkv[r, :width] = (pick_heads(parts).T * HEAD_SCALE).astype(BF16)

    grad_qkv[:, width : 2 * width] = k_sum[...].astype(BF16)
    grad_qkv[:, 2 * width :] = v_sum[...].astype(BF16)
    sums_out[...] = jnp.broadcast_to(
        jnp.sum(grad_qkv[...].astype(F32), axis=0, keepdims=True), sums_out.shape
    )

    @pl.loop(0, total // CHUNK)
    def _(at):
        r = chunk(at)
        branch = lax.dot_general(
            grad_qkv[r], weights[:, : 3 * width], CONTRACT_LAST, preferred_element_type=F32
        )
        branch_out[r] = branch.astype(BF16)

    @pl.loop(0, rows.shape[1] // CHUNK)
    def _(at):
        c = chunk(at)
        turned = lax.dot_general(
            grad_qkv[...], rows[:, c], CONTRACT_FIRST, preferred_element_type=F32
        )
        g_qkv[c] = turned.T.astype(BF16)
        turned = lax.dot_general(
            context[...], grad_rows[:, c], CONTRACT_FIRST, preferred_element_type=F32
        )
        g_out[c] = turned.T.astype(BF16)


def attend_back(lengths, grad_rows, rows, weights, qkv, context, lse):
    total, width = context.shape
    depth = rows.shape[1]
    shape = jax.ShapeDtypeStruct
    return pl.pallas_call(
        attend_back_kernel,
        out_shape=(
            shape((depth, 3 * width), BF16),
            shape((depth, width), BF16),
            shape((total, depth), BF16),
            shape((8, 3 * width), F32),
        ),
        in_specs=[pl.BlockSpec(memory_space=pltpu.SMEM)] + [VMEM] * 6,
        out_specs=(VMEM,) * 4,
        scratch_shapes=[
            pltpu.VMEM((total, width), BF16),
            pltpu.VMEM((total, 3 * width), BF16),
            pltpu.VMEM((width, total), BF16),
            pltpu.VMEM((total, width), F32),
            pltpu.VMEM((total, width), F32),
            pltpu.VMEM((8, total), jnp.int32),
        ],
        compiler_params=pltpu.CompilerParams(vmem_limit_bytes=48 * 2**20),
        name="attend_back",
    )(lengths, grad_rows, rows, weights, qkv, context, lse)


def shards(
    tokens,
    lengths,
    w_qkv,
    b_qv,
    w_out,
    b_out,
    w_in,
    b_in,
    w_down,
    b_down,
    ln_gain,
    ln_bias,
    cotangent,
):
    x, y, z, core = place()
    column = core * 4 + y
    own_rows, width = tokens.shape
    total_rows = own_rows * 8
    layers, kept = w_qkv.shape[:2]
    col_width = w_qkv.shape[3]
    hidden_width = w_in.shape[2]

    attention_shards = jnp.concatenate(
        [w_qkv.reshape(layers, kept, 3 * col_width), w_out.transpose(0, 2, 1)], axis=2
    )
    hidden_shards = jnp.concatenate([w_in, w_down.transpose(0, 2, 1)], axis=2)
    lengths = jnp.pad(lengths, ((0, 7), (0, 128 - lengths.shape[1])))
    rows_zero, attention_zero, attention_shard, hidden_moved, lengths = start(
        tokens, attention_shards, hidden_shards, lengths
    )
    hidden = lax.dynamic_index_in_dim(rows_zero, column, 0, keepdims=False)

    norm_params = jnp.concatenate(
        [b_out, b_down, ln_gain.reshape(4, width), ln_bias.reshape(4, width)]
    ).astype(F32)
    bias_in = lax.dynamic_slice_in_dim(b_in, column * hidden_width, hidden_width, 1).astype(F32)
    bias_qv = lax.dynamic_slice_in_dim(b_qv, column * col_width, col_width, 2).astype(F32)
    bias_qkv = jnp.concatenate(
        [bias_qv[:, 0], jnp.zeros((layers, col_width), F32), bias_qv[:, 1]], axis=1
    )

    own_kind = ((own_rows, width), F32)
    sum_kind = ((8, width), F32)
    low_kind = ((own_rows, width), BF16)
    all_kind = ((8, own_rows, width), BF16)
    act_kind = ((8, own_rows, hidden_width), BF16)
    gelu_kind = ((8, own_rows, hidden_width), F32)
    in_sum_kind = ((8, hidden_width), F32)
    hidden_kind = ((16, kept, 2 * hidden_width), BF16)
    attention_kind = ((16, kept, 4 * col_width), BF16)
    grads_kind = ((kept, 4 * col_width + 2 * hidden_width), BF16)

    def attention(at, rows, full):
        rows, full = rows.reshape(total_rows, width), full.reshape(width, 4 * col_width)
        qkv, context, lse, branch = attend(lengths, rows, full, bias_qkv[at : at + 1])
        return branch.reshape(all_kind[0]), (rows, full, qkv, context, lse)

    def attention_back(stored, rows):
        grad_rows = rows.reshape(total_rows, width)
        g_qkv, g_out, branch, sums = attend_back(lengths, grad_rows, *stored)
        pieces = (g_qkv.reshape(16, kept, -1), g_out.reshape(16, kept, -1))
        return branch.reshape(all_kind[0]), pieces, sums

    branch, stored_zero = attention(0, rows_zero, attention_zero)

    def zero_stages(ref, counting):
        if counting:
            return 2
        ref.layer = 0
        return [
            dict(
                part=ref.branch,
                rows=ref.mlp_input,
                between=forward_norm(ref, ref.held, 0, 0, ref.first_sum, ref.normed),
                work=hidden_forward(ref, hidden_width),
            ),
            dict(
                part=ref.branch_two,
                rows=ref.rows,
                between=forward_norm(ref, ref.normed, 0, 1, ref.second_sum, ref.hidden),
            ),
        ]

    zero = chain_call(
        2,
        "layer_zero",
        dict(
            branch=branch,
            held=hidden,
            params=norm_params,
            bias_in=bias_in,
            hidden_shard=hidden_moved[0],
            attention_shard=attention_shard,
            next_cotangent=cotangent,
        ),
        dict(
            first_sum=own_kind,
            second_sum=own_kind,
            hidden=own_kind,
            mlp_input=all_kind,
            pre_gelu=gelu_kind,
            act=act_kind,
            rows=all_kind,
            hidden_full=hidden_kind,
            attention_full=attention_kind,
            moved_cotangent=low_kind,
        ),
        dict(normed=own_kind, branch_two=all_kind),
        zero_stages,
        gathers=(("hidden_shard", "hidden_full"), ("attention_shard", "attention_full")),
        swapped=(("next_cotangent", "moved_cotangent"),),
        early=((("first_sum", "mlp_input", "pre_gelu", "act", "hidden_full"), 0),),
    )

    branch, stored_one = attention(1, zero["rows"], zero["attention_full"])

    def one_stages(ref, counting):
        if counting:
            return 3
        ref.layer = 1
        return [
            dict(
                part=ref.branch,
                rows=ref.mlp_input,
                between=forward_norm(ref, ref.held, 1, 0, ref.first_sum, ref.normed),
                work=hidden_forward(ref, hidden_width),
            ),
            dict(
                part=ref.branch_two,
                rows=ref.down_full,
                between=turn_norm(ref, ref.normed, 1, 1, ref.pulled, ref.sums_two),
                work=hidden_backward(ref, hidden_width),
            ),
            dict(
                part=ref.branch_three,
                rows=ref.rows,
                between=backward_norm(ref, ref.pulled, 1, 0, ref.first_sum, ref.grad_first, ref.sums_one),
                **hidden_grads(ref, ref.grads),
            ),
        ]

    one = chain_call(
        3,
        "layer_one",
        dict(
            branch=branch,
            held=zero["hidden"],
            params=norm_params,
            bias_in=bias_in,
            hidden_shard=hidden_moved[1],
            cotangent=zero["moved_cotangent"],
        ),
        dict(
            encoded=low_kind,
            grad_first=own_kind,
            sums_one=sum_kind,
            sums_two=sum_kind,
            in_sums=in_sum_kind,
            rows=all_kind,
            grads=hidden_kind,
        ),
        dict(
            mlp_input=all_kind,
            act=act_kind,
            down_full=all_kind,
            pre_low=act_kind,
            first_sum=own_kind,
            normed=own_kind,
            pulled=own_kind,
            pre_gelu=gelu_kind,
            hidden_full=hidden_kind,
            branch_two=all_kind,
            branch_three=all_kind,
        ),
        one_stages,
        gathers=(("hidden_shard", "hidden_full"),),
        early=((("encoded",), 1),),
    )
    branch, pieces, qkv_sums_one = attention_back(stored_one, one["rows"])

    def back_stages(ref, counting):
        if counting:
            return 2
        return [
            dict(
                part=ref.branch,
                rows=ref.down_full,
                between=backward_norm(ref, ref.held, 0, 1, ref.second_sum, ref.pulled, ref.sums_two),
                work=hidden_backward(ref, hidden_width),
            ),
            dict(
                part=ref.branch_three,
                rows=ref.rows,
                between=backward_norm(ref, ref.pulled, 0, 0, ref.first_sum, ref.grad_first, ref.sums_one),
                **hidden_grads(ref, ref.grads),
            ),
        ]

    back = chain_call(
        4,
        "layer_back",
        dict(
            branch=branch,
            held=one["grad_first"],
            params=norm_params,
            first_sum=zero["first_sum"],
            second_sum=zero["second_sum"],
            pre_gelu=zero["pre_gelu"],
            hidden_full=zero["hidden_full"],
            mlp_input=zero["mlp_input"],
            act=zero["act"],
            grad_w_qkv=pieces[0],
            grad_w_out=pieces[1],
            grad_hidden=one["grads"],
            own_encoded=one["encoded"],
        ),
        dict(
            grad_first=own_kind,
            sums_one=sum_kind,
            sums_two=sum_kind,
            in_sums=in_sum_kind,
            rows=all_kind,
            moved_grads=grads_kind,
            grads=hidden_kind,
            encoded=low_kind,
        ),
        dict(later_grads=grads_kind, down_full=all_kind, pre_low=act_kind, pulled=own_kind, branch_three=all_kind),
        back_stages,
        scatters=((("grad_w_qkv", "grad_w_out", "grad_hidden"), "later_grads"),),
        swapped=(("own_encoded", "encoded"),),
        swapped_after=(("later_grads", "moved_grads"),),
        late=("pre_gelu", "hidden_full", "mlp_input", "act"),
        pace=2,
    )
    branch, pieces, qkv_sums_zero = attention_back(stored_zero, back["rows"])
    g_tokens, grads_zero, small = end(
        branch,
        back["grad_first"],
        (*pieces, back["grads"]),
        (
            (back["sums_one"], back["sums_two"], qkv_sums_zero, back["in_sums"]),
            (one["sums_one"], one["sums_two"], qkv_sums_one, one["in_sums"]),
        ),
    )
    return (
        back["encoded"],
        g_tokens,
        *finish(small, grads_zero, back["moved_grads"], col_width),
    )


def solution(mesh):
    placed = (
        P(("dp", "tensor"), None),
        P("dp", None),
        P(None, "dp", None, "tensor"),
        P(),
        P(None, "tensor", "dp"),
        P(),
        P(None, "dp", "tensor"),
        P(),
        P(None, "tensor", "dp"),
        P(),
        P(),
        P(),
        P(("dp", "tensor"), None),
    )
    return jax.shard_map(
        shards,
        mesh=mesh,
        in_specs=placed,
        out_specs=(
            P(("dp", "tensor"), None),
            P(("dp", "tensor"), None),
            P(None, "dp", None, "tensor"),
            P(),
            P(None, "tensor", "dp"),
            P(),
            P(None, "dp", "tensor"),
            P(),
            P(None, "tensor", "dp"),
            P(),
            P(),
            P(),
        ),
        check_vma=False,
    )
```

```python
import functools
import types

import jax
import jax.numpy as jnp
from jax import lax
from jax.experimental import pallas as pl
from jax.experimental.pallas import tpu as pltpu
from jax.sharding import PartitionSpec as P

DH = 64
EPSILON = 1e-06
MESH = pl.DeviceIdType.MESH
F32 = jnp.float32
BF16 = jnp.bfloat16


def place():
    dp, tensor = lax.axis_index("dp"), lax.axis_index("tensor")
    core = lax.rem(dp, 2)
    z = lax.rem(lax.div(dp, 2), 4)
    x = lax.rem(lax.div(tensor, 4) * 2 + lax.div(dp, 8), 4)
    y = lax.rem(tensor, 4)
    return x, y, z, core


def device(x, y, z, core):
    x, y, z = lax.rem(x, 4), lax.rem(y, 4), lax.rem(z, 4)
    return (lax.rem(x, 2) * 8 + z * 2 + core, lax.div(x, 2) * 4 + y)


def block_of(x, z):
    x, z = lax.rem(x, 4), lax.rem(z, 4)
    return lax.rem(x, 2) * 8 + z * 2 + lax.div(x, 2)


def greet(devices):
    barrier = pltpu.get_barrier_semaphore()
    for other in devices:
        pl.semaphore_signal(barrier, inc=1, device_id=other, device_id_type=MESH)
    pl.semaphore_wait(barrier, len(devices))


class Copies:
    def __init__(self, send, recv):
        self.send, self.recv, self.started = send, recv, []

    def start(self, src, dst, to):
        at = len(self.started)
        copy = pltpu.make_async_remote_copy(
            src_ref=src,
            dst_ref=dst,
            send_sem=self.send.at[at],
            recv_sem=self.recv.at[at],
            device_id=to,
            device_id_type=MESH,
        )
        copy.start()
        self.started.append(copy)
        return copy

    def wait_sends(self):
        for copy in self.started:
            copy.wait_send()


def group_neighbours():
    x, y, z, core = place()
    return (
        device(x, y, z, 1 - core),
        device(x, y + 1, z, core),
        device(x, y + 3, z, core),
    )


GATHER_COPIES = 24
SCATTER_COPIES = 20


class Gather:
    def __init__(self, copies, out, base, count):
        self.x, self.y, self.z, self.core = place()
        self.pair, self.after, self.before = group_neighbours()
        half = count // 2
        self.top, self.low = pl.ds(base, half), pl.ds(base + half, half)
        self.both = pl.ds(base, count)
        self.copies, self.out = copies, out

    def send(self, step, rows, to):
        ref = self.out.at[self.core * 4 + lax.rem(self.y + step, 4), rows]
        return self.copies.start(ref, ref, to)

    def f(self, low=None):
        if low is not None:
            self.out[self.core * 4 + self.y, self.both] = low
        self.top_after = self.send(0, self.top, self.after)
        self.low_before = self.send(0, self.low, self.before)

    def f2(self):
        self.low_after = self.send(0, self.low, self.after)
        self.top_before = self.send(0, self.top, self.before)

    def f3(self):
        self.paired = [self.send(0, self.both, self.pair)]

    def g(self):
        self.top_after.wait_recv()
        self.far_top = self.send(3, self.top, self.after)
        self.low_before.wait_recv()
        self.far_low = self.send(1, self.low, self.before)

    def h(self):
        self.low_after.wait_recv()
        self.paired.append(self.send(3, self.both, self.pair))
        self.top_before.wait_recv()
        self.paired.append(self.send(1, self.both, self.pair))

    def i(self):
        self.far_top.wait_recv()
        self.paired.append(self.send(2, self.top, self.pair))
        self.far_low.wait_recv()
        self.paired.append(self.send(2, self.low, self.pair))

    def j(self):
        for copy in self.paired:
            copy.wait_recv()


class Scatter:
    def __init__(self, copies, part, bufs, base, count):
        self.x, self.y, self.z, self.core = place()
        self.pair, self.after, self.before = group_neighbours()
        half = count // 2
        self.top, self.low = pl.ds(base, half), pl.ds(base + half, half)
        self.both = pl.ds(base, count)
        self.copies, self.part = copies, part
        self.from_pair, self.staged, self.far, self.near = bufs
        self.swaps = []

    STEPS = (2, 1, 3, 0)

    def swap(self, slot):
        at = (1 - self.core) * 4 + lax.rem(self.y + self.STEPS[slot], 4)
        src, dst = self.part.at[at, self.both], self.from_pair.at[slot, self.both]
        self.swaps.append(self.copies.start(src, dst, self.pair))

    def chip(self, slot, rows):
        own = self.part[self.core * 4 + lax.rem(self.y + self.STEPS[slot], 4), rows]
        return own.astype(F32) + self.from_pair[slot, rows].astype(F32)

    def pass_on(self, slot, rows, value, dst, to):
        self.staged[slot, rows] = value.astype(BF16)
        return self.copies.start(self.staged.at[slot, rows], dst, to)

    def a0(self):
        self.swap(0)

    def a1(self):
        for slot in (1, 2, 3):
            self.swap(slot)

    def b(self):
        self.swaps[0].wait_recv()
        top, low = self.top, self.low
        self.far_top = self.pass_on(0, top, self.chip(0, top), self.far.at[top], self.after)
        self.far_low = self.pass_on(0, low, self.chip(0, low), self.far.at[low], self.before)

    def c(self):
        top, low = self.top, self.low
        self.swaps[1].wait_recv()
        low_after = self.pass_on(1, low, self.chip(1, low), self.near.at[0, low], self.after)
        self.swaps[2].wait_recv()
        top_before = self.pass_on(2, top, self.chip(2, top), self.near.at[1, top], self.before)
        self.last = [low_after, top_before]

    def d(self):
        top, low = self.top, self.low
        self.far_top.wait_recv()
        value = self.chip(1, top) + self.far[top].astype(F32)
        self.last.append(self.pass_on(1, top, value, self.near.at[0, top], self.after))
        self.far_low.wait_recv()
        value = self.chip(2, low) + self.far[low].astype(F32)
        self.last.append(self.pass_on(2, low, value, self.near.at[1, low], self.before))

    def e(self):
        self.swaps[3].wait_recv()
        own = self.chip(3, self.both)
        for copy in self.last:
            copy.wait_recv()
        return own + self.near[0, self.both].astype(F32) + self.near[1, self.both].astype(F32)


OPENING = (
    "Aa0", "Ab", "Ba0", "Aa1", "Bb", "t", "Ac", "Ad", "t", "Ba1",
    "Bc", "Bd", "t",
)
MIDDLE = (
    "x", "x", "Ae", "Af", "Af2", "x", "x", "Be", "Bf", "Bf3",
    "Af3", "t", "Bf2", "x", "x", "Ag", "t", "Bg", "Bh", "x",
    "x", "t", "Ah", "Ai", "Aj",
)
TURN_ONE = (
    "Aw0", "+Aa0", "Bi", "+Aa1", "Aw1", "t", "+Ab", "Bj", "Bw0", "+Ba0",
)
TURN_TWO = (
    "t", "+Ac", "Bw1", "+Bb", "t", "+Ad", "+Ba1", "+Bc", "+Bd", "t",
)
CLOSING = (
    "Bi", "t", "Bj",
)


def run_chain(scatter, gather, stages, tick, before_work, after_work=None):
    x, y, z, core = place()
    count = stages[0]["part"].shape[1] // 2

    def steps_of(stage):
        return {
            half: (
                Scatter(scatter, stage["part"], stage["bufs"], at * count, count),
                Gather(gather, stage["rows"], at * count, count),
            )
            for at, half in enumerate("AB")
        }

    def run(order, stage, now, then=None):
        for name in order:
            if name == "t":
                tick()
                continue
            if name == "x":
                if stage.get("side"):
                    stage["side"].pop(0)()
                continue
            if name[0] == "+":
                steps, name = then, name[1:]
            else:
                steps = now
            half, name = name[0], name[1:]
            rows = pl.ds("AB".index(half) * count, count)
            own_scatter, own_gather = steps[half]
            if name == "e":
                stage[half] = own_scatter.e()
            elif name == "f":
                own_gather.f(stage["between"](stage[half], rows))
            elif name in ("w0", "w1"):
                blocks = pl.ds((core if name == "w1" else 1 - core) * 4, 4)
                stage["work"](blocks, rows)
            elif hasattr(own_scatter, name):
                getattr(own_scatter, name)()
            else:
                getattr(own_gather, name)()

    now = steps_of(stages[0])
    run(OPENING, stages[0], now)
    for at, stage in enumerate(stages):
        run(MIDDLE, stage, now)
        if at == len(stages) - 1:
            run(CLOSING, stage, now)
            break
        if at == 0:
            before_work()
        then = steps_of(stages[at + 1])
        run(TURN_ONE, stage, now, then)
        run(TURN_TWO, stage, now, then)
        if after_work is not None:
            after_work(at)
        now = then


def gather_all(gather, rows_out, tick, arrivals):
    count = rows_out.shape[1] // 2
    halves = [Gather(gather, rows_out, at * count, count) for at in (0, 1)]
    for half, arrive in zip(halves, arrivals):
        arrive()
        for name in ("f", "f2", "f3"):
            getattr(half, name)()
    for name in ("g", "h", "i", "j"):
        tick()
        for half in halves:
            getattr(half, name)()
        tick()


def scatter_all(scatter, part, bufs, tick):
    count = part.shape[1] // 2
    first, second = [Scatter(scatter, part, bufs, at * count, count) for at in (0, 1)]
    for name in OPENING:
        if name == "t":
            tick()
        else:
            getattr(first if name[0] == "A" else second, name[1:])()
    return first.e(), second.e()


def scatter_scratch(rows, width):
    return [
        pltpu.VMEM((4, rows, width), BF16),
        pltpu.VMEM((3, rows, width), BF16),
        pltpu.VMEM((rows, width), BF16),
        pltpu.VMEM((2, rows, width), BF16),
    ]


def sems(count):
    return [pltpu.SemaphoreType.DMA((count,)), pltpu.SemaphoreType.DMA((count,))]


def plane_ring(axis):
    x, y, z, core = place()
    if axis == "x":
        return device(x + 1, y, z, core), device(x + 3, y, z, core)
    return device(x, y, z + 1, core), device(x, y, z + 3, core)


def plane_at(first, u, v):
    return block_of(u, v) if first == "x" else block_of(v, u)


PLANE_GATHER_COPIES = 36
PLANE_SCATTER_COPIES = 36


def gather_plane(copies, out):
    x, y, z, core = place()
    quarter = out.shape[1] // 4
    paths = []
    for first, base in (("x", 0), ("z", 2 * quarter)):
        v, u = (x, z) if first == "x" else (z, x)
        other = "z" if first == "x" else "x"
        paths.append(
            types.SimpleNamespace(
                first=first,
                v=v,
                u=u,
                ring=plane_ring(first),
                cross=plane_ring(other),
                halves=(pl.ds(base, quarter), pl.ds(base + quarter, quarter)),
                whole=pl.ds(base, 2 * quarter),
            )
        )

    def send(path, dv, du, rows, to):
        at = plane_at(path.first, path.v + dv, path.u + du)
        return copies.start(out.at[at, rows], out.at[at, rows], to)

    for path in paths:
        after, before = path.ring
        top, low = path.halves
        path.ta = send(path, 0, 0, top, after)
        path.lb = send(path, 0, 0, low, before)
        path.la = send(path, 0, 0, low, after)
        path.tb = send(path, 0, 0, top, before)
        path.c = {0: [send(path, 0, 0, path.whole, to) for to in path.cross]}
    yield
    for path in paths:
        path.ta.wait_recv()
        path.ft = send(path, 3, 0, path.halves[0], path.ring[0])
        path.lb.wait_recv()
        path.fl = send(path, 1, 0, path.halves[1], path.ring[1])
    yield
    for path in paths:
        path.la.wait_recv()
        path.c[3] = [send(path, 3, 0, path.whole, to) for to in path.cross]
        path.tb.wait_recv()
        path.c[1] = [send(path, 1, 0, path.whole, to) for to in path.cross]
    last = []
    for path in paths:
        path.c[0][0].wait_recv()
        last.append(send(path, 0, 3, path.whole, path.cross[0]))
    yield
    for path in paths:
        path.ft.wait_recv()
        path.fl.wait_recv()
        path.c[2] = [send(path, 2, 0, path.whole, to) for to in path.cross]
    yield
    for path in paths:
        path.c[3][0].wait_recv()
        last.append(send(path, 3, 3, path.whole, path.cross[0]))
        path.c[1][1].wait_recv()
        last.append(send(path, 1, 1, path.whole, path.cross[1]))
    yield
    for path in paths:
        path.c[2][1].wait_recv()
        last.append(send(path, 2, 1, path.whole, path.cross[1]))
    yield
    for path in paths:
        for copy in (path.c[0][1], path.c[3][1], path.c[1][0], path.c[2][0]):
            copy.wait_recv()
    for copy in last:
        copy.wait_recv()


def scatter_plane_scratch(rows, width):
    half = rows // 2
    return [
        pltpu.VMEM((2, 4, half, width), BF16),
        pltpu.VMEM((2, 2, 4, half, width), BF16),
        pltpu.VMEM((2, 4, half, width), BF16),
        pltpu.VMEM((2, 4, half, width), BF16),
        pltpu.VMEM((2, half, width), BF16),
        pltpu.VMEM((2, 2, half, width), BF16),
        pltpu.VMEM((2, 2, half // 2, width), BF16),
    ]


def scatter_plane(copies, part, out, far, near, passed, summed, far2, near2, passed2):
    x, y, z, core = place()
    half = part.shape[1] // 2
    quarter = half // 2
    paths = []
    for at, (first, base) in enumerate((("x", 0), ("z", half))):
        u, v = (x, z) if first == "x" else (z, x)
        other = "z" if first == "x" else "x"
        paths.append(
            types.SimpleNamespace(
                at=at,
                first=first,
                u=u,
                v=v,
                ring=plane_ring(first),
                cross=plane_ring(other),
                rows=pl.ds(base, half),
                base=base,
            )
        )

    def source(path, du, v):
        return (plane_at(path.first, path.u + du, v), path.rows)

    for path in paths:
        at, (after, before) = path.at, path.ring
        path.far = [
            copies.start(
                part.at[source(path, 2, v)], far.at[at, v], after if v < 2 else before
            )
            for v in range(4)
        ]
    for path in paths:
        at, (after, before) = path.at, path.ring
        path.near = [
            copies.start(part.at[source(path, 1, v)], near.at[at, 0, v], after) for v in (2, 3)
        ] + [
            copies.start(part.at[source(path, 3, v)], near.at[at, 1, v], before) for v in (0, 1)
        ]
    yield
    for path in paths:
        at, (after, before) = path.at, path.ring
        for v in (0, 2, 1, 3):
            path.far[v].wait_recv()
            du, slot, to = (1, 0, after) if v < 2 else (3, 1, before)
            own = part[source(path, du, v)].astype(F32)
            passed[at, v] = (own + far[at, v].astype(F32)).astype(BF16)
            path.near.append(copies.start(passed.at[at, v], near.at[at, slot, v], to))
    yield
    for path in paths:
        at = path.at
        for copy in path.near:
            copy.wait_recv()
        for v in range(4):
            own = part[source(path, 0, v)].astype(F32)
            summed[at, v] = (
                own + near[at, 0, v].astype(F32) + near[at, 1, v].astype(F32)
            ).astype(BF16)
        v, (after, before) = path.v, path.cross
        top, low = pl.ds(0, quarter), pl.ds(quarter, quarter)
        v1, v2, v3 = lax.rem(v + 1, 4), lax.rem(v + 2, 4), lax.rem(v + 3, 4)
        path.ft = copies.start(summed.at[at, v2, top], far2.at[at, top], after)
        path.fl = copies.start(summed.at[at, v2, low], far2.at[at, low], before)
        path.last = [
            copies.start(summed.at[at, v1, low], near2.at[at, 0, low], after),
            copies.start(summed.at[at, v3, top], near2.at[at, 1, top], before),
        ]
    yield
    for path in paths:
        at, v, (after, before) = path.at, path.v, path.cross
        top, low = pl.ds(0, quarter), pl.ds(quarter, quarter)
        v1, v3 = lax.rem(v + 1, 4), lax.rem(v + 3, 4)
        path.ft.wait_recv()
        passed2[at, 0] = (summed[at, v1, top].astype(F32) + far2[at, top].astype(F32)).astype(BF16)
        path.last.append(copies.start(passed2.at[at, 0], near2.at[at, 0, top], after))
        path.fl.wait_recv()
        passed2[at, 1] = (summed[at, v3, low].astype(F32) + far2[at, low].astype(F32)).astype(BF16)
        path.last.append(copies.start(passed2.at[at, 1], near2.at[at, 1, low], before))
    yield
    for path in paths:
        at, v = path.at, path.v
        for copy in path.last:
            copy.wait_recv()
        total = summed[at, v].astype(F32) + near2[at, 0].astype(F32) + near2[at, 1].astype(F32)
        out[path.rows] = total.astype(out.dtype)


def params(number):
    return pltpu.CompilerParams(
        collective_id=number, has_side_effects=True, vmem_limit_bytes=56 * 2**20
    )


VMEM = pl.BlockSpec(memory_space=pltpu.VMEM)
HBM = pl.BlockSpec(memory_space=pl.ANY)


def neighbours():
    return [*group_neighbours(), *plane_ring("x"), *plane_ring("z")]


def drain(steps):
    for _ in steps:
        pass


def swap_partner():
    x, y, z, core = place()
    upper = lax.div(x, 2)
    return core != upper, device(core * 2 + lax.rem(x, 2), y, z, upper)


def greet_with_partner(others):
    moves, partner = swap_partner()
    barrier = pltpu.get_barrier_semaphore()
    for other in others:
        pl.semaphore_signal(barrier, inc=1, device_id=other, device_id_type=MESH)

    @pl.when(moves)
    def _():
        pl.semaphore_signal(barrier, inc=1, device_id=partner, device_id_type=MESH)

    pl.semaphore_wait(barrier, len(others) + moves.astype(jnp.int32))


def partner_copy(src, dst, send, recv):
    return pltpu.make_async_remote_copy(
        src_ref=src,
        dst_ref=dst,
        send_sem=send,
        recv_sem=recv,
        device_id=swap_partner()[1],
        device_id_type=MESH,
    )


class Swaps:
    def __init__(self, send, recv):
        self.send, self.recv, self.moves = send, recv, []

    def copy(self, src, dst, own_dst=None):
        at = len(self.moves)
        copy = partner_copy(src, dst, self.send.at[at], self.recv.at[at])
        self.moves.append(copy)
        moves, _ = swap_partner()

        @pl.when(moves)
        def _():
            copy.start()

        @pl.when(jnp.logical_not(moves))
        def _():
            target = dst if own_dst is None else own_dst
            target[...] = src[...]

        return copy

    def arrive(self, copy):
        @pl.when(swap_partner()[0])
        def _():
            copy.wait_recv()

    def finish(self, *arrived):
        @pl.when(swap_partner()[0])
        def _():
            for copy in self.moves:
                copy.wait_send()
                if not any(copy is other for other in arrived):
                    copy.wait_recv()


def start_kernel(
    tokens, attention, hidden, lengths,
    rows_out, own_out, weights_out, attention_out, hidden_first, hidden_later, lengths_out,
    ssend, srecv, send, recv, wsend, wrecv,
):
    x, y, z, core = place()
    greet_with_partner(neighbours())
    plane, group, swaps = Copies(wsend, wrecv), Copies(send, recv), Swaps(ssend, srecv)
    there = block_of(core * 2 + lax.rem(x, 2), z)
    own = weights_out.at[block_of(x, z)]
    weights_move = swaps.copy(attention.at[0], weights_out.at[there], own)
    count = tokens.shape[0] // 2
    rows_moves = []
    for half in (pl.ds(0, count), pl.ds(count, count)):
        own = rows_out.at[core * 4 + y, half]
        target = rows_out.at[lax.div(x, 2) * 4 + y, half]
        rows_moves.append(swaps.copy(tokens.at[half], target, own))
    swaps.copy(lengths, lengths_out)
    swaps.arrive(weights_move)
    steps = gather_plane(plane, weights_out)
    next(steps)
    arrivals = [functools.partial(swaps.arrive, move) for move in rows_moves]
    ticks = []

    def tick():
        ticks.append(None)
        next(steps, None)
        if len(ticks) == 3:
            swaps.copy(hidden.at[0], hidden_first)
            swaps.copy(attention.at[1], attention_out)
            swaps.copy(hidden.at[1], hidden_later)

    gather_all(group, rows_out, tick, arrivals)
    own_out[...] = rows_out[core * 4 + y]
    drain(steps)
    swaps.finish(weights_move, *rows_moves)
    group.wait_sends()
    plane.wait_sends()


def start(tokens, attention, hidden, lengths):
    rows, width = tokens.shape
    _, held, columns = attention.shape
    shape = jax.ShapeDtypeStruct
    return pl.pallas_call(
        start_kernel,
        out_shape=(
            shape((8, rows, width), BF16),
            shape((rows, width), BF16),
            shape((16, held, columns), BF16),
            shape((held, columns), BF16),
            shape(hidden.shape[1:], BF16),
            shape(hidden.shape[1:], BF16),
            shape(lengths.shape, lengths.dtype),
        ),
        in_specs=[VMEM] * 4,
        out_specs=(VMEM,) * 7,
        scratch_shapes=sems(7) + sems(GATHER_COPIES) + sems(PLANE_GATHER_COPIES),
        compiler_params=params(0),
        name="start",
    )(tokens, attention, hidden, lengths)


def normed_parts(stream):
    row_mean = jnp.mean(stream, axis=-1, keepdims=True)
    centered = stream - row_mean
    row_var = jnp.mean(centered * centered, axis=-1, keepdims=True)
    scale = lax.rsqrt(row_var + EPSILON)
    return centered * scale, scale


def norm_pull(unit, scale, gain, grad, sums):
    scaled = grad * gain
    inner = jnp.mean(scaled * unit, axis=-1, keepdims=True)
    pulled = scale * (scaled - jnp.mean(scaled, axis=-1, keepdims=True) - unit * inner)
    low = pulled.astype(BF16)
    sums[0:1] += jnp.sum(grad * unit, axis=0, keepdims=True)
    sums[1:2] += jnp.sum(grad, axis=0, keepdims=True)
    sums[2:3] += jnp.sum(low.astype(F32), axis=0, keepdims=True)
    return pulled, low


INV_SQRT2 = 0.7071067811865476
INV_SQRT_2PI = 0.3989422804014327
CONTRACT_LAST = (((1,), (1,)), ((), ()))
CONTRACT_FIRST = (((0,), (0,)), ((), ()))


def normal_cdf(values):
    return 0.5 * (1.0 + lax.erf(values * INV_SQRT2))


def flatten(block):
    return block.reshape(block.shape[0] * block.shape[1], block.shape[2])


def hidden_forward(ref, hidden_width):
    def work(blocks, rows):
        full_in = flatten(ref.hidden_full[:, :, :hidden_width])
        full_down = flatten(ref.hidden_full[:, :, hidden_width:])
        values = flatten(ref.mlp_input[blocks, rows])
        pre_gelu = jnp.dot(values, full_in, preferred_element_type=F32) + ref.bias_in[ref.layer : ref.layer + 1]
        act = (pre_gelu * normal_cdf(pre_gelu)).astype(BF16)
        branch = lax.dot_general(act, full_down, CONTRACT_LAST, preferred_element_type=F32)
        shape = ref.mlp_input[blocks, rows].shape
        ref.pre_gelu[blocks, rows] = pre_gelu.reshape(*shape[:2], -1)
        ref.act[blocks, rows] = act.reshape(*shape[:2], -1)
        ref.branch_two[blocks, rows] = branch.astype(BF16).reshape(shape)

    return work


def hidden_backward(ref, hidden_width):
    def work(blocks, rows):
        full_in = flatten(ref.hidden_full[:, :, :hidden_width])
        full_down = flatten(ref.hidden_full[:, :, hidden_width:])
        values = flatten(ref.down_full[blocks, rows])
        grad_act = jnp.dot(values, full_down, preferred_element_type=F32)
        pre_gelu = flatten(ref.pre_gelu[blocks, rows])
        slope = normal_cdf(pre_gelu) + pre_gelu * (
            jnp.exp(pre_gelu * pre_gelu * -0.5) * INV_SQRT_2PI
        )
        low = (slope * grad_act).astype(BF16)
        branch = lax.dot_general(low, full_in, CONTRACT_LAST, preferred_element_type=F32)
        shape = ref.down_full[blocks, rows].shape
        ref.pre_low[blocks, rows] = low.reshape(*shape[:2], -1)
        ref.in_sums[0:1] += jnp.sum(low.astype(F32), axis=0, keepdims=True)
        ref.branch_three[blocks, rows] = branch.astype(BF16).reshape(shape)

    return work


def hidden_grads(ref, out):
    pieces = []
    into = out
    hidden_width = into.shape[2] // 2

    def piece(quarter, left, right, base):
        def work():
            values = flatten(left[:, :, quarter * 256 : (quarter + 1) * 256])
            grad = lax.dot_general(
                values, flatten(right[...]), CONTRACT_FIRST, preferred_element_type=F32
            )
            into[quarter * 4 : (quarter + 1) * 4, :, base : base + hidden_width] = grad.astype(
                BF16
            ).reshape(4, 64, hidden_width)

        return work

    for quarter in range(4):
        pieces.append(piece(quarter, ref.down_full, ref.act, hidden_width))
    for quarter in range(4):
        pieces.append(piece(quarter, ref.mlp_input, ref.pre_low, 0))
    return dict(side=pieces)


def param_rows(ref, at, which):
    rows = (2 * which + at, 4 + 2 * at + which, 8 + 2 * at + which)
    return [ref.params[row : row + 1] for row in rows]


def forward_norm(ref, held, at, which, stream_out, normed_out):
    def between(total, rows):
        bias, gain, shift = param_rows(ref, at, which)
        stream = held[rows].astype(F32) + total + bias
        stream_out[rows] = stream
        unit, _ = normed_parts(stream)
        normed = unit * gain + shift
        normed_out[rows] = normed
        return normed.astype(BF16)

    return between


def turn_norm(ref, held, at, which, pulled_out, sums):
    def between(total, rows):
        bias, gain, shift = param_rows(ref, at, which)
        unit, scale = normed_parts(held[rows] + total + bias)
        ref.encoded[rows] = (unit * gain + shift).astype(BF16)
        grad = ref.cotangent[rows].astype(F32)
        pulled, low = norm_pull(unit, scale, gain, grad, sums)
        pulled_out[rows] = pulled
        return low

    return between


def backward_norm(ref, held, at, which, stream, pulled_out, sums):
    def between(total, rows):
        unit, scale = normed_parts(stream[rows])
        grad = held[rows] + total
        pulled, low = norm_pull(unit, scale, param_rows(ref, at, which)[1], grad, sums)
        pulled_out[rows] = pulled
        return low

    return between


def zeroed(ref):
    if not hasattr(ref, "in_sums"):
        return ()
    return (ref.sums_one, ref.sums_two, ref.in_sums)


def chain_call(
    number, name, inputs, outputs, scratch, stages_of,
    gathers=(), scatters=(), swapped=(), late=(), early=(), pace=1, swapped_after=(),
):
    rows, width = 128, 1024
    names_in, names_out, names_scratch = list(inputs), list(outputs), list(scratch)
    stage_count = stages_of({}, True)
    shapes = []
    for key in names_out:
        shape, kind = outputs[key]
        shapes.append(jax.ShapeDtypeStruct(shape, kind))
    scratch_shapes = [pltpu.VMEM(shape, kind) for shape, kind in scratch.values()]
    for _ in range(stage_count):
        scratch_shapes += scatter_scratch(rows, width)
    scratch_shapes += sems(SCATTER_COPIES * stage_count) + sems(GATHER_COPIES * stage_count)
    pieces = [key for sources, _ in scatters for key in sources]
    stored = [key for keys, _ in early for key in keys]
    scratch_shapes += [pltpu.VMEM(inputs[key].shape, inputs[key].dtype) for key in late]
    scratch_shapes += [pltpu.VMEM(*outputs[key]) for key in stored]
    scratch_shapes += [pltpu.SemaphoreType.DMA((len(late) + len(stored) + len(pieces) + 1,))]
    for _ in gathers:
        scratch_shapes += sems(PLANE_GATHER_COPIES)
    for sources, out in scatters:
        kept, columns = {**outputs, **scratch}[out][0]
        scratch_shapes += [pltpu.VMEM((16, kept, columns), BF16)]
        scratch_shapes += sems(PLANE_SCATTER_COPIES) + scatter_plane_scratch(kept, columns)
    if swapped:
        scratch_shapes += sems(len(swapped) + len(swapped_after))

    def kernel(*refs):
        refs = list(refs)
        take = lambda count: [refs.pop(0) for _ in range(count)]
        ref = types.SimpleNamespace()
        held = vars(ref)
        for names in (names_in, names_out, names_scratch):
            held.update(zip(names, take(len(names))))
        bufs = [take(4) for _ in range(stage_count)]
        scatter, gather = Copies(*take(2)), Copies(*take(2))
        far_refs = {key: held[key] for key in (*late, *stored)}
        held.update(zip((*late, *stored), take(len(late) + len(stored))))
        (local,) = take(1)
        fetches, stores, count = [], [], []

        def local_copy(src, dst, kept):
            copy = pltpu.make_async_copy(src, dst, local.at[len(count)])
            copy.start()
            count.append(None)
            kept.append(copy)
            return copy

        for key in late:
            local_copy(far_refs[key], held[key], fetches)

        def after_work(at):
            for keys, stage in early:
                if stage == at:
                    for key in keys:
                        local_copy(held[key], far_refs[key], stores)

        x, y, z, core = place()
        others = neighbours() if gathers or scatters else group_neighbours()
        planes, queue = [], []
        for source, out in gathers:
            plane = Copies(*take(2))
            planes.append(plane)
            queue.append((gather_plane(plane, held[out]), (), True))
        for sources, out in scatters:
            (assembled,) = take(1)
            plane = Copies(*take(2))
            planes.append(plane)
            at, parts = 0, []
            for source in sources:
                columns = pl.ds(at, held[source].shape[-1])
                local_copy(held[source], assembled.at[:, :, columns], parts)
                at += held[source].shape[-1]
            steps = scatter_plane(plane, assembled, held[out], *take(7))
            queue.append((steps, parts, sources))
        stages = stages_of(ref, False)
        for stage, own in zip(stages, bufs):
            stage["bufs"] = own
        if swapped:
            swaps = Swaps(*take(2))
            greet_with_partner(others)
        else:
            greet(others)
        for sums in zeroed(ref):
            sums[...] = jnp.zeros_like(sums)
        for source, out in gathers:
            held[out][block_of(x, z)] = held[source][...]
        started, ended, ticks = [], [], [None] * (pace - 1)

        def tick():
            if not started:
                started.append(True)
                for _, parts, _ in queue:
                    for part in parts:
                        part.wait()
                for source, out in swapped:
                    swaps.copy(held[source], held[out])
            ticks.append(None)
            if len(ticks) % pace:
                return
            advance_planes()

        def advance_planes():
            while queue:
                try:
                    next(queue[0][0])
                    return
                except StopIteration:
                    queue.pop(0)
            if not ended:
                ended.append(True)
                for source, out in swapped_after:
                    swaps.copy(held[source], held[out])

        def before_work():
            if gathers and len(queue) == len(gathers) + len(scatters):
                drain(queue.pop(0)[0])
            for copy in fetches:
                copy.wait()
            fetches.clear()

        run_chain(scatter, gather, stages, tick, before_work, after_work)
        for steps, *_ in queue:
            drain(steps)
        queue.clear()
        advance_planes()
        for copies in (scatter, gather, *planes):
            copies.wait_sends()
        for copy in stores:
            copy.wait()
        if swapped:
            swaps.finish()

    results = pl.pallas_call(
        kernel,
        out_shape=tuple(shapes),
        in_specs=[HBM if key in (*late, *pieces) else VMEM for key in names_in],
        out_specs=tuple(HBM if key in stored else VMEM for key in names_out),
        scratch_shapes=scratch_shapes,
        compiler_params=params(number),
        name=name,
    )(*inputs.values())
    return dict(zip(names_out, results))


def sum_small(copies, small, out, got_x, got_z):
    x, y, z, core = place()
    own = core * 4 + y
    along_x = [device(x + step, y, z, core) for step in (1, 2, 3)]
    along_z = [device(x, y, z + step, core) for step in (1, 2, 3)]
    along_y = [device(x, y + step, z, core) for step in (1, 2, 3)]
    first = [copies.start(small, got_x.at[at], to) for at, to in enumerate(along_x)]
    yield
    for copy in first:
        copy.wait_recv()
    got_z[3] = small[...] + got_x[0] + got_x[1] + got_x[2]
    second = [copies.start(got_z.at[3], got_z.at[at], to) for at, to in enumerate(along_z)]
    yield
    for copy in second:
        copy.wait_recv()
    out[own] = got_z[3] + got_z[0] + got_z[1] + got_z[2]
    third = [copies.start(out.at[own], out.at[own], to) for to in along_y]
    yield
    for copy in third:
        copy.wait_recv()
    held = out.at[pl.ds(core * 4, 4)]
    copies.start(held, held, device(x, y, z, 1 - core)).wait_recv()


def end_kernel(*refs):
    refs = list(refs)
    take = lambda count: [refs.pop(0) for _ in range(count)]
    part, held, *pieces = take(5)
    layer_sums = [take(4), take(4)]
    rows_out, grads_out, small_out = take(3)
    grads, local = take(2)
    bufs, plane_bufs = take(4), take(7)
    rows_stage, grads_stage, small, got_x, got_z = take(5)
    swaps, group, plane, tiny = Swaps(*take(2)), Copies(*take(2)), Copies(*take(2)), Copies(*take(2))
    x, y, z, core = place()
    at, fetches = 0, []
    for number, piece in enumerate(pieces):
        columns = pl.ds(at, piece.shape[2])
        fetches.append(pltpu.make_async_copy(piece, grads.at[:, :, columns], local.at[number]))
        fetches[-1].start()
        at += piece.shape[2]
    small[...] = jnp.zeros_like(small)
    for base, (sums_one, sums_two, qkv_sums, in_sums) in zip((0, 8), layer_sums):
        third, hidden_width = qkv_sums.shape[1] // 3, in_sums.shape[1]
        small[base : base + 3] = sums_one[0:3]
        small[base + 3 : base + 6] = sums_two[0:3]
        small[base + 6 : base + 7, :third] = qkv_sums[0:1, :third]
        small[base + 6 : base + 7, third : 2 * third] = qkv_sums[0:1, 2 * third :]
        small[base + 6 : base + 7, 2 * third : 2 * third + hidden_width] = in_sums[0:1]
    greet_with_partner(
        neighbours()
        + [device(x + 2, y, z, core), device(x, y + 2, z, core), device(x, y, z + 2, core)]
    )
    tiny_steps = sum_small(tiny, small, small_out, got_x, got_z)
    plane_steps = scatter_plane(plane, grads, grads_stage, *plane_bufs)
    ticks = []

    def tick():
        ticks.append(None)
        if len(ticks) == 1:
            next(tiny_steps)
            for copy in fetches:
                copy.wait()
            next(plane_steps)
        elif len(ticks) == 2:
            next(tiny_steps)
        elif len(ticks) == 3:
            next(plane_steps)

    totals = scatter_all(group, part, bufs, tick)
    count = rows_stage.shape[0] // 2
    for at in (0, 1):
        rows = pl.ds(at * count, count)
        rows_stage[rows] = (held[rows] + totals[at]).astype(BF16)
    swaps.copy(rows_stage, rows_out)
    next(plane_steps)
    next(tiny_steps)
    next(plane_steps)
    drain(tiny_steps)
    drain(plane_steps)
    swaps.copy(grads_stage, grads_out)
    swaps.finish()
    group.wait_sends()
    plane.wait_sends()
    tiny.wait_sends()


def end(part, held, pieces, layer_sums):
    rows, width = held.shape
    kept, columns = pieces[0].shape[1], sum(piece.shape[2] for piece in pieces)
    shape = jax.ShapeDtypeStruct
    return pl.pallas_call(
        end_kernel,
        out_shape=(
            shape((rows, width), BF16),
            shape((kept, columns), BF16),
            shape((8, 16, width), F32),
        ),
        in_specs=[VMEM] * 2 + [HBM] * 3 + [VMEM] * 8,
        out_specs=(VMEM,) * 3,
        scratch_shapes=[pltpu.VMEM((16, kept, columns), BF16), pltpu.SemaphoreType.DMA((3,))]
        + scatter_scratch(rows, width)
        + scatter_plane_scratch(kept, columns)
        + [
            pltpu.VMEM((rows, width), BF16),
            pltpu.VMEM((kept, columns), BF16),
            pltpu.VMEM((16, width), F32),
            pltpu.VMEM((3, 16, width), F32),
            pltpu.VMEM((4, 16, width), F32),
        ]
        + sems(2)
        + sems(SCATTER_COPIES)
        + sems(PLANE_SCATTER_COPIES)
        + sems(10),
        compiler_params=params(1),
        name="end",
    )(part, held, *pieces, *layer_sums[0], *layer_sums[1])


def finish_kernel(
    small, zero, one,
    g_qkv, g_b_qv, g_out, g_b_out, g_in, g_b_in, g_down, g_b_down, g_gain, g_shift,
):
    third, hidden_width = g_out.shape[1], g_in.shape[2]
    cut = 4 * third
    for at, grads in enumerate((zero, one)):
        for which in range(3):
            columns = slice(which * third, (which + 1) * third)
            g_qkv[at, :, which] = grads[:, columns].astype(F32)
        g_out[at] = grads[:, 3 * third : cut].astype(F32).T
        g_in[at] = grads[:, cut : cut + hidden_width].astype(F32)
        g_down[at] = grads[:, cut + hidden_width :].astype(F32).T
        rows = jnp.sum(small[:, at * 8 : at * 8 + 8], axis=0)
        g_gain[at, 0:1], g_shift[at, 0:1], g_b_out[at : at + 1] = rows[0:1], rows[1:2], rows[2:3]
        g_gain[at, 1:2], g_shift[at, 1:2], g_b_down[at : at + 1] = rows[3:4], rows[4:5], rows[5:6]
        for block in range(8):
            row = small[block, at * 8 + 6 : at * 8 + 7]
            columns = slice(block * third, (block + 1) * third)
            g_b_qv[at, 0:1, columns] = row[:, :third]
            g_b_qv[at, 1:2, columns] = row[:, third : 2 * third]
            columns = slice(block * hidden_width, (block + 1) * hidden_width)
            g_b_in[at : at + 1, columns] = row[:, 2 * third : 2 * third + hidden_width]


def finish(small, zero, one, third):
    kept, hidden_width = zero.shape[0], (zero.shape[1] - 4 * third) // 2
    width = small.shape[2]
    shapes = (
        (2, kept, 3, third),
        (2, 2, width),
        (2, third, kept),
        (2, width),
        (2, kept, hidden_width),
        (2, 8 * hidden_width),
        (2, hidden_width, kept),
        (2, width),
        (2, 2, width),
        (2, 2, width),
    )
    return pl.pallas_call(
        finish_kernel,
        out_shape=tuple(jax.ShapeDtypeStruct(shape, F32) for shape in shapes),
        in_specs=[VMEM] * 3,
        out_specs=(VMEM,) * len(shapes),
        compiler_params=pltpu.CompilerParams(vmem_limit_bytes=48 * 2**20),
        name="finish",
    )(small, zero, one)


HEAD_SCALE = DH ** (-0.5)


def segment_parts(lengths, rows):
    def of(shape, dim):
        positions = lax.broadcasted_iota(jnp.int32, shape, dim)
        end, segments = 0, jnp.zeros(shape, jnp.int32)
        for at in range(4):
            end = end + lengths[0, at]
            segments += (positions >= end).astype(jnp.int32)
        return jnp.where(segments == 4, 4 + positions, segments)

    return of((rows, 1), 0), of((1, rows), 1)


def head_lanes(values, head):
    lanes = lax.broadcasted_iota(jnp.int32, values.shape, 1)
    return jnp.where((lanes >= head * DH) & (lanes < (head + 1) * DH), values, 0)


def pick_heads(parts):
    features = lax.broadcasted_iota(jnp.int32, parts[0].shape, 0)
    return jnp.where(features < DH, parts[0], parts[1])


CHUNK = 1024


def attend_kernel(lengths, rows, weights, bias, qkv_out, context_out, lse_out, branch_out, v_turned, seg_row):
    total, width = rows.shape[0], context_out.shape[1]
    column, row = segment_parts(lengths, total)
    seg_row[...] = jnp.broadcast_to(row, seg_row.shape)

    def chunk(at):
        return pl.ds(pl.multiple_of(at * CHUNK, CHUNK), CHUNK)

    @pl.loop(0, total // CHUNK)
    def _(at):
        r = chunk(at)
        qkv = jnp.dot(rows[r], weights[:, : 3 * width], preferred_element_type=F32)
        qkv_out[r] = (qkv + bias[0:1]).astype(BF16)

    keys = qkv_out[:, width : 2 * width]
    v_turned[...] = qkv_out[:, 2 * width :].astype(F32).T.astype(BF16)

    @pl.loop(0, total // CHUNK)
    def _(at):
        r = chunk(at)
        queries = qkv_out[r, :width].astype(F32) * HEAD_SCALE
        allowed = column == seg_row[0:1, r]
        parts = []
        for head in range(2):
            own = head_lanes(queries, head).astype(BF16)
            scores = lax.dot_general(keys, own, CONTRACT_LAST, preferred_element_type=F32)
            scores = jnp.where(allowed, scores, -1e30)
            peak = jnp.max(scores, axis=0, keepdims=True)
            raised = jnp.exp(scores - peak)
            total_row = jnp.sum(raised, axis=0, keepdims=True)
            probs = (raised * (1.0 / total_row)).astype(BF16)
            parts.append(jnp.dot(v_turned[...], probs, preferred_element_type=F32))
            lse_out[head : head + 1, r] = peak + jnp.log(total_row)
        context = pick_heads(parts).T.astype(BF16)
        context_out[r] = context
        branch = lax.dot_general(
            context, weights[:, 3 * width :], CONTRACT_LAST, preferred_element_type=F32
        )
        branch_out[r] = branch.astype(BF16)


def attend(lengths, rows, weights, bias):
    total, width = rows.shape[0], weights.shape[1] // 4
    shape = jax.ShapeDtypeStruct
    return pl.pallas_call(
        attend_kernel,
        out_shape=(
            shape((total, 3 * width), BF16),
            shape((total, width), BF16),
            shape((8, total), F32),
            shape((total, rows.shape[1]), BF16),
        ),
        in_specs=[pl.BlockSpec(memory_space=pltpu.SMEM)] + [VMEM] * 3,
        out_specs=(VMEM,) * 4,
        scratch_shapes=[pltpu.VMEM((width, total), BF16), pltpu.VMEM((8, total), jnp.int32)],
        compiler_params=pltpu.CompilerParams(vmem_limit_bytes=48 * 2**20),
        name="attend",
    )(lengths, rows, weights, bias)


def attend_back_kernel(
    lengths, grad_rows, rows, weights, qkv, context, lse,
    g_qkv, g_out, branch_out, sums_out,
    grad_context, grad_qkv, k_turned, k_sum, v_sum, seg_row,
):
    total, width = rows.shape[0], context.shape[1]
    column, row = segment_parts(lengths, total)
    seg_row[...] = jnp.broadcast_to(row, seg_row.shape)

    def chunk(at):
        return pl.ds(pl.multiple_of(at * CHUNK, CHUNK), CHUNK)

    @pl.loop(0, total // CHUNK)
    def _(at):
        r = chunk(at)
        grad_context[r] = jnp.dot(
            grad_rows[r], weights[:, 3 * width :], preferred_element_type=F32
        ).astype(BF16)

    keys, values = qkv[:, width : 2 * width], qkv[:, 2 * width :]
    k_turned[...] = keys.astype(F32).T.astype(BF16)
    k_sum[...] = jnp.zeros_like(k_sum)
    v_sum[...] = jnp.zeros_like(v_sum)

    @pl.loop(0, total // CHUNK)
    def _(at):
        r = chunk(at)
        queries = qkv[r, :width].astype(F32) * HEAD_SCALE
        grads = grad_context[r].astype(F32)
        allowed = column == seg_row[0:1, r]
        parts = []
        for head in range(2):
            own = head_lanes(queries, head).astype(BF16)
            own_grads = head_lanes(grads, head).astype(BF16)
            scores = lax.dot_general(keys, own, CONTRACT_LAST, preferred_element_type=F32)
            scores = jnp.where(allowed, scores, -1e30)
            probs = jnp.exp(scores - lse[head : head + 1, r])
            grad_probs = lax.dot_general(
                values, own_grads, CONTRACT_LAST, preferred_element_type=F32
            )
            v_sum[...] += jnp.dot(probs.astype(BF16), own_grads, preferred_element_type=F32)
            inner = jnp.sum(probs * grad_probs, axis=0, keepdims=True)
            grad_scores = (probs * (grad_probs - inner)).astype(BF16)
            k_sum[...] += jnp.dot(grad_scores, own, preferred_element_type=F32)
            parts.append(jnp.dot(k_turned[...], grad_scores, preferred_element_type=F32))
        grad_qkv[r, :width] = (pick_heads(parts).T * HEAD_SCALE).astype(BF16)

    grad_qkv[:, width : 2 * width] = k_sum[...].astype(BF16)
    grad_qkv[:, 2 * width :] = v_sum[...].astype(BF16)
    sums_out[...] = jnp.broadcast_to(
        jnp.sum(grad_qkv[...].astype(F32), axis=0, keepdims=True), sums_out.shape
    )

    @pl.loop(0, total // CHUNK)
    def _(at):
        r = chunk(at)
        branch = lax.dot_general(
            grad_qkv[r], weights[:, : 3 * width], CONTRACT_LAST, preferred_element_type=F32
        )
        branch_out[r] = branch.astype(BF16)

    @pl.loop(0, rows.shape[1] // CHUNK)
    def _(at):
        c = chunk(at)
        turned = lax.dot_general(
            grad_qkv[...], rows[:, c], CONTRACT_FIRST, preferred_element_type=F32
        )
        g_qkv[c] = turned.T.astype(BF16)
        turned = lax.dot_general(
            context[...], grad_rows[:, c], CONTRACT_FIRST, preferred_element_type=F32
        )
        g_out[c] = turned.T.astype(BF16)


def attend_back(lengths, grad_rows, rows, weights, qkv, context, lse):
    total, width = context.shape
    depth = rows.shape[1]
    shape = jax.ShapeDtypeStruct
    return pl.pallas_call(
        attend_back_kernel,
        out_shape=(
            shape((depth, 3 * width), BF16),
            shape((depth, width), BF16),
            shape((total, depth), BF16),
            shape((8, 3 * width), F32),
        ),
        in_specs=[pl.BlockSpec(memory_space=pltpu.SMEM)] + [VMEM] * 6,
        out_specs=(VMEM,) * 4,
        scratch_shapes=[
            pltpu.VMEM((total, width), BF16),
            pltpu.VMEM((total, 3 * width), BF16),
            pltpu.VMEM((width, total), BF16),
            pltpu.VMEM((total, width), F32),
            pltpu.VMEM((total, width), F32),
            pltpu.VMEM((8, total), jnp.int32),
        ],
        compiler_params=pltpu.CompilerParams(vmem_limit_bytes=48 * 2**20),
        name="attend_back",
    )(lengths, grad_rows, rows, weights, qkv, context, lse)


def shards(
    tokens,
    lengths,
    w_qkv,
    b_qv,
    w_out,
    b_out,
    w_in,
    b_in,
    w_down,
    b_down,
    ln_gain,
    ln_bias,
    cotangent,
):
    x, y, z, core = place()
    column = core * 4 + y
    own_rows, width = tokens.shape
    total_rows = own_rows * 8
    layers, kept = w_qkv.shape[:2]
    col_width = w_qkv.shape[3]
    hidden_width = w_in.shape[2]

    attention_shards = jnp.concatenate(
        [w_qkv.reshape(layers, kept, 3 * col_width), w_out.transpose(0, 2, 1)], axis=2
    )
    hidden_shards = jnp.concatenate([w_in, w_down.transpose(0, 2, 1)], axis=2)
    lengths = jnp.pad(lengths, ((0, 7), (0, 128 - lengths.shape[1])))
    rows_zero, hidden, attention_zero, attention_shard, hidden_zero, hidden_one, lengths = start(
        tokens, attention_shards, hidden_shards, lengths
    )

    norm_params = jnp.concatenate(
        [b_out, b_down, ln_gain.reshape(4, width), ln_bias.reshape(4, width)]
    ).astype(F32)
    bias_in = lax.dynamic_slice_in_dim(b_in, column * hidden_width, hidden_width, 1).astype(F32)
    bias_qv = lax.dynamic_slice_in_dim(b_qv, column * col_width, col_width, 2).astype(F32)
    bias_qkv = jnp.concatenate(
        [bias_qv[:, 0], jnp.zeros((layers, col_width), F32), bias_qv[:, 1]], axis=1
    )

    own_kind = ((own_rows, width), F32)
    sum_kind = ((8, width), F32)
    low_kind = ((own_rows, width), BF16)
    all_kind = ((8, own_rows, width), BF16)
    act_kind = ((8, own_rows, hidden_width), BF16)
    gelu_kind = ((8, own_rows, hidden_width), F32)
    in_sum_kind = ((8, hidden_width), F32)
    hidden_kind = ((16, kept, 2 * hidden_width), BF16)
    attention_kind = ((16, kept, 4 * col_width), BF16)
    grads_kind = ((kept, 4 * col_width + 2 * hidden_width), BF16)

    def attention(at, rows, full):
        rows, full = rows.reshape(total_rows, width), full.reshape(width, 4 * col_width)
        qkv, context, lse, branch = attend(lengths, rows, full, bias_qkv[at : at + 1])
        return branch.reshape(all_kind[0]), (rows, full, qkv, context, lse)

    def attention_back(stored, rows):
        grad_rows = rows.reshape(total_rows, width)
        g_qkv, g_out, branch, sums = attend_back(lengths, grad_rows, *stored)
        pieces = (g_qkv.reshape(16, kept, -1), g_out.reshape(16, kept, -1))
        return branch.reshape(all_kind[0]), pieces, sums

    branch, stored_zero = attention(0, rows_zero, attention_zero)

    def zero_stages(ref, counting):
        if counting:
            return 2
        ref.layer = 0
        return [
            dict(
                part=ref.branch,
                rows=ref.mlp_input,
                between=forward_norm(ref, ref.held, 0, 0, ref.first_sum, ref.normed),
                work=hidden_forward(ref, hidden_width),
            ),
            dict(
                part=ref.branch_two,
                rows=ref.rows,
                between=forward_norm(ref, ref.normed, 0, 1, ref.second_sum, ref.hidden),
            ),
        ]

    zero = chain_call(
        2,
        "layer_zero",
        dict(
            branch=branch,
            held=hidden,
            params=norm_params,
            bias_in=bias_in,
            hidden_shard=hidden_zero,
            attention_shard=attention_shard,
            next_cotangent=cotangent,
        ),
        dict(
            first_sum=own_kind,
            second_sum=own_kind,
            hidden=own_kind,
            mlp_input=all_kind,
            pre_gelu=gelu_kind,
            act=act_kind,
            rows=all_kind,
            hidden_full=hidden_kind,
            attention_full=attention_kind,
            moved_cotangent=low_kind,
        ),
        dict(normed=own_kind, branch_two=all_kind),
        zero_stages,
        gathers=(("hidden_shard", "hidden_full"), ("attention_shard", "attention_full")),
        swapped=(("next_cotangent", "moved_cotangent"),),
        early=((("first_sum", "mlp_input", "pre_gelu", "act", "hidden_full"), 0),),
    )

    branch, stored_one = attention(1, zero["rows"], zero["attention_full"])

    def one_stages(ref, counting):
        if counting:
            return 3
        ref.layer = 1
        return [
            dict(
                part=ref.branch,
                rows=ref.mlp_input,
                between=forward_norm(ref, ref.held, 1, 0, ref.first_sum, ref.normed),
                work=hidden_forward(ref, hidden_width),
            ),
            dict(
                part=ref.branch_two,
                rows=ref.down_full,
                between=turn_norm(ref, ref.normed, 1, 1, ref.pulled, ref.sums_two),
                work=hidden_backward(ref, hidden_width),
            ),
            dict(
                part=ref.branch_three,
                rows=ref.rows,
                between=backward_norm(ref, ref.pulled, 1, 0, ref.first_sum, ref.grad_first, ref.sums_one),
                **hidden_grads(ref, ref.grads),
            ),
        ]

    one = chain_call(
        3,
        "layer_one",
        dict(
            branch=branch,
            held=zero["hidden"],
            params=norm_params,
            bias_in=bias_in,
            hidden_shard=hidden_one,
            cotangent=zero["moved_cotangent"],
        ),
        dict(
            encoded=low_kind,
            grad_first=own_kind,
            sums_one=sum_kind,
            sums_two=sum_kind,
            in_sums=in_sum_kind,
            rows=all_kind,
            grads=hidden_kind,
        ),
        dict(
            mlp_input=all_kind,
            act=act_kind,
            down_full=all_kind,
            pre_low=act_kind,
            first_sum=own_kind,
            normed=own_kind,
            pulled=own_kind,
            pre_gelu=gelu_kind,
            hidden_full=hidden_kind,
            branch_two=all_kind,
            branch_three=all_kind,
        ),
        one_stages,
        gathers=(("hidden_shard", "hidden_full"),),
        early=((("encoded",), 1),),
    )
    branch, pieces, qkv_sums_one = attention_back(stored_one, one["rows"])

    def back_stages(ref, counting):
        if counting:
            return 2
        return [
            dict(
                part=ref.branch,
                rows=ref.down_full,
                between=backward_norm(ref, ref.held, 0, 1, ref.second_sum, ref.pulled, ref.sums_two),
                work=hidden_backward(ref, hidden_width),
            ),
            dict(
                part=ref.branch_three,
                rows=ref.rows,
                between=backward_norm(ref, ref.pulled, 0, 0, ref.first_sum, ref.grad_first, ref.sums_one),
                **hidden_grads(ref, ref.grads),
            ),
        ]

    back = chain_call(
        4,
        "layer_back",
        dict(
            branch=branch,
            held=one["grad_first"],
            params=norm_params,
            first_sum=zero["first_sum"],
            second_sum=zero["second_sum"],
            pre_gelu=zero["pre_gelu"],
            hidden_full=zero["hidden_full"],
            mlp_input=zero["mlp_input"],
            act=zero["act"],
            grad_w_qkv=pieces[0],
            grad_w_out=pieces[1],
            grad_hidden=one["grads"],
            own_encoded=one["encoded"],
        ),
        dict(
            grad_first=own_kind,
            sums_one=sum_kind,
            sums_two=sum_kind,
            in_sums=in_sum_kind,
            rows=all_kind,
            moved_grads=grads_kind,
            grads=hidden_kind,
            encoded=low_kind,
        ),
        dict(later_grads=grads_kind, down_full=all_kind, pre_low=act_kind, pulled=own_kind, branch_three=all_kind),
        back_stages,
        scatters=((("grad_w_qkv", "grad_w_out", "grad_hidden"), "later_grads"),),
        swapped=(("own_encoded", "encoded"),),
        swapped_after=(("later_grads", "moved_grads"),),
        late=("pre_gelu", "hidden_full", "mlp_input", "act"),
        pace=2,
    )
    branch, pieces, qkv_sums_zero = attention_back(stored_zero, back["rows"])
    g_tokens, grads_zero, small = end(
        branch,
        back["grad_first"],
        (*pieces, back["grads"]),
        (
            (back["sums_one"], back["sums_two"], qkv_sums_zero, back["in_sums"]),
            (one["sums_one"], one["sums_two"], qkv_sums_one, one["in_sums"]),
        ),
    )
    return (
        back["encoded"],
        g_tokens,
        *finish(small, grads_zero, back["moved_grads"], col_width),
    )


def solution(mesh):
    placed = (
        P(("dp", "tensor"), None),
        P("dp", None),
        P(None, "dp", None, "tensor"),
        P(),
        P(None, "tensor", "dp"),
        P(),
        P(None, "dp", "tensor"),
        P(),
        P(None, "tensor", "dp"),
        P(),
        P(),
        P(),
        P(("dp", "tensor"), None),
    )
    return jax.shard_map(
        shards,
        mesh=mesh,
        in_specs=placed,
        out_specs=(
            P(("dp", "tensor"), None),
            P(("dp", "tensor"), None),
            P(None, "dp", None, "tensor"),
            P(),
            P(None, "tensor", "dp"),
            P(),
            P(None, "dp", "tensor"),
            P(),
            P(None, "tensor", "dp"),
            P(),
            P(),
            P(),
        ),
        check_vma=False,
    )
```

```python
import functools
import types

import jax
import jax.numpy as jnp
from jax import lax
from jax.experimental import pallas as pl
from jax.experimental.pallas import tpu as pltpu
from jax.sharding import PartitionSpec as P

DH = 64
EPSILON = 1e-06
MESH = pl.DeviceIdType.MESH
F32 = jnp.float32
BF16 = jnp.bfloat16


def place():
    dp, tensor = lax.axis_index("dp"), lax.axis_index("tensor")
    core = lax.rem(dp, 2)
    z = lax.rem(lax.div(dp, 2), 4)
    x = lax.rem(lax.div(tensor, 4) * 2 + lax.div(dp, 8), 4)
    y = lax.rem(tensor, 4)
    return x, y, z, core


def device(x, y, z, core):
    x, y, z = lax.rem(x, 4), lax.rem(y, 4), lax.rem(z, 4)
    return (lax.rem(x, 2) * 8 + z * 2 + core, lax.div(x, 2) * 4 + y)


def block_of(x, z):
    x, z = lax.rem(x, 4), lax.rem(z, 4)
    return lax.rem(x, 2) * 8 + z * 2 + lax.div(x, 2)


def greet(devices):
    barrier = pltpu.get_barrier_semaphore()
    for other in devices:
        pl.semaphore_signal(barrier, inc=1, device_id=other, device_id_type=MESH)
    pl.semaphore_wait(barrier, len(devices))


class Copies:
    def __init__(self, send, recv):
        self.send, self.recv, self.started = send, recv, []

    def start(self, src, dst, to):
        at = len(self.started)
        copy = pltpu.make_async_remote_copy(
            src_ref=src,
            dst_ref=dst,
            send_sem=self.send.at[at],
            recv_sem=self.recv.at[at],
            device_id=to,
            device_id_type=MESH,
        )
        copy.start()
        self.started.append(copy)
        return copy

    def wait_sends(self):
        for copy in self.started:
            copy.wait_send()


def group_neighbours():
    x, y, z, core = place()
    return (
        device(x, y, z, 1 - core),
        device(x, y + 1, z, core),
        device(x, y + 3, z, core),
    )


GATHER_COPIES = 24
SCATTER_COPIES = 20


class Gather:
    def __init__(self, copies, out, base, count):
        self.x, self.y, self.z, self.core = place()
        self.pair, self.after, self.before = group_neighbours()
        half = count // 2
        self.top, self.low = pl.ds(base, half), pl.ds(base + half, half)
        self.both = pl.ds(base, count)
        self.copies, self.out = copies, out

    def send(self, step, rows, to):
        ref = self.out.at[self.core * 4 + lax.rem(self.y + step, 4), rows]
        return self.copies.start(ref, ref, to)

    def f(self, low=None):
        if low is not None:
            self.out[self.core * 4 + self.y, self.both] = low
        self.top_after = self.send(0, self.top, self.after)
        self.low_before = self.send(0, self.low, self.before)

    def f2(self):
        self.low_after = self.send(0, self.low, self.after)
        self.top_before = self.send(0, self.top, self.before)

    def f3(self):
        self.paired = [self.send(0, self.both, self.pair)]

    def g(self):
        self.top_after.wait_recv()
        self.far_top = self.send(3, self.top, self.after)
        self.low_before.wait_recv()
        self.far_low = self.send(1, self.low, self.before)

    def h(self):
        self.low_after.wait_recv()
        self.paired.append(self.send(3, self.both, self.pair))
        self.top_before.wait_recv()
        self.paired.append(self.send(1, self.both, self.pair))

    def i(self):
        self.far_top.wait_recv()
        self.paired.append(self.send(2, self.top, self.pair))
        self.far_low.wait_recv()
        self.paired.append(self.send(2, self.low, self.pair))

    def j(self):
        for copy in self.paired:
            copy.wait_recv()


class Scatter:
    def __init__(self, copies, part, bufs, base, count):
        self.x, self.y, self.z, self.core = place()
        self.pair, self.after, self.before = group_neighbours()
        half = count // 2
        self.top, self.low = pl.ds(base, half), pl.ds(base + half, half)
        self.both = pl.ds(base, count)
        self.copies, self.part = copies, part
        self.from_pair, self.staged, self.far, self.near = bufs
        self.swaps = []

    STEPS = (2, 1, 3, 0)

    def swap(self, slot):
        at = (1 - self.core) * 4 + lax.rem(self.y + self.STEPS[slot], 4)
        src, dst = self.part.at[at, self.both], self.from_pair.at[slot, self.both]
        self.swaps.append(self.copies.start(src, dst, self.pair))

    def chip(self, slot, rows):
        own = self.part[self.core * 4 + lax.rem(self.y + self.STEPS[slot], 4), rows]
        return own.astype(F32) + self.from_pair[slot, rows].astype(F32)

    def pass_on(self, slot, rows, value, dst, to):
        self.staged[slot, rows] = value.astype(BF16)
        return self.copies.start(self.staged.at[slot, rows], dst, to)

    def a0(self):
        self.swap(0)

    def a1(self):
        for slot in (1, 2, 3):
            self.swap(slot)

    def b(self):
        self.swaps[0].wait_recv()
        top, low = self.top, self.low
        self.far_top = self.pass_on(0, top, self.chip(0, top), self.far.at[top], self.after)
        self.far_low = self.pass_on(0, low, self.chip(0, low), self.far.at[low], self.before)

    def c(self):
        top, low = self.top, self.low
        self.swaps[1].wait_recv()
        low_after = self.pass_on(1, low, self.chip(1, low), self.near.at[0, low], self.after)
        self.swaps[2].wait_recv()
        top_before = self.pass_on(2, top, self.chip(2, top), self.near.at[1, top], self.before)
        self.last = [low_after, top_before]

    def d(self):
        top, low = self.top, self.low
        self.far_top.wait_recv()
        value = self.chip(1, top) + self.far[top].astype(F32)
        self.last.append(self.pass_on(1, top, value, self.near.at[0, top], self.after))
        self.far_low.wait_recv()
        value = self.chip(2, low) + self.far[low].astype(F32)
        self.last.append(self.pass_on(2, low, value, self.near.at[1, low], self.before))

    def e(self):
        self.swaps[3].wait_recv()
        own = self.chip(3, self.both)
        for copy in self.last:
            copy.wait_recv()
        return own + self.near[0, self.both].astype(F32) + self.near[1, self.both].astype(F32)


OPENING = (
    "Aa0", "Ab", "Ba0", "Aa1", "Bb", "t", "Ac", "Ad", "t", "Ba1",
    "Bc", "Bd", "t",
)
MIDDLE = (
    "x", "x", "Ae", "Af", "Af2", "x", "x", "Be", "Bf", "Bf3",
    "Af3", "t", "Bf2", "x", "x", "Ag", "t", "Bg", "Bh", "x",
    "x", "t", "Ah", "Ai", "Aj",
)
TURN_ONE = (
    "Aw0", "+Aa0", "Bi", "+Aa1", "Aw1", "t", "+Ab", "Bj", "Bw0", "+Ba0",
)
TURN_TWO = (
    "t", "+Ac", "Bw1", "+Bb", "t", "+Ad", "+Ba1", "+Bc", "+Bd", "t",
)
CLOSING = (
    "Bi", "t", "Bj",
)


def run_chain(scatter, gather, stages, tick, before_work, after_work=None):
    x, y, z, core = place()
    count = stages[0]["part"].shape[1] // 2

    def steps_of(stage):
        return {
            half: (
                Scatter(scatter, stage["part"], stage["bufs"], at * count, count),
                Gather(gather, stage["rows"], at * count, count),
            )
            for at, half in enumerate("AB")
        }

    def run(order, stage, now, then=None):
        for name in order:
            if name == "t":
                tick()
                continue
            if name == "x":
                if stage.get("side"):
                    stage["side"].pop(0)()
                continue
            if name[0] == "+":
                steps, name = then, name[1:]
            else:
                steps = now
            half, name = name[0], name[1:]
            rows = pl.ds("AB".index(half) * count, count)
            own_scatter, own_gather = steps[half]
            if name == "e":
                stage[half] = own_scatter.e()
            elif name == "f":
                own_gather.f(stage["between"](stage[half], rows))
            elif name in ("w0", "w1"):
                blocks = pl.ds((core if name == "w1" else 1 - core) * 4, 4)
                stage["work"](blocks, rows)
            elif hasattr(own_scatter, name):
                getattr(own_scatter, name)()
            else:
                getattr(own_gather, name)()

    now = steps_of(stages[0])
    run(OPENING, stages[0], now)
    for at, stage in enumerate(stages):
        run(MIDDLE, stage, now)
        if at == len(stages) - 1:
            run(CLOSING, stage, now)
            break
        if at == 0:
            before_work()
        then = steps_of(stages[at + 1])
        run(TURN_ONE, stage, now, then)
        run(TURN_TWO, stage, now, then)
        if after_work is not None:
            after_work(at)
        now = then


def gather_all(gather, rows_out, tick, arrivals):
    count = rows_out.shape[1] // 2
    halves = [Gather(gather, rows_out, at * count, count) for at in (0, 1)]
    for half, arrive in zip(halves, arrivals):
        arrive()
        for name in ("f", "f2", "f3"):
            getattr(half, name)()
    for name in ("g", "h", "i", "j"):
        tick()
        for half in halves:
            getattr(half, name)()
        tick()


def scatter_all(scatter, part, bufs, tick):
    count = part.shape[1] // 2
    first, second = [Scatter(scatter, part, bufs, at * count, count) for at in (0, 1)]
    for name in OPENING:
        if name == "t":
            tick()
        else:
            getattr(first if name[0] == "A" else second, name[1:])()
    return first.e(), second.e()


def scatter_scratch(rows, width):
    return [
        pltpu.VMEM((4, rows, width), BF16),
        pltpu.VMEM((3, rows, width), BF16),
        pltpu.VMEM((rows, width), BF16),
        pltpu.VMEM((2, rows, width), BF16),
    ]


def sems(count):
    return [pltpu.SemaphoreType.DMA((count,)), pltpu.SemaphoreType.DMA((count,))]


def plane_ring(axis):
    x, y, z, core = place()
    if axis == "x":
        return device(x + 1, y, z, core), device(x + 3, y, z, core)
    return device(x, y, z + 1, core), device(x, y, z + 3, core)


def plane_at(first, u, v):
    return block_of(u, v) if first == "x" else block_of(v, u)


PLANE_GATHER_COPIES = 36
PLANE_SCATTER_COPIES = 36


def gather_plane(copies, out):
    x, y, z, core = place()
    quarter = out.shape[1] // 4
    paths = []
    for first, base in (("x", 0), ("z", 2 * quarter)):
        v, u = (x, z) if first == "x" else (z, x)
        other = "z" if first == "x" else "x"
        paths.append(
            types.SimpleNamespace(
                first=first,
                v=v,
                u=u,
                ring=plane_ring(first),
                cross=plane_ring(other),
                halves=(pl.ds(base, quarter), pl.ds(base + quarter, quarter)),
                whole=pl.ds(base, 2 * quarter),
            )
        )

    def send(path, dv, du, rows, to):
        at = plane_at(path.first, path.v + dv, path.u + du)
        return copies.start(out.at[at, rows], out.at[at, rows], to)

    for path in paths:
        after, before = path.ring
        top, low = path.halves
        path.ta = send(path, 0, 0, top, after)
        path.lb = send(path, 0, 0, low, before)
        path.la = send(path, 0, 0, low, after)
        path.tb = send(path, 0, 0, top, before)
        path.c = {0: [send(path, 0, 0, path.whole, to) for to in path.cross]}
    yield
    for path in paths:
        path.ta.wait_recv()
        path.ft = send(path, 3, 0, path.halves[0], path.ring[0])
        path.lb.wait_recv()
        path.fl = send(path, 1, 0, path.halves[1], path.ring[1])
    yield
    for path in paths:
        path.la.wait_recv()
        path.c[3] = [send(path, 3, 0, path.whole, to) for to in path.cross]
        path.tb.wait_recv()
        path.c[1] = [send(path, 1, 0, path.whole, to) for to in path.cross]
    last = []
    for path in paths:
        path.c[0][0].wait_recv()
        last.append(send(path, 0, 3, path.whole, path.cross[0]))
    yield
    for path in paths:
        path.ft.wait_recv()
        path.fl.wait_recv()
        path.c[2] = [send(path, 2, 0, path.whole, to) for to in path.cross]
    yield
    for path in paths:
        path.c[3][0].wait_recv()
        last.append(send(path, 3, 3, path.whole, path.cross[0]))
        path.c[1][1].wait_recv()
        last.append(send(path, 1, 1, path.whole, path.cross[1]))
    yield
    for path in paths:
        path.c[2][1].wait_recv()
        last.append(send(path, 2, 1, path.whole, path.cross[1]))
    yield
    for path in paths:
        for copy in (path.c[0][1], path.c[3][1], path.c[1][0], path.c[2][0]):
            copy.wait_recv()
    for copy in last:
        copy.wait_recv()


def scatter_plane_scratch(rows, width):
    half = rows // 2
    return [
        pltpu.VMEM((2, 4, half, width), BF16),
        pltpu.VMEM((2, 2, 4, half, width), BF16),
        pltpu.VMEM((2, 4, half, width), BF16),
        pltpu.VMEM((2, 4, half, width), BF16),
        pltpu.VMEM((2, half, width), BF16),
        pltpu.VMEM((2, 2, half, width), BF16),
        pltpu.VMEM((2, 2, half // 2, width), BF16),
    ]


def scatter_plane(copies, part, out, far, near, passed, summed, far2, near2, passed2):
    x, y, z, core = place()
    half = part.shape[1] // 2
    quarter = half // 2
    paths = []
    for at, (first, base) in enumerate((("x", 0), ("z", half))):
        u, v = (x, z) if first == "x" else (z, x)
        other = "z" if first == "x" else "x"
        paths.append(
            types.SimpleNamespace(
                at=at,
                first=first,
                u=u,
                v=v,
                ring=plane_ring(first),
                cross=plane_ring(other),
                rows=pl.ds(base, half),
                base=base,
            )
        )

    def source(path, du, v):
        return (plane_at(path.first, path.u + du, v), path.rows)

    for path in paths:
        at, (after, before) = path.at, path.ring
        path.far = [
            copies.start(
                part.at[source(path, 2, v)], far.at[at, v], after if v < 2 else before
            )
            for v in range(4)
        ]
    for path in paths:
        at, (after, before) = path.at, path.ring
        path.near = [
            copies.start(part.at[source(path, 1, v)], near.at[at, 0, v], after) for v in (2, 3)
        ] + [
            copies.start(part.at[source(path, 3, v)], near.at[at, 1, v], before) for v in (0, 1)
        ]
    yield
    for path in paths:
        at, (after, before) = path.at, path.ring
        for v in (0, 2, 1, 3):
            path.far[v].wait_recv()
            du, slot, to = (1, 0, after) if v < 2 else (3, 1, before)
            own = part[source(path, du, v)].astype(F32)
            passed[at, v] = (own + far[at, v].astype(F32)).astype(BF16)
            path.near.append(copies.start(passed.at[at, v], near.at[at, slot, v], to))
    yield
    for path in paths:
        at = path.at
        for copy in path.near:
            copy.wait_recv()
        for v in range(4):
            own = part[source(path, 0, v)].astype(F32)
            summed[at, v] = (
                own + near[at, 0, v].astype(F32) + near[at, 1, v].astype(F32)
            ).astype(BF16)
        v, (after, before) = path.v, path.cross
        top, low = pl.ds(0, quarter), pl.ds(quarter, quarter)
        v1, v2, v3 = lax.rem(v + 1, 4), lax.rem(v + 2, 4), lax.rem(v + 3, 4)
        path.ft = copies.start(summed.at[at, v2, top], far2.at[at, top], after)
        path.fl = copies.start(summed.at[at, v2, low], far2.at[at, low], before)
        path.last = [
            copies.start(summed.at[at, v1, low], near2.at[at, 0, low], after),
            copies.start(summed.at[at, v3, top], near2.at[at, 1, top], before),
        ]
    yield
    for path in paths:
        at, v, (after, before) = path.at, path.v, path.cross
        top, low = pl.ds(0, quarter), pl.ds(quarter, quarter)
        v1, v3 = lax.rem(v + 1, 4), lax.rem(v + 3, 4)
        path.ft.wait_recv()
        passed2[at, 0] = (summed[at, v1, top].astype(F32) + far2[at, top].astype(F32)).astype(BF16)
        path.last.append(copies.start(passed2.at[at, 0], near2.at[at, 0, top], after))
        path.fl.wait_recv()
        passed2[at, 1] = (summed[at, v3, low].astype(F32) + far2[at, low].astype(F32)).astype(BF16)
        path.last.append(copies.start(passed2.at[at, 1], near2.at[at, 1, low], before))
    yield
    for path in paths:
        at, v = path.at, path.v
        for copy in path.last:
            copy.wait_recv()
        total = summed[at, v].astype(F32) + near2[at, 0].astype(F32) + near2[at, 1].astype(F32)
        out[path.rows] = total.astype(out.dtype)


def params(number):
    return pltpu.CompilerParams(
        collective_id=number, has_side_effects=True, vmem_limit_bytes=56 * 2**20
    )


VMEM = pl.BlockSpec(memory_space=pltpu.VMEM)
HBM = pl.BlockSpec(memory_space=pl.ANY)


def neighbours():
    return [*group_neighbours(), *plane_ring("x"), *plane_ring("z")]


def drain(steps):
    for _ in steps:
        pass


def swap_partner():
    x, y, z, core = place()
    upper = lax.div(x, 2)
    return core != upper, device(core * 2 + lax.rem(x, 2), y, z, upper)


def greet_with_partner(others):
    moves, partner = swap_partner()
    barrier = pltpu.get_barrier_semaphore()
    for other in others:
        pl.semaphore_signal(barrier, inc=1, device_id=other, device_id_type=MESH)

    @pl.when(moves)
    def _():
        pl.semaphore_signal(barrier, inc=1, device_id=partner, device_id_type=MESH)

    pl.semaphore_wait(barrier, len(others) + moves.astype(jnp.int32))


def partner_copy(src, dst, send, recv):
    return pltpu.make_async_remote_copy(
        src_ref=src,
        dst_ref=dst,
        send_sem=send,
        recv_sem=recv,
        device_id=swap_partner()[1],
        device_id_type=MESH,
    )


class Swaps:
    def __init__(self, send, recv):
        self.send, self.recv, self.moves = send, recv, []

    def copy(self, src, dst, own_dst=None):
        at = len(self.moves)
        copy = partner_copy(src, dst, self.send.at[at], self.recv.at[at])
        self.moves.append(copy)
        moves, _ = swap_partner()

        @pl.when(moves)
        def _():
            copy.start()

        @pl.when(jnp.logical_not(moves))
        def _():
            target = dst if own_dst is None else own_dst
            target[...] = src[...]

        return copy

    def arrive(self, copy):
        @pl.when(swap_partner()[0])
        def _():
            copy.wait_recv()

    def finish(self, *arrived):
        @pl.when(swap_partner()[0])
        def _():
            for copy in self.moves:
                copy.wait_send()
                if not any(copy is other for other in arrived):
                    copy.wait_recv()


def start_kernel(
    tokens, w_qkv, w_out, w_in, w_down, row_lengths, b_qv, b_out, b_in, b_down, ln_gain, ln_bias,
    rows_out, own_out, weights_out, attention_out, hidden_first, hidden_later, lengths_out,
    norms_out, bias_in_out, bias_qkv_out, attention, hidden, lengths,
    ssend, srecv, send, recv, wsend, wrecv,
):
    x, y, z, core = place()
    third, width = w_out.shape[2], w_in.shape[2]
    for at in (0, 1):
        for which in range(3):
            attention[at, :, which * third : (which + 1) * third] = w_qkv[at, which]
        attention[at, :, 3 * third :] = w_out[at]
        hidden[at, :, :width] = w_in[at]
        hidden[at, :, width:] = w_down[at]
    lengths[...] = jnp.zeros_like(lengths)
    lengths[0:1, 0:4] = row_lengths[...]
    greet_with_partner(neighbours())
    plane, group, swaps = Copies(wsend, wrecv), Copies(send, recv), Swaps(ssend, srecv)
    there = block_of(core * 2 + lax.rem(x, 2), z)
    own = weights_out.at[block_of(x, z)]
    weights_move = swaps.copy(attention.at[0], weights_out.at[there], own)
    count = tokens.shape[0] // 2
    rows_moves = []
    for half in (pl.ds(0, count), pl.ds(count, count)):
        own = rows_out.at[core * 4 + y, half]
        target = rows_out.at[lax.div(x, 2) * 4 + y, half]
        rows_moves.append(swaps.copy(tokens.at[half], target, own))
    swaps.copy(lengths, lengths_out)
    swaps.arrive(weights_move)
    steps = gather_plane(plane, weights_out)
    next(steps)
    arrivals = [functools.partial(swaps.arrive, move) for move in rows_moves]
    ticks = []

    def tick():
        ticks.append(None)
        next(steps, None)
        if len(ticks) == 3:
            swaps.copy(hidden.at[0], hidden_first)
            swaps.copy(attention.at[1], attention_out)
            swaps.copy(hidden.at[1], hidden_later)

    gather_all(group, rows_out, tick, arrivals)
    own_out[...] = rows_out[core * 4 + y]
    norms_out[0:2] = b_out[...].astype(F32)
    norms_out[2:4] = b_down[...].astype(F32)
    for at in (0, 1):
        norms_out[4 + 2 * at : 6 + 2 * at] = ln_gain[at].astype(F32)
        norms_out[8 + 2 * at : 10 + 2 * at] = ln_bias[at].astype(F32)
    column = core * 4 + y
    own_in = pl.ds(pl.multiple_of(column * width, width), width)
    own_qv = pl.ds(pl.multiple_of(column * third, third), third)
    bias_in_out[...] = b_in[:, own_in].astype(F32)
    for at in (0, 1):
        row = b_qv[at, :, own_qv].astype(F32)
        bias_qkv_out[at : at + 1, :third] = row[0:1]
        bias_qkv_out[at : at + 1, third : 2 * third] = jnp.zeros((1, third), F32)
        bias_qkv_out[at : at + 1, 2 * third :] = row[1:2]
    drain(steps)
    swaps.finish(weights_move, *rows_moves)
    group.wait_sends()
    plane.wait_sends()


def start(tokens, w_qkv, w_out, w_in, w_down, *others):
    rows, width = tokens.shape
    layers, held, hidden_width = w_in.shape
    third = w_out.shape[2]
    columns, hidden_columns = 4 * third, 2 * hidden_width
    shape = jax.ShapeDtypeStruct
    return pl.pallas_call(
        start_kernel,
        out_shape=(
            shape((8, rows, width), BF16),
            shape((rows, width), BF16),
            shape((16, held, columns), BF16),
            shape((held, columns), BF16),
            shape((held, hidden_columns), BF16),
            shape((held, hidden_columns), BF16),
            shape((8, 128), jnp.int32),
            shape((12, width), F32),
            shape((2, hidden_width), F32),
            shape((2, 3 * third), F32),
        ),
        in_specs=[VMEM] * 12,
        out_specs=(VMEM,) * 10,
        scratch_shapes=[
            pltpu.VMEM((layers, held, columns), BF16),
            pltpu.VMEM((layers, held, hidden_columns), BF16),
            pltpu.VMEM((8, 128), jnp.int32),
        ]
        + sems(7)
        + sems(GATHER_COPIES)
        + sems(PLANE_GATHER_COPIES),
        compiler_params=params(0),
        name="start",
    )(tokens, w_qkv, w_out, w_in, w_down, *others)


def normed_parts(stream):
    row_mean = jnp.mean(stream, axis=-1, keepdims=True)
    centered = stream - row_mean
    row_var = jnp.mean(centered * centered, axis=-1, keepdims=True)
    scale = lax.rsqrt(row_var + EPSILON)
    return centered * scale, scale


def norm_pull(unit, scale, gain, grad, sums):
    scaled = grad * gain
    inner = jnp.mean(scaled * unit, axis=-1, keepdims=True)
    pulled = scale * (scaled - jnp.mean(scaled, axis=-1, keepdims=True) - unit * inner)
    low = pulled.astype(BF16)
    sums[0:1] += jnp.sum(grad * unit, axis=0, keepdims=True)
    sums[1:2] += jnp.sum(grad, axis=0, keepdims=True)
    sums[2:3] += jnp.sum(low.astype(F32), axis=0, keepdims=True)
    return pulled, low


INV_SQRT2 = 0.7071067811865476
INV_SQRT_2PI = 0.3989422804014327
CONTRACT_LAST = (((1,), (1,)), ((), ()))
CONTRACT_FIRST = (((0,), (0,)), ((), ()))


def normal_cdf(values):
    return 0.5 * (1.0 + lax.erf(values * INV_SQRT2))


def flatten(block):
    return block.reshape(block.shape[0] * block.shape[1], block.shape[2])


def hidden_forward(ref, hidden_width):
    def work(blocks, rows):
        full_in = flatten(ref.hidden_full[:, :, :hidden_width])
        full_down = flatten(ref.hidden_full[:, :, hidden_width:])
        values = flatten(ref.mlp_input[blocks, rows])
        pre_gelu = jnp.dot(values, full_in, preferred_element_type=F32) + ref.bias_in[ref.layer : ref.layer + 1]
        act = (pre_gelu * normal_cdf(pre_gelu)).astype(BF16)
        branch = lax.dot_general(act, full_down, CONTRACT_LAST, preferred_element_type=F32)
        shape = ref.mlp_input[blocks, rows].shape
        ref.pre_gelu[blocks, rows] = pre_gelu.reshape(*shape[:2], -1)
        ref.act[blocks, rows] = act.reshape(*shape[:2], -1)
        ref.branch_two[blocks, rows] = branch.astype(BF16).reshape(shape)

    return work


def hidden_backward(ref, hidden_width):
    def work(blocks, rows):
        full_in = flatten(ref.hidden_full[:, :, :hidden_width])
        full_down = flatten(ref.hidden_full[:, :, hidden_width:])
        values = flatten(ref.down_full[blocks, rows])
        grad_act = jnp.dot(values, full_down, preferred_element_type=F32)
        pre_gelu = flatten(ref.pre_gelu[blocks, rows])
        slope = normal_cdf(pre_gelu) + pre_gelu * (
            jnp.exp(pre_gelu * pre_gelu * -0.5) * INV_SQRT_2PI
        )
        low = (slope * grad_act).astype(BF16)
        branch = lax.dot_general(low, full_in, CONTRACT_LAST, preferred_element_type=F32)
        shape = ref.down_full[blocks, rows].shape
        ref.pre_low[blocks, rows] = low.reshape(*shape[:2], -1)
        ref.in_sums[0:1] += jnp.sum(low.astype(F32), axis=0, keepdims=True)
        ref.branch_three[blocks, rows] = branch.astype(BF16).reshape(shape)

    return work


def hidden_grads(ref, out):
    pieces = []
    into = out
    hidden_width = into.shape[2] // 2

    def piece(quarter, left, right, base):
        def work():
            values = flatten(left[:, :, quarter * 256 : (quarter + 1) * 256])
            grad = lax.dot_general(
                values, flatten(right[...]), CONTRACT_FIRST, preferred_element_type=F32
            )
            into[quarter * 4 : (quarter + 1) * 4, :, base : base + hidden_width] = grad.astype(
                BF16
            ).reshape(4, 64, hidden_width)

        return work

    for quarter in range(4):
        pieces.append(piece(quarter, ref.down_full, ref.act, hidden_width))
    for quarter in range(4):
        pieces.append(piece(quarter, ref.mlp_input, ref.pre_low, 0))
    return dict(side=pieces)


def param_rows(ref, at, which):
    rows = (2 * which + at, 4 + 2 * at + which, 8 + 2 * at + which)
    return [ref.params[row : row + 1] for row in rows]


def forward_norm(ref, held, at, which, stream_out, normed_out):
    def between(total, rows):
        bias, gain, shift = param_rows(ref, at, which)
        stream = held[rows].astype(F32) + total + bias
        stream_out[rows] = stream
        unit, _ = normed_parts(stream)
        normed = unit * gain + shift
        normed_out[rows] = normed
        return normed.astype(BF16)

    return between


def turn_norm(ref, held, at, which, pulled_out, sums):
    def between(total, rows):
        bias, gain, shift = param_rows(ref, at, which)
        unit, scale = normed_parts(held[rows] + total + bias)
        ref.encoded[rows] = (unit * gain + shift).astype(BF16)
        grad = ref.cotangent[rows].astype(F32)
        pulled, low = norm_pull(unit, scale, gain, grad, sums)
        pulled_out[rows] = pulled
        return low

    return between


def backward_norm(ref, held, at, which, stream, pulled_out, sums):
    def between(total, rows):
        unit, scale = normed_parts(stream[rows])
        grad = held[rows] + total
        pulled, low = norm_pull(unit, scale, param_rows(ref, at, which)[1], grad, sums)
        pulled_out[rows] = pulled
        return low

    return between


def zeroed(ref):
    if not hasattr(ref, "in_sums"):
        return ()
    return (ref.sums_one, ref.sums_two, ref.in_sums)


def chain_call(
    number, name, inputs, outputs, scratch, stages_of,
    gathers=(), scatters=(), swapped=(), late=(), early=(), pace=1, swapped_after=(),
):
    rows, width = 128, 1024
    names_in, names_out, names_scratch = list(inputs), list(outputs), list(scratch)
    stage_count = stages_of({}, True)
    shapes = []
    for key in names_out:
        shape, kind = outputs[key]
        shapes.append(jax.ShapeDtypeStruct(shape, kind))
    scratch_shapes = [pltpu.VMEM(shape, kind) for shape, kind in scratch.values()]
    for _ in range(stage_count):
        scratch_shapes += scatter_scratch(rows, width)
    scratch_shapes += sems(SCATTER_COPIES * stage_count) + sems(GATHER_COPIES * stage_count)
    pieces = [key for sources, _ in scatters for key in sources]
    stored = [key for keys, _ in early for key in keys]
    scratch_shapes += [pltpu.VMEM(inputs[key].shape, inputs[key].dtype) for key in late]
    scratch_shapes += [pltpu.VMEM(*outputs[key]) for key in stored]
    scratch_shapes += [pltpu.SemaphoreType.DMA((len(late) + len(stored) + len(pieces) + 1,))]
    for _ in gathers:
        scratch_shapes += sems(PLANE_GATHER_COPIES)
    for sources, out in scatters:
        kept, columns = {**outputs, **scratch}[out][0]
        scratch_shapes += [pltpu.VMEM((16, kept, columns), BF16)]
        scratch_shapes += sems(PLANE_SCATTER_COPIES) + scatter_plane_scratch(kept, columns)
    if swapped:
        scratch_shapes += sems(len(swapped) + len(swapped_after))

    def kernel(*refs):
        refs = list(refs)
        take = lambda count: [refs.pop(0) for _ in range(count)]
        ref = types.SimpleNamespace()
        held = vars(ref)
        for names in (names_in, names_out, names_scratch):
            held.update(zip(names, take(len(names))))
        bufs = [take(4) for _ in range(stage_count)]
        scatter, gather = Copies(*take(2)), Copies(*take(2))
        far_refs = {key: held[key] for key in (*late, *stored)}
        held.update(zip((*late, *stored), take(len(late) + len(stored))))
        (local,) = take(1)
        fetches, stores, count = [], [], []

        def local_copy(src, dst, kept):
            copy = pltpu.make_async_copy(src, dst, local.at[len(count)])
            copy.start()
            count.append(None)
            kept.append(copy)
            return copy

        for key in late:
            local_copy(far_refs[key], held[key], fetches)

        def after_work(at):
            for keys, stage in early:
                if stage == at:
                    for key in keys:
                        local_copy(held[key], far_refs[key], stores)

        x, y, z, core = place()
        others = neighbours() if gathers or scatters else group_neighbours()
        planes, queue = [], []
        for source, out in gathers:
            plane = Copies(*take(2))
            planes.append(plane)
            queue.append((gather_plane(plane, held[out]), (), True))
        for sources, out in scatters:
            (assembled,) = take(1)
            plane = Copies(*take(2))
            planes.append(plane)
            at, parts = 0, []
            for source in sources:
                columns = pl.ds(at, held[source].shape[-1])
                local_copy(held[source], assembled.at[:, :, columns], parts)
                at += held[source].shape[-1]
            steps = scatter_plane(plane, assembled, held[out], *take(7))
            queue.append((steps, parts, sources))
        stages = stages_of(ref, False)
        for stage, own in zip(stages, bufs):
            stage["bufs"] = own
        if swapped:
            swaps = Swaps(*take(2))
            greet_with_partner(others)
        else:
            greet(others)
        for sums in zeroed(ref):
            sums[...] = jnp.zeros_like(sums)
        for source, out in gathers:
            held[out][block_of(x, z)] = held[source][...]
        started, ended, ticks = [], [], [None] * (pace - 1)

        def tick():
            if not started:
                started.append(True)
                for _, parts, _ in queue:
                    for part in parts:
                        part.wait()
                for source, out in swapped:
                    swaps.copy(held[source], held[out])
            ticks.append(None)
            if len(ticks) % pace:
                return
            advance_planes()

        def advance_planes():
            while queue:
                try:
                    next(queue[0][0])
                    return
                except StopIteration:
                    queue.pop(0)
            if not ended:
                ended.append(True)
                for source, out in swapped_after:
                    swaps.copy(held[source], held[out])

        def before_work():
            if gathers and len(queue) == len(gathers) + len(scatters):
                drain(queue.pop(0)[0])
            for copy in fetches:
                copy.wait()
            fetches.clear()

        run_chain(scatter, gather, stages, tick, before_work, after_work)
        for steps, *_ in queue:
            drain(steps)
        queue.clear()
        advance_planes()
        for copies in (scatter, gather, *planes):
            copies.wait_sends()
        for copy in stores:
            copy.wait()
        if swapped:
            swaps.finish()

    results = pl.pallas_call(
        kernel,
        out_shape=tuple(shapes),
        in_specs=[HBM if key in (*late, *pieces) else VMEM for key in names_in],
        out_specs=tuple(HBM if key in stored else VMEM for key in names_out),
        scratch_shapes=scratch_shapes,
        compiler_params=params(number),
        name=name,
    )(*inputs.values())
    return dict(zip(names_out, results))


def sum_small(copies, small, out, got_x, got_z):
    x, y, z, core = place()
    own = core * 4 + y
    along_x = [device(x + step, y, z, core) for step in (1, 2, 3)]
    along_z = [device(x, y, z + step, core) for step in (1, 2, 3)]
    along_y = [device(x, y + step, z, core) for step in (1, 2, 3)]
    first = [copies.start(small, got_x.at[at], to) for at, to in enumerate(along_x)]
    yield
    for copy in first:
        copy.wait_recv()
    got_z[3] = small[...] + got_x[0] + got_x[1] + got_x[2]
    second = [copies.start(got_z.at[3], got_z.at[at], to) for at, to in enumerate(along_z)]
    yield
    for copy in second:
        copy.wait_recv()
    out[own] = got_z[3] + got_z[0] + got_z[1] + got_z[2]
    third = [copies.start(out.at[own], out.at[own], to) for to in along_y]
    yield
    for copy in third:
        copy.wait_recv()
    held = out.at[pl.ds(core * 4, 4)]
    copies.start(held, held, device(x, y, z, 1 - core)).wait_recv()


def end_kernel(*refs):
    refs = list(refs)
    take = lambda count: [refs.pop(0) for _ in range(count)]
    part, held, *pieces = take(5)
    layer_sums = [take(4), take(4)]
    rows_out, grads_out, small_out = take(3)
    grads, local = take(2)
    bufs, plane_bufs = take(4), take(7)
    rows_stage, grads_stage, small, got_x, got_z = take(5)
    swaps, group, plane, tiny = Swaps(*take(2)), Copies(*take(2)), Copies(*take(2)), Copies(*take(2))
    x, y, z, core = place()
    at, fetches = 0, []
    for number, piece in enumerate(pieces):
        columns = pl.ds(at, piece.shape[2])
        fetches.append(pltpu.make_async_copy(piece, grads.at[:, :, columns], local.at[number]))
        fetches[-1].start()
        at += piece.shape[2]
    small[...] = jnp.zeros_like(small)
    for base, (sums_one, sums_two, qkv_sums, in_sums) in zip((0, 8), layer_sums):
        third, hidden_width = qkv_sums.shape[1] // 3, in_sums.shape[1]
        small[base : base + 3] = sums_one[0:3]
        small[base + 3 : base + 6] = sums_two[0:3]
        small[base + 6 : base + 7, :third] = qkv_sums[0:1, :third]
        small[base + 6 : base + 7, third : 2 * third] = qkv_sums[0:1, 2 * third :]
        small[base + 6 : base + 7, 2 * third : 2 * third + hidden_width] = in_sums[0:1]
    greet_with_partner(
        neighbours()
        + [device(x + 2, y, z, core), device(x, y + 2, z, core), device(x, y, z + 2, core)]
    )
    tiny_steps = sum_small(tiny, small, small_out, got_x, got_z)
    plane_steps = scatter_plane(plane, grads, grads_stage, *plane_bufs)
    ticks = []

    def tick():
        ticks.append(None)
        if len(ticks) == 1:
            next(tiny_steps)
            for copy in fetches:
                copy.wait()
            next(plane_steps)
        elif len(ticks) == 2:
            next(tiny_steps)
        elif len(ticks) == 3:
            next(plane_steps)

    totals = scatter_all(group, part, bufs, tick)
    count = rows_stage.shape[0] // 2
    for at in (0, 1):
        rows = pl.ds(at * count, count)
        rows_stage[rows] = (held[rows] + totals[at]).astype(BF16)
    swaps.copy(rows_stage, rows_out)
    next(plane_steps)
    next(tiny_steps)
    next(plane_steps)
    drain(tiny_steps)
    drain(plane_steps)
    swaps.copy(grads_stage, grads_out)
    swaps.finish()
    group.wait_sends()
    plane.wait_sends()
    tiny.wait_sends()


def end(part, held, pieces, layer_sums):
    rows, width = held.shape
    kept, columns = pieces[0].shape[1], sum(piece.shape[2] for piece in pieces)
    shape = jax.ShapeDtypeStruct
    return pl.pallas_call(
        end_kernel,
        out_shape=(
            shape((rows, width), BF16),
            shape((kept, columns), BF16),
            shape((8, 16, width), F32),
        ),
        in_specs=[VMEM] * 2 + [HBM] * 3 + [VMEM] * 8,
        out_specs=(VMEM,) * 3,
        scratch_shapes=[pltpu.VMEM((16, kept, columns), BF16), pltpu.SemaphoreType.DMA((3,))]
        + scatter_scratch(rows, width)
        + scatter_plane_scratch(kept, columns)
        + [
            pltpu.VMEM((rows, width), BF16),
            pltpu.VMEM((kept, columns), BF16),
            pltpu.VMEM((16, width), F32),
            pltpu.VMEM((3, 16, width), F32),
            pltpu.VMEM((4, 16, width), F32),
        ]
        + sems(2)
        + sems(SCATTER_COPIES)
        + sems(PLANE_SCATTER_COPIES)
        + sems(10),
        compiler_params=params(1),
        name="end",
    )(part, held, *pieces, *layer_sums[0], *layer_sums[1])


def finish_kernel(
    small, zero, one, encoded, rows,
    encoded_out, rows_out, g_qkv, g_b_qv, g_out, g_b_out, g_in, g_b_in, g_down, g_b_down, g_gain, g_shift,
):
    third, hidden_width = g_out.shape[2], g_in.shape[2]
    cut = 4 * third
    encoded_out[...] = encoded[...]
    rows_out[...] = rows[...]
    for at, grads in enumerate((zero, one)):
        for which in range(3):
            columns = slice(which * third, (which + 1) * third)
            g_qkv[at, which] = grads[:, columns].astype(F32)
        g_out[at] = grads[:, 3 * third : cut].astype(F32)
        g_in[at] = grads[:, cut : cut + hidden_width].astype(F32)
        g_down[at] = grads[:, cut + hidden_width :].astype(F32)
        rows = jnp.sum(small[:, at * 8 : at * 8 + 8], axis=0)
        g_gain[at, 0:1], g_shift[at, 0:1], g_b_out[at : at + 1] = rows[0:1], rows[1:2], rows[2:3]
        g_gain[at, 1:2], g_shift[at, 1:2], g_b_down[at : at + 1] = rows[3:4], rows[4:5], rows[5:6]
        for block in range(8):
            row = small[block, at * 8 + 6 : at * 8 + 7]
            columns = slice(block * third, (block + 1) * third)
            g_b_qv[at, 0:1, columns] = row[:, :third]
            g_b_qv[at, 1:2, columns] = row[:, third : 2 * third]
            columns = slice(block * hidden_width, (block + 1) * hidden_width)
            g_b_in[at : at + 1, columns] = row[:, 2 * third : 2 * third + hidden_width]


def finish(small, zero, one, encoded, rows, third):
    kept, hidden_width = zero.shape[0], (zero.shape[1] - 4 * third) // 2
    width = small.shape[2]
    shapes = (
        (2, 3, kept, third),
        (2, 2, width),
        (2, kept, third),
        (2, width),
        (2, kept, hidden_width),
        (2, 8 * hidden_width),
        (2, kept, hidden_width),
        (2, width),
        (2, 2, width),
        (2, 2, width),
    )
    outs = [jax.ShapeDtypeStruct(encoded.shape, BF16)] * 2
    outs += [jax.ShapeDtypeStruct(shape, F32) for shape in shapes]
    return pl.pallas_call(
        finish_kernel,
        out_shape=tuple(outs),
        in_specs=[VMEM] * 5,
        out_specs=(VMEM,) * len(outs),
        compiler_params=pltpu.CompilerParams(vmem_limit_bytes=48 * 2**20),
        name="finish",
    )(small, zero, one, encoded, rows)


HEAD_SCALE = DH ** (-0.5)


def segment_parts(lengths, rows):
    def of(shape, dim):
        positions = lax.broadcasted_iota(jnp.int32, shape, dim)
        end, segments = 0, jnp.zeros(shape, jnp.int32)
        for at in range(4):
            end = end + lengths[0, at]
            segments += (positions >= end).astype(jnp.int32)
        return jnp.where(segments == 4, 4 + positions, segments)

    return of((rows, 1), 0), of((1, rows), 1)


def head_lanes(values, head):
    lanes = lax.broadcasted_iota(jnp.int32, values.shape, 1)
    return jnp.where((lanes >= head * DH) & (lanes < (head + 1) * DH), values, 0)


def pick_heads(parts):
    features = lax.broadcasted_iota(jnp.int32, parts[0].shape, 0)
    return jnp.where(features < DH, parts[0], parts[1])


CHUNK = 1024


def attend_kernel(lengths, rows, weights, bias, qkv_out, context_out, lse_out, branch_out, v_turned, seg_row):
    total, width = rows.shape[0], context_out.shape[1]
    column, row = segment_parts(lengths, total)
    seg_row[...] = jnp.broadcast_to(row, seg_row.shape)

    def chunk(at):
        return pl.ds(pl.multiple_of(at * CHUNK, CHUNK), CHUNK)

    @pl.loop(0, total // CHUNK)
    def _(at):
        r = chunk(at)
        qkv = jnp.dot(rows[r], weights[:, : 3 * width], preferred_element_type=F32)
        qkv_out[r] = (qkv + bias[0:1]).astype(BF16)

    keys = qkv_out[:, width : 2 * width]
    v_turned[...] = qkv_out[:, 2 * width :].astype(F32).T.astype(BF16)

    @pl.loop(0, total // CHUNK)
    def _(at):
        r = chunk(at)
        queries = qkv_out[r, :width].astype(F32) * HEAD_SCALE
        allowed = column == seg_row[0:1, r]
        parts = []
        for head in range(2):
            own = head_lanes(queries, head).astype(BF16)
            scores = lax.dot_general(keys, own, CONTRACT_LAST, preferred_element_type=F32)
            scores = jnp.where(allowed, scores, -1e30)
            peak = jnp.max(scores, axis=0, keepdims=True)
            raised = jnp.exp(scores - peak)
            total_row = jnp.sum(raised, axis=0, keepdims=True)
            probs = (raised * (1.0 / total_row)).astype(BF16)
            parts.append(jnp.dot(v_turned[...], probs, preferred_element_type=F32))
            lse_out[head : head + 1, r] = peak + jnp.log(total_row)
        context = pick_heads(parts).T.astype(BF16)
        context_out[r] = context
        branch = lax.dot_general(
            context, weights[:, 3 * width :], CONTRACT_LAST, preferred_element_type=F32
        )
        branch_out[r] = branch.astype(BF16)


def attend(lengths, rows, weights, bias):
    total, width = rows.shape[0], weights.shape[1] // 4
    shape = jax.ShapeDtypeStruct
    return pl.pallas_call(
        attend_kernel,
        out_shape=(
            shape((total, 3 * width), BF16),
            shape((total, width), BF16),
            shape((8, total), F32),
            shape((total, rows.shape[1]), BF16),
        ),
        in_specs=[pl.BlockSpec(memory_space=pltpu.SMEM)] + [VMEM] * 3,
        out_specs=(VMEM,) * 4,
        scratch_shapes=[pltpu.VMEM((width, total), BF16), pltpu.VMEM((8, total), jnp.int32)],
        compiler_params=pltpu.CompilerParams(vmem_limit_bytes=60 * 2**20),
        name="attend",
    )(lengths, rows, weights, bias)


def attend_back_kernel(
    lengths, grad_rows, rows, weights, qkv, context, lse,
    g_qkv, g_out, branch_out, sums_out,
    grad_context, grad_qkv, k_turned, k_sum, v_sum, seg_row,
):
    total, width = rows.shape[0], context.shape[1]
    column, row = segment_parts(lengths, total)
    seg_row[...] = jnp.broadcast_to(row, seg_row.shape)

    def chunk(at):
        return pl.ds(pl.multiple_of(at * CHUNK, CHUNK), CHUNK)

    @pl.loop(0, total // CHUNK)
    def _(at):
        r = chunk(at)
        grad_context[r] = jnp.dot(
            grad_rows[r], weights[:, 3 * width :], preferred_element_type=F32
        ).astype(BF16)

    keys, values = qkv[:, width : 2 * width], qkv[:, 2 * width :]
    k_turned[...] = keys.astype(F32).T.astype(BF16)
    k_sum[...] = jnp.zeros_like(k_sum)
    v_sum[...] = jnp.zeros_like(v_sum)

    @pl.loop(0, total // CHUNK)
    def _(at):
        r = chunk(at)
        queries = qkv[r, :width].astype(F32) * HEAD_SCALE
        grads = grad_context[r].astype(F32)
        allowed = column == seg_row[0:1, r]
        parts = []
        for head in range(2):
            own = head_lanes(queries, head).astype(BF16)
            own_grads = head_lanes(grads, head).astype(BF16)
            scores = lax.dot_general(keys, own, CONTRACT_LAST, preferred_element_type=F32)
            scores = jnp.where(allowed, scores, -1e30)
            probs = jnp.exp(scores - lse[head : head + 1, r])
            grad_probs = lax.dot_general(
                values, own_grads, CONTRACT_LAST, preferred_element_type=F32
            )
            v_sum[...] += jnp.dot(probs.astype(BF16), own_grads, preferred_element_type=F32)
            inner = jnp.sum(probs * grad_probs, axis=0, keepdims=True)
            grad_scores = (probs * (grad_probs - inner)).astype(BF16)
            k_sum[...] += jnp.dot(grad_scores, own, preferred_element_type=F32)
            parts.append(jnp.dot(k_turned[...], grad_scores, preferred_element_type=F32))
        grad_qkv[r, :width] = (pick_heads(parts).T * HEAD_SCALE).astype(BF16)

    grad_qkv[:, width : 2 * width] = k_sum[...].astype(BF16)
    grad_qkv[:, 2 * width :] = v_sum[...].astype(BF16)
    sums_out[...] = jnp.broadcast_to(
        jnp.sum(grad_qkv[...].astype(F32), axis=0, keepdims=True), sums_out.shape
    )

    @pl.loop(0, total // CHUNK)
    def _(at):
        r = chunk(at)
        branch = lax.dot_general(
            grad_qkv[r], weights[:, : 3 * width], CONTRACT_LAST, preferred_element_type=F32
        )
        branch_out[r] = branch.astype(BF16)

    @pl.loop(0, rows.shape[1] // CHUNK)
    def _(at):
        c = chunk(at)
        turned = lax.dot_general(
            grad_qkv[...], rows[:, c], CONTRACT_FIRST, preferred_element_type=F32
        )
        g_qkv[c] = turned.T.astype(BF16)
        turned = lax.dot_general(
            context[...], grad_rows[:, c], CONTRACT_FIRST, preferred_element_type=F32
        )
        g_out[c] = turned.T.astype(BF16)


def attend_back(lengths, grad_rows, rows, weights, qkv, context, lse):
    total, width = context.shape
    depth = rows.shape[1]
    shape = jax.ShapeDtypeStruct
    return pl.pallas_call(
        attend_back_kernel,
        out_shape=(
            shape((depth, 3 * width), BF16),
            shape((depth, width), BF16),
            shape((total, depth), BF16),
            shape((8, 3 * width), F32),
        ),
        in_specs=[pl.BlockSpec(memory_space=pltpu.SMEM)] + [VMEM] * 6,
        out_specs=(VMEM,) * 4,
        scratch_shapes=[
            pltpu.VMEM((total, width), BF16),
            pltpu.VMEM((total, 3 * width), BF16),
            pltpu.VMEM((width, total), BF16),
            pltpu.VMEM((total, width), F32),
            pltpu.VMEM((total, width), F32),
            pltpu.VMEM((8, total), jnp.int32),
        ],
        compiler_params=pltpu.CompilerParams(vmem_limit_bytes=60 * 2**20),
        name="attend_back",
    )(lengths, grad_rows, rows, weights, qkv, context, lse)


def shards(
    tokens,
    lengths,
    w_qkv,
    b_qv,
    w_out,
    b_out,
    w_in,
    b_in,
    w_down,
    b_down,
    ln_gain,
    ln_bias,
    cotangent,
):
    own_rows, width = tokens.shape
    total_rows = own_rows * 8
    layers, kept = w_qkv.shape[:2]
    col_width = w_qkv.shape[3]
    hidden_width = w_in.shape[2]

    (
        rows_zero, hidden, attention_zero, attention_shard, hidden_zero, hidden_one, lengths,
        norm_params, bias_in, bias_qkv,
    ) = start(
        tokens, w_qkv.transpose(0, 2, 1, 3), w_out.transpose(0, 2, 1), w_in,
        w_down.transpose(0, 2, 1), lengths, b_qv, b_out, b_in, b_down, ln_gain, ln_bias,
    )

    own_kind = ((own_rows, width), F32)
    sum_kind = ((8, width), F32)
    low_kind = ((own_rows, width), BF16)
    all_kind = ((8, own_rows, width), BF16)
    act_kind = ((8, own_rows, hidden_width), BF16)
    gelu_kind = ((8, own_rows, hidden_width), F32)
    in_sum_kind = ((8, hidden_width), F32)
    hidden_kind = ((16, kept, 2 * hidden_width), BF16)
    attention_kind = ((16, kept, 4 * col_width), BF16)
    grads_kind = ((kept, 4 * col_width + 2 * hidden_width), BF16)

    def attention(at, rows, full):
        rows, full = rows.reshape(total_rows, width), full.reshape(width, 4 * col_width)
        qkv, context, lse, branch = attend(lengths, rows, full, bias_qkv[at : at + 1])
        return branch.reshape(all_kind[0]), (rows, full, qkv, context, lse)

    def attention_back(stored, rows):
        grad_rows = rows.reshape(total_rows, width)
        g_qkv, g_out, branch, sums = attend_back(lengths, grad_rows, *stored)
        pieces = (g_qkv.reshape(16, kept, -1), g_out.reshape(16, kept, -1))
        return branch.reshape(all_kind[0]), pieces, sums

    branch, stored_zero = attention(0, rows_zero, attention_zero)

    def zero_stages(ref, counting):
        if counting:
            return 2
        ref.layer = 0
        return [
            dict(
                part=ref.branch,
                rows=ref.mlp_input,
                between=forward_norm(ref, ref.held, 0, 0, ref.first_sum, ref.normed),
                work=hidden_forward(ref, hidden_width),
            ),
            dict(
                part=ref.branch_two,
                rows=ref.rows,
                between=forward_norm(ref, ref.normed, 0, 1, ref.second_sum, ref.hidden),
            ),
        ]

    zero = chain_call(
        2,
        "layer_zero",
        dict(
            branch=branch,
            held=hidden,
            params=norm_params,
            bias_in=bias_in,
            hidden_shard=hidden_zero,
            attention_shard=attention_shard,
            next_cotangent=cotangent,
        ),
        dict(
            first_sum=own_kind,
            second_sum=own_kind,
            hidden=own_kind,
            mlp_input=all_kind,
            pre_gelu=gelu_kind,
            act=act_kind,
            rows=all_kind,
            hidden_full=hidden_kind,
            attention_full=attention_kind,
            moved_cotangent=low_kind,
        ),
        dict(normed=own_kind, branch_two=all_kind),
        zero_stages,
        gathers=(("hidden_shard", "hidden_full"), ("attention_shard", "attention_full")),
        swapped=(("next_cotangent", "moved_cotangent"),),
        early=((("first_sum", "mlp_input", "pre_gelu", "act", "hidden_full"), 0),),
    )

    branch, stored_one = attention(1, zero["rows"], zero["attention_full"])

    def one_stages(ref, counting):
        if counting:
            return 3
        ref.layer = 1
        return [
            dict(
                part=ref.branch,
                rows=ref.mlp_input,
                between=forward_norm(ref, ref.held, 1, 0, ref.first_sum, ref.normed),
                work=hidden_forward(ref, hidden_width),
            ),
            dict(
                part=ref.branch_two,
                rows=ref.down_full,
                between=turn_norm(ref, ref.normed, 1, 1, ref.pulled, ref.sums_two),
                work=hidden_backward(ref, hidden_width),
            ),
            dict(
                part=ref.branch_three,
                rows=ref.rows,
                between=backward_norm(ref, ref.pulled, 1, 0, ref.first_sum, ref.grad_first, ref.sums_one),
                **hidden_grads(ref, ref.grads),
            ),
        ]

    one = chain_call(
        3,
        "layer_one",
        dict(
            branch=branch,
            held=zero["hidden"],
            params=norm_params,
            bias_in=bias_in,
            hidden_shard=hidden_one,
            cotangent=zero["moved_cotangent"],
        ),
        dict(
            encoded=low_kind,
            grad_first=own_kind,
            sums_one=sum_kind,
            sums_two=sum_kind,
            in_sums=in_sum_kind,
            rows=all_kind,
            grads=hidden_kind,
        ),
        dict(
            mlp_input=all_kind,
            act=act_kind,
            down_full=all_kind,
            pre_low=act_kind,
            first_sum=own_kind,
            normed=own_kind,
            pulled=own_kind,
            pre_gelu=gelu_kind,
            hidden_full=hidden_kind,
            branch_two=all_kind,
            branch_three=all_kind,
        ),
        one_stages,
        gathers=(("hidden_shard", "hidden_full"),),
        early=((("encoded",), 1),),
    )
    branch, pieces, qkv_sums_one = attention_back(stored_one, one["rows"])

    def back_stages(ref, counting):
        if counting:
            return 2
        return [
            dict(
                part=ref.branch,
                rows=ref.down_full,
                between=backward_norm(ref, ref.held, 0, 1, ref.second_sum, ref.pulled, ref.sums_two),
                work=hidden_backward(ref, hidden_width),
            ),
            dict(
                part=ref.branch_three,
                rows=ref.rows,
                between=backward_norm(ref, ref.pulled, 0, 0, ref.first_sum, ref.grad_first, ref.sums_one),
                **hidden_grads(ref, ref.grads),
            ),
        ]

    back = chain_call(
        4,
        "layer_back",
        dict(
            branch=branch,
            held=one["grad_first"],
            params=norm_params,
            first_sum=zero["first_sum"],
            second_sum=zero["second_sum"],
            pre_gelu=zero["pre_gelu"],
            hidden_full=zero["hidden_full"],
            mlp_input=zero["mlp_input"],
            act=zero["act"],
            grad_w_qkv=pieces[0],
            grad_w_out=pieces[1],
            grad_hidden=one["grads"],
            own_encoded=one["encoded"],
        ),
        dict(
            grad_first=own_kind,
            sums_one=sum_kind,
            sums_two=sum_kind,
            in_sums=in_sum_kind,
            rows=all_kind,
            moved_grads=grads_kind,
            grads=hidden_kind,
            encoded=low_kind,
        ),
        dict(later_grads=grads_kind, down_full=all_kind, pre_low=act_kind, pulled=own_kind, branch_three=all_kind),
        back_stages,
        scatters=((("grad_w_qkv", "grad_w_out", "grad_hidden"), "later_grads"),),
        swapped=(("own_encoded", "encoded"),),
        swapped_after=(("later_grads", "moved_grads"),),
        late=("pre_gelu", "hidden_full", "mlp_input", "act"),
        pace=2,
    )
    branch, pieces, qkv_sums_zero = attention_back(stored_zero, back["rows"])
    g_tokens, grads_zero, small = end(
        branch,
        back["grad_first"],
        (*pieces, back["grads"]),
        (
            (back["sums_one"], back["sums_two"], qkv_sums_zero, back["in_sums"]),
            (one["sums_one"], one["sums_two"], qkv_sums_one, one["in_sums"]),
        ),
    )
    (
        encoded, g_tokens, g_qkv, g_b_qv, g_out, g_b_out, g_in, g_b_in, g_down, g_b_down, g_gain, g_shift,
    ) = finish(small, grads_zero, back["moved_grads"], back["encoded"], g_tokens, col_width)
    return (
        encoded,
        g_tokens,
        g_qkv.transpose(0, 2, 1, 3),
        g_b_qv,
        g_out.transpose(0, 2, 1),
        g_b_out,
        g_in,
        g_b_in,
        g_down.transpose(0, 2, 1),
        g_b_down,
        g_gain,
        g_shift,
    )


def solution(mesh):
    placed = (
        P(("dp", "tensor"), None),
        P("dp", None),
        P(None, "dp", None, "tensor"),
        P(),
        P(None, "tensor", "dp"),
        P(),
        P(None, "dp", "tensor"),
        P(),
        P(None, "tensor", "dp"),
        P(),
        P(),
        P(),
        P(("dp", "tensor"), None),
    )
    return jax.shard_map(
        shards,
        mesh=mesh,
        in_specs=placed,
        out_specs=(
            P(("dp", "tensor"), None),
            P(("dp", "tensor"), None),
            P(None, "dp", None, "tensor"),
            P(),
            P(None, "tensor", "dp"),
            P(),
            P(None, "dp", "tensor"),
            P(),
            P(None, "tensor", "dp"),
            P(),
            P(),
            P(),
        ),
        check_vma=False,
    )
```

```python
import functools
import types

import jax
import jax.numpy as jnp
from jax import lax
from jax.experimental import pallas as pl
from jax.experimental.pallas import tpu as pltpu
from jax.sharding import PartitionSpec as P

DH = 64
EPSILON = 1e-06
MESH = pl.DeviceIdType.MESH
F32 = jnp.float32
BF16 = jnp.bfloat16


def place():
    dp, tensor = lax.axis_index("dp"), lax.axis_index("tensor")
    core = lax.rem(dp, 2)
    z = lax.rem(lax.div(dp, 2), 4)
    x = lax.rem(lax.div(tensor, 4) * 2 + lax.div(dp, 8), 4)
    y = lax.rem(tensor, 4)
    return x, y, z, core


def device(x, y, z, core):
    x, y, z = lax.rem(x, 4), lax.rem(y, 4), lax.rem(z, 4)
    return (lax.rem(x, 2) * 8 + z * 2 + core, lax.div(x, 2) * 4 + y)


def block_of(x, z):
    x, z = lax.rem(x, 4), lax.rem(z, 4)
    return lax.rem(x, 2) * 8 + z * 2 + lax.div(x, 2)


def greet(devices):
    barrier = pltpu.get_barrier_semaphore()
    for other in devices:
        pl.semaphore_signal(barrier, inc=1, device_id=other, device_id_type=MESH)
    pl.semaphore_wait(barrier, len(devices))


class Copies:
    def __init__(self, send, recv):
        self.send, self.recv, self.started = send, recv, []

    def start(self, src, dst, to):
        at = len(self.started)
        copy = pltpu.make_async_remote_copy(
            src_ref=src,
            dst_ref=dst,
            send_sem=self.send.at[at],
            recv_sem=self.recv.at[at],
            device_id=to,
            device_id_type=MESH,
        )
        copy.start()
        self.started.append(copy)
        return copy

    def wait_sends(self):
        for copy in self.started:
            copy.wait_send()


def group_neighbours():
    x, y, z, core = place()
    return (
        device(x, y, z, 1 - core),
        device(x, y + 1, z, core),
        device(x, y + 3, z, core),
    )


GATHER_COPIES = 24
SCATTER_COPIES = 20


class Gather:
    def __init__(self, copies, out, base, count):
        self.x, self.y, self.z, self.core = place()
        self.pair, self.after, self.before = group_neighbours()
        half = count // 2
        self.top, self.low = pl.ds(base, half), pl.ds(base + half, half)
        self.both = pl.ds(base, count)
        self.copies, self.out = copies, out

    def send(self, step, rows, to):
        ref = self.out.at[self.core * 4 + lax.rem(self.y + step, 4), rows]
        return self.copies.start(ref, ref, to)

    def f(self, low=None):
        if low is not None:
            self.out[self.core * 4 + self.y, self.both] = low
        self.top_after = self.send(0, self.top, self.after)
        self.low_before = self.send(0, self.low, self.before)

    def f2(self):
        self.low_after = self.send(0, self.low, self.after)
        self.top_before = self.send(0, self.top, self.before)

    def f3(self):
        self.paired = [self.send(0, self.both, self.pair)]

    def g(self):
        self.top_after.wait_recv()
        self.far_top = self.send(3, self.top, self.after)
        self.low_before.wait_recv()
        self.far_low = self.send(1, self.low, self.before)

    def h(self):
        self.low_after.wait_recv()
        self.paired.append(self.send(3, self.both, self.pair))
        self.top_before.wait_recv()
        self.paired.append(self.send(1, self.both, self.pair))

    def i(self):
        self.far_top.wait_recv()
        self.paired.append(self.send(2, self.top, self.pair))
        self.far_low.wait_recv()
        self.paired.append(self.send(2, self.low, self.pair))

    def j(self):
        for copy in self.paired:
            copy.wait_recv()


class Scatter:
    def __init__(self, copies, part, bufs, base, count):
        self.x, self.y, self.z, self.core = place()
        self.pair, self.after, self.before = group_neighbours()
        half = count // 2
        self.top, self.low = pl.ds(base, half), pl.ds(base + half, half)
        self.both = pl.ds(base, count)
        self.copies, self.part = copies, part
        self.from_pair, self.staged, self.far, self.near = bufs
        self.swaps = []

    STEPS = (2, 1, 3, 0)

    def swap(self, slot):
        at = (1 - self.core) * 4 + lax.rem(self.y + self.STEPS[slot], 4)
        src, dst = self.part.at[at, self.both], self.from_pair.at[slot, self.both]
        self.swaps.append(self.copies.start(src, dst, self.pair))

    def chip(self, slot, rows):
        own = self.part[self.core * 4 + lax.rem(self.y + self.STEPS[slot], 4), rows]
        return own.astype(F32) + self.from_pair[slot, rows].astype(F32)

    def pass_on(self, slot, rows, value, dst, to):
        self.staged[slot, rows] = value.astype(BF16)
        return self.copies.start(self.staged.at[slot, rows], dst, to)

    def a0(self):
        self.swap(0)

    def a1(self):
        for slot in (1, 2, 3):
            self.swap(slot)

    def b(self):
        self.swaps[0].wait_recv()
        top, low = self.top, self.low
        self.far_top = self.pass_on(0, top, self.chip(0, top), self.far.at[top], self.after)
        self.far_low = self.pass_on(0, low, self.chip(0, low), self.far.at[low], self.before)

    def c(self):
        top, low = self.top, self.low
        self.swaps[1].wait_recv()
        low_after = self.pass_on(1, low, self.chip(1, low), self.near.at[0, low], self.after)
        self.swaps[2].wait_recv()
        top_before = self.pass_on(2, top, self.chip(2, top), self.near.at[1, top], self.before)
        self.last = [low_after, top_before]

    def d(self):
        top, low = self.top, self.low
        self.far_top.wait_recv()
        value = self.chip(1, top) + self.far[top].astype(F32)
        self.last.append(self.pass_on(1, top, value, self.near.at[0, top], self.after))
        self.far_low.wait_recv()
        value = self.chip(2, low) + self.far[low].astype(F32)
        self.last.append(self.pass_on(2, low, value, self.near.at[1, low], self.before))

    def e(self):
        self.swaps[3].wait_recv()
        own = self.chip(3, self.both)
        for copy in self.last:
            copy.wait_recv()
        return own + self.near[0, self.both].astype(F32) + self.near[1, self.both].astype(F32)


OPENING = (
    "Aa0", "Ab", "Ba0", "Aa1", "Bb", "t", "Ac", "Ad", "t", "Ba1",
    "Bc", "Bd", "t",
)
MIDDLE = (
    "x", "x", "Ae", "Af", "Af2", "x", "x", "Be", "Bf", "Bf3",
    "Af3", "t", "Bf2", "x", "x", "Ag", "t", "Bg", "Bh", "x",
    "x", "t", "Ah", "Ai", "Aj",
)
TURN_ONE = (
    "Aw0", "+Aa0", "Bi", "+Aa1", "Aw1", "t", "+Ab", "Bj", "Bw0", "+Ba0",
)
TURN_TWO = (
    "t", "+Ac", "Bw1", "+Bb", "t", "+Ad", "+Ba1", "+Bc", "+Bd", "t",
)
CLOSING = (
    "Bi", "t", "Bj",
)


def run_chain(scatter, gather, stages, tick, before_work, after_work=None):
    x, y, z, core = place()
    count = stages[0]["part"].shape[1] // 2

    def steps_of(stage):
        return {
            half: (
                Scatter(scatter, stage["part"], stage["bufs"], at * count, count),
                Gather(gather, stage["rows"], at * count, count),
            )
            for at, half in enumerate("AB")
        }

    def run(order, stage, now, then=None):
        for name in order:
            if name == "t":
                tick()
                continue
            if name == "x":
                if stage.get("side"):
                    stage["side"].pop(0)()
                continue
            if name[0] == "+":
                steps, name = then, name[1:]
            else:
                steps = now
            half, name = name[0], name[1:]
            rows = pl.ds("AB".index(half) * count, count)
            own_scatter, own_gather = steps[half]
            if name == "e":
                stage[half] = own_scatter.e()
            elif name == "f":
                own_gather.f(stage["between"](stage[half], rows))
            elif name in ("w0", "w1"):
                blocks = pl.ds((core if name == "w1" else 1 - core) * 4, 4)
                stage["work"](blocks, rows)
            elif hasattr(own_scatter, name):
                getattr(own_scatter, name)()
            else:
                getattr(own_gather, name)()

    now = steps_of(stages[0])
    run(OPENING, stages[0], now)
    for at, stage in enumerate(stages):
        run(MIDDLE, stage, now)
        if at == len(stages) - 1:
            run(CLOSING, stage, now)
            break
        if at == 0:
            before_work()
        then = steps_of(stages[at + 1])
        run(TURN_ONE, stage, now, then)
        run(TURN_TWO, stage, now, then)
        if after_work is not None:
            after_work(at)
        now = then


def gather_all(gather, rows_out, tick, arrivals):
    count = rows_out.shape[1] // 2
    halves = [Gather(gather, rows_out, at * count, count) for at in (0, 1)]
    for half, arrive in zip(halves, arrivals):
        arrive()
        for name in ("f", "f2", "f3"):
            getattr(half, name)()
    for name in ("g", "h", "i", "j"):
        tick()
        for half in halves:
            getattr(half, name)()
        tick()


def scatter_all(scatter, part, bufs, tick):
    count = part.shape[1] // 2
    first, second = [Scatter(scatter, part, bufs, at * count, count) for at in (0, 1)]
    for name in OPENING:
        if name == "t":
            tick()
        else:
            getattr(first if name[0] == "A" else second, name[1:])()
    return first.e(), second.e()


def scatter_scratch(rows, width):
    return [
        pltpu.VMEM((4, rows, width), BF16),
        pltpu.VMEM((3, rows, width), BF16),
        pltpu.VMEM((rows, width), BF16),
        pltpu.VMEM((2, rows, width), BF16),
    ]


def sems(count):
    return [pltpu.SemaphoreType.DMA((count,)), pltpu.SemaphoreType.DMA((count,))]


def plane_ring(axis):
    x, y, z, core = place()
    if axis == "x":
        return device(x + 1, y, z, core), device(x + 3, y, z, core)
    return device(x, y, z + 1, core), device(x, y, z + 3, core)


def plane_at(first, u, v):
    return block_of(u, v) if first == "x" else block_of(v, u)


PLANE_GATHER_COPIES = 36
PLANE_SCATTER_COPIES = 36


def gather_plane(copies, out):
    x, y, z, core = place()
    quarter = out.shape[1] // 4
    paths = []
    for first, base in (("x", 0), ("z", 2 * quarter)):
        v, u = (x, z) if first == "x" else (z, x)
        other = "z" if first == "x" else "x"
        paths.append(
            types.SimpleNamespace(
                first=first,
                v=v,
                u=u,
                ring=plane_ring(first),
                cross=plane_ring(other),
                halves=(pl.ds(base, quarter), pl.ds(base + quarter, quarter)),
                whole=pl.ds(base, 2 * quarter),
            )
        )

    def send(path, dv, du, rows, to):
        at = plane_at(path.first, path.v + dv, path.u + du)
        return copies.start(out.at[at, rows], out.at[at, rows], to)

    for path in paths:
        after, before = path.ring
        top, low = path.halves
        path.ta = send(path, 0, 0, top, after)
        path.lb = send(path, 0, 0, low, before)
        path.la = send(path, 0, 0, low, after)
        path.tb = send(path, 0, 0, top, before)
        path.c = {0: [send(path, 0, 0, path.whole, to) for to in path.cross]}
    yield
    for path in paths:
        path.ta.wait_recv()
        path.ft = send(path, 3, 0, path.halves[0], path.ring[0])
        path.lb.wait_recv()
        path.fl = send(path, 1, 0, path.halves[1], path.ring[1])
    yield
    for path in paths:
        path.la.wait_recv()
        path.c[3] = [send(path, 3, 0, path.whole, to) for to in path.cross]
        path.tb.wait_recv()
        path.c[1] = [send(path, 1, 0, path.whole, to) for to in path.cross]
    last = []
    for path in paths:
        path.c[0][0].wait_recv()
        last.append(send(path, 0, 3, path.whole, path.cross[0]))
    yield
    for path in paths:
        path.ft.wait_recv()
        path.fl.wait_recv()
        path.c[2] = [send(path, 2, 0, path.whole, to) for to in path.cross]
    yield
    for path in paths:
        path.c[3][0].wait_recv()
        last.append(send(path, 3, 3, path.whole, path.cross[0]))
        path.c[1][1].wait_recv()
        last.append(send(path, 1, 1, path.whole, path.cross[1]))
    yield
    for path in paths:
        path.c[2][1].wait_recv()
        last.append(send(path, 2, 1, path.whole, path.cross[1]))
    yield
    for path in paths:
        for copy in (path.c[0][1], path.c[3][1], path.c[1][0], path.c[2][0]):
            copy.wait_recv()
    for copy in last:
        copy.wait_recv()


def scatter_plane_scratch(rows, width):
    half = rows // 2
    return [
        pltpu.VMEM((2, 4, half, width), BF16),
        pltpu.VMEM((2, 2, 4, half, width), BF16),
        pltpu.VMEM((2, 4, half, width), BF16),
        pltpu.VMEM((2, 4, half, width), BF16),
        pltpu.VMEM((2, half, width), BF16),
        pltpu.VMEM((2, 2, half, width), BF16),
        pltpu.VMEM((2, 2, half // 2, width), BF16),
    ]


def scatter_plane(copies, part, out, far, near, passed, summed, far2, near2, passed2):
    x, y, z, core = place()
    half = part.shape[1] // 2
    quarter = half // 2
    paths = []
    for at, (first, base) in enumerate((("x", 0), ("z", half))):
        u, v = (x, z) if first == "x" else (z, x)
        other = "z" if first == "x" else "x"
        paths.append(
            types.SimpleNamespace(
                at=at,
                first=first,
                u=u,
                v=v,
                ring=plane_ring(first),
                cross=plane_ring(other),
                rows=pl.ds(base, half),
                base=base,
            )
        )

    def source(path, du, v):
        return (plane_at(path.first, path.u + du, v), path.rows)

    for path in paths:
        at, (after, before) = path.at, path.ring
        path.far = [
            copies.start(
                part.at[source(path, 2, v)], far.at[at, v], after if v < 2 else before
            )
            for v in range(4)
        ]
    for path in paths:
        at, (after, before) = path.at, path.ring
        path.near = [
            copies.start(part.at[source(path, 1, v)], near.at[at, 0, v], after) for v in (2, 3)
        ] + [
            copies.start(part.at[source(path, 3, v)], near.at[at, 1, v], before) for v in (0, 1)
        ]
    yield
    for path in paths:
        at, (after, before) = path.at, path.ring
        for v in (0, 2, 1, 3):
            path.far[v].wait_recv()
            du, slot, to = (1, 0, after) if v < 2 else (3, 1, before)
            own = part[source(path, du, v)].astype(F32)
            passed[at, v] = (own + far[at, v].astype(F32)).astype(BF16)
            path.near.append(copies.start(passed.at[at, v], near.at[at, slot, v], to))
    yield
    for path in paths:
        at = path.at
        for copy in path.near:
            copy.wait_recv()
        for v in range(4):
            own = part[source(path, 0, v)].astype(F32)
            summed[at, v] = (
                own + near[at, 0, v].astype(F32) + near[at, 1, v].astype(F32)
            ).astype(BF16)
        v, (after, before) = path.v, path.cross
        top, low = pl.ds(0, quarter), pl.ds(quarter, quarter)
        v1, v2, v3 = lax.rem(v + 1, 4), lax.rem(v + 2, 4), lax.rem(v + 3, 4)
        path.ft = copies.start(summed.at[at, v2, top], far2.at[at, top], after)
        path.fl = copies.start(summed.at[at, v2, low], far2.at[at, low], before)
        path.last = [
            copies.start(summed.at[at, v1, low], near2.at[at, 0, low], after),
            copies.start(summed.at[at, v3, top], near2.at[at, 1, top], before),
        ]
    yield
    for path in paths:
        at, v, (after, before) = path.at, path.v, path.cross
        top, low = pl.ds(0, quarter), pl.ds(quarter, quarter)
        v1, v3 = lax.rem(v + 1, 4), lax.rem(v + 3, 4)
        path.ft.wait_recv()
        passed2[at, 0] = (summed[at, v1, top].astype(F32) + far2[at, top].astype(F32)).astype(BF16)
        path.last.append(copies.start(passed2.at[at, 0], near2.at[at, 0, top], after))
        path.fl.wait_recv()
        passed2[at, 1] = (summed[at, v3, low].astype(F32) + far2[at, low].astype(F32)).astype(BF16)
        path.last.append(copies.start(passed2.at[at, 1], near2.at[at, 1, low], before))
    yield
    for path in paths:
        at, v = path.at, path.v
        for copy in path.last:
            copy.wait_recv()
        total = summed[at, v].astype(F32) + near2[at, 0].astype(F32) + near2[at, 1].astype(F32)
        out[path.rows] = total.astype(out.dtype)


def params(number):
    return pltpu.CompilerParams(
        collective_id=number, has_side_effects=True, vmem_limit_bytes=56 * 2**20
    )


VMEM = pl.BlockSpec(memory_space=pltpu.VMEM)
HBM = pl.BlockSpec(memory_space=pl.ANY)


def neighbours():
    return [*group_neighbours(), *plane_ring("x"), *plane_ring("z")]


def drain(steps):
    for _ in steps:
        pass


def swap_partner():
    x, y, z, core = place()
    upper = lax.div(x, 2)
    return core != upper, device(core * 2 + lax.rem(x, 2), y, z, upper)


def greet_with_partner(others):
    moves, partner = swap_partner()
    barrier = pltpu.get_barrier_semaphore()
    for other in others:
        pl.semaphore_signal(barrier, inc=1, device_id=other, device_id_type=MESH)

    @pl.when(moves)
    def _():
        pl.semaphore_signal(barrier, inc=1, device_id=partner, device_id_type=MESH)

    pl.semaphore_wait(barrier, len(others) + moves.astype(jnp.int32))


def partner_copy(src, dst, send, recv):
    return pltpu.make_async_remote_copy(
        src_ref=src,
        dst_ref=dst,
        send_sem=send,
        recv_sem=recv,
        device_id=swap_partner()[1],
        device_id_type=MESH,
    )


class Swaps:
    def __init__(self, send, recv):
        self.send, self.recv, self.moves = send, recv, []

    def copy(self, src, dst, own_dst=None):
        at = len(self.moves)
        copy = partner_copy(src, dst, self.send.at[at], self.recv.at[at])
        self.moves.append(copy)
        moves, _ = swap_partner()

        @pl.when(moves)
        def _():
            copy.start()

        @pl.when(jnp.logical_not(moves))
        def _():
            target = dst if own_dst is None else own_dst
            target[...] = src[...]

        return copy

    def arrive(self, copy):
        @pl.when(swap_partner()[0])
        def _():
            copy.wait_recv()

    def finish(self, *arrived):
        @pl.when(swap_partner()[0])
        def _():
            for copy in self.moves:
                copy.wait_send()
                if not any(copy is other for other in arrived):
                    copy.wait_recv()


def start_kernel(
    tokens, w_qkv, w_out, w_in, w_down, row_lengths, b_qv, b_out, b_in, b_down, ln_gain, ln_bias,
    rows_out, own_out, weights_out, attention_out, hidden_first, hidden_later, lengths_out,
    norms_out, bias_in_out, bias_qkv_out, attention, hidden, lengths,
    ssend, srecv, send, recv, wsend, wrecv,
):
    x, y, z, core = place()
    third, width = w_out.shape[2], w_in.shape[2]
    for at in (0, 1):
        for which in range(3):
            attention[at, :, which * third : (which + 1) * third] = w_qkv[at, which]
        attention[at, :, 3 * third :] = w_out[at]
        hidden[at, :, :width] = w_in[at]
        hidden[at, :, width:] = w_down[at]
    lengths[...] = jnp.zeros_like(lengths)
    lengths[0:1, 0:4] = row_lengths[...]
    greet_with_partner(neighbours())
    plane, group, swaps = Copies(wsend, wrecv), Copies(send, recv), Swaps(ssend, srecv)
    there = block_of(core * 2 + lax.rem(x, 2), z)
    own = weights_out.at[block_of(x, z)]
    weights_move = swaps.copy(attention.at[0], weights_out.at[there], own)
    count = tokens.shape[0] // 2
    rows_moves = []
    for half in (pl.ds(0, count), pl.ds(count, count)):
        own = rows_out.at[core * 4 + y, half]
        target = rows_out.at[lax.div(x, 2) * 4 + y, half]
        rows_moves.append(swaps.copy(tokens.at[half], target, own))
    swaps.copy(lengths, lengths_out)
    swaps.arrive(weights_move)
    steps = gather_plane(plane, weights_out)
    next(steps)
    arrivals = [functools.partial(swaps.arrive, move) for move in rows_moves]
    ticks = []

    def tick():
        ticks.append(None)
        next(steps, None)
        if len(ticks) == 3:
            swaps.copy(hidden.at[0], hidden_first)
            swaps.copy(attention.at[1], attention_out)
            swaps.copy(hidden.at[1], hidden_later)

    gather_all(group, rows_out, tick, arrivals)
    own_out[...] = rows_out[core * 4 + y]
    norms_out[0:2] = b_out[...].astype(F32)
    norms_out[2:4] = b_down[...].astype(F32)
    for at in (0, 1):
        norms_out[4 + 2 * at : 6 + 2 * at] = ln_gain[at].astype(F32)
        norms_out[8 + 2 * at : 10 + 2 * at] = ln_bias[at].astype(F32)
    column = core * 4 + y
    own_in = pl.ds(pl.multiple_of(column * width, width), width)
    own_qv = pl.ds(pl.multiple_of(column * third, third), third)
    bias_in_out[...] = b_in[:, own_in].astype(F32)
    for at in (0, 1):
        row = b_qv[at, :, own_qv].astype(F32)
        bias_qkv_out[at : at + 1, :third] = row[0:1]
        bias_qkv_out[at : at + 1, third : 2 * third] = jnp.zeros((1, third), F32)
        bias_qkv_out[at : at + 1, 2 * third :] = row[1:2]
    drain(steps)
    swaps.finish(weights_move, *rows_moves)
    group.wait_sends()
    plane.wait_sends()


def start(tokens, w_qkv, w_out, w_in, w_down, *others):
    rows, width = tokens.shape
    layers, held, hidden_width = w_in.shape
    third = w_out.shape[2]
    columns, hidden_columns = 4 * third, 2 * hidden_width
    shape = jax.ShapeDtypeStruct
    return pl.pallas_call(
        start_kernel,
        out_shape=(
            shape((8, rows, width), BF16),
            shape((rows, width), BF16),
            shape((16, held, columns), BF16),
            shape((held, columns), BF16),
            shape((held, hidden_columns), BF16),
            shape((held, hidden_columns), BF16),
            shape((8, 128), jnp.int32),
            shape((12, width), F32),
            shape((2, hidden_width), F32),
            shape((2, 3 * third), F32),
        ),
        in_specs=[VMEM] * 12,
        out_specs=(VMEM,) * 10,
        scratch_shapes=[
            pltpu.VMEM((layers, held, columns), BF16),
            pltpu.VMEM((layers, held, hidden_columns), BF16),
            pltpu.VMEM((8, 128), jnp.int32),
        ]
        + sems(7)
        + sems(GATHER_COPIES)
        + sems(PLANE_GATHER_COPIES),
        compiler_params=params(0),
        name="start",
    )(tokens, w_qkv, w_out, w_in, w_down, *others)


def normed_parts(stream):
    row_mean = jnp.mean(stream, axis=-1, keepdims=True)
    centered = stream - row_mean
    row_var = jnp.mean(centered * centered, axis=-1, keepdims=True)
    scale = lax.rsqrt(row_var + EPSILON)
    return centered * scale, scale


def norm_pull(unit, scale, gain, grad, sums):
    scaled = grad * gain
    inner = jnp.mean(scaled * unit, axis=-1, keepdims=True)
    pulled = scale * (scaled - jnp.mean(scaled, axis=-1, keepdims=True) - unit * inner)
    low = pulled.astype(BF16)
    sums[0:1] += jnp.sum(grad * unit, axis=0, keepdims=True)
    sums[1:2] += jnp.sum(grad, axis=0, keepdims=True)
    sums[2:3] += jnp.sum(low.astype(F32), axis=0, keepdims=True)
    return pulled, low


INV_SQRT2 = 0.7071067811865476
INV_SQRT_2PI = 0.3989422804014327
CONTRACT_LAST = (((1,), (1,)), ((), ()))
CONTRACT_FIRST = (((0,), (0,)), ((), ()))


def normal_cdf(values):
    return 0.5 * (1.0 + lax.erf(values * INV_SQRT2))


def flatten(block):
    return block.reshape(block.shape[0] * block.shape[1], block.shape[2])


def hidden_forward(ref, hidden_width):
    def work(blocks, rows):
        full_in = flatten(ref.hidden_full[:, :, :hidden_width])
        full_down = flatten(ref.hidden_full[:, :, hidden_width:])
        values = flatten(ref.mlp_input[blocks, rows])
        pre_gelu = jnp.dot(values, full_in, preferred_element_type=F32) + ref.bias_in[ref.layer : ref.layer + 1]
        act = (pre_gelu * normal_cdf(pre_gelu)).astype(BF16)
        branch = lax.dot_general(act, full_down, CONTRACT_LAST, preferred_element_type=F32)
        shape = ref.mlp_input[blocks, rows].shape
        ref.pre_gelu[blocks, rows] = pre_gelu.reshape(*shape[:2], -1)
        ref.act[blocks, rows] = act.reshape(*shape[:2], -1)
        ref.branch_two[blocks, rows] = branch.astype(BF16).reshape(shape)

    return work


def hidden_backward(ref, hidden_width):
    def work(blocks, rows):
        full_in = flatten(ref.hidden_full[:, :, :hidden_width])
        full_down = flatten(ref.hidden_full[:, :, hidden_width:])
        values = flatten(ref.down_full[blocks, rows])
        grad_act = jnp.dot(values, full_down, preferred_element_type=F32)
        pre_gelu = flatten(ref.pre_gelu[blocks, rows])
        slope = normal_cdf(pre_gelu) + pre_gelu * (
            jnp.exp(pre_gelu * pre_gelu * -0.5) * INV_SQRT_2PI
        )
        low = (slope * grad_act).astype(BF16)
        branch = lax.dot_general(low, full_in, CONTRACT_LAST, preferred_element_type=F32)
        shape = ref.down_full[blocks, rows].shape
        ref.pre_low[blocks, rows] = low.reshape(*shape[:2], -1)
        ref.in_sums[0:1] += jnp.sum(low.astype(F32), axis=0, keepdims=True)
        ref.branch_three[blocks, rows] = branch.astype(BF16).reshape(shape)

    return work


def hidden_grads(ref, out):
    pieces = []
    into = out
    hidden_width = into.shape[2] // 2

    def piece(quarter, left, right, base):
        def work():
            values = flatten(left[:, :, quarter * 256 : (quarter + 1) * 256])
            grad = lax.dot_general(
                values, flatten(right[...]), CONTRACT_FIRST, preferred_element_type=F32
            )
            into[quarter * 4 : (quarter + 1) * 4, :, base : base + hidden_width] = grad.astype(
                BF16
            ).reshape(4, 64, hidden_width)

        return work

    for quarter in range(4):
        pieces.append(piece(quarter, ref.down_full, ref.act, hidden_width))
    for quarter in range(4):
        pieces.append(piece(quarter, ref.mlp_input, ref.pre_low, 0))
    return dict(side=pieces)


def param_rows(ref, at, which):
    rows = (2 * which + at, 4 + 2 * at + which, 8 + 2 * at + which)
    return [ref.params[row : row + 1] for row in rows]


def forward_norm(ref, held, at, which, stream_out, normed_out):
    def between(total, rows):
        bias, gain, shift = param_rows(ref, at, which)
        stream = held[rows].astype(F32) + total + bias
        stream_out[rows] = stream
        unit, _ = normed_parts(stream)
        normed = unit * gain + shift
        normed_out[rows] = normed
        return normed.astype(BF16)

    return between


def turn_norm(ref, held, at, which, pulled_out, sums):
    def between(total, rows):
        bias, gain, shift = param_rows(ref, at, which)
        unit, scale = normed_parts(held[rows] + total + bias)
        ref.encoded[rows] = (unit * gain + shift).astype(BF16)
        grad = ref.cotangent[rows].astype(F32)
        pulled, low = norm_pull(unit, scale, gain, grad, sums)
        pulled_out[rows] = pulled
        return low

    return between


def backward_norm(ref, held, at, which, stream, pulled_out, sums):
    def between(total, rows):
        unit, scale = normed_parts(stream[rows])
        grad = held[rows] + total
        pulled, low = norm_pull(unit, scale, param_rows(ref, at, which)[1], grad, sums)
        pulled_out[rows] = pulled
        return low

    return between


def zeroed(ref):
    if not hasattr(ref, "in_sums"):
        return ()
    return (ref.sums_one, ref.sums_two, ref.in_sums)


def chain_call(
    number, name, inputs, outputs, scratch, stages_of,
    gathers=(), scatters=(), swapped=(), late=(), early=(), pace=1, swapped_after=(),
):
    rows, width = 128, 1024
    names_in, names_out, names_scratch = list(inputs), list(outputs), list(scratch)
    stage_count = stages_of({}, True)
    shapes = []
    for key in names_out:
        shape, kind = outputs[key]
        shapes.append(jax.ShapeDtypeStruct(shape, kind))
    scratch_shapes = [pltpu.VMEM(shape, kind) for shape, kind in scratch.values()]
    for _ in range(stage_count):
        scratch_shapes += scatter_scratch(rows, width)
    scratch_shapes += sems(SCATTER_COPIES * stage_count) + sems(GATHER_COPIES * stage_count)
    pieces = [key for sources, _ in scatters for key in sources]
    stored = [key for keys, _ in early for key in keys]
    scratch_shapes += [pltpu.VMEM(inputs[key].shape, inputs[key].dtype) for key in late]
    scratch_shapes += [pltpu.VMEM(*outputs[key]) for key in stored]
    scratch_shapes += [pltpu.SemaphoreType.DMA((len(late) + len(stored) + len(pieces) + 1,))]
    for _ in gathers:
        scratch_shapes += sems(PLANE_GATHER_COPIES)
    for sources, out in scatters:
        kept, columns = {**outputs, **scratch}[out][0]
        scratch_shapes += [pltpu.VMEM((16, kept, columns), BF16)]
        scratch_shapes += sems(PLANE_SCATTER_COPIES) + scatter_plane_scratch(kept, columns)
    if swapped:
        scratch_shapes += sems(len(swapped) + len(swapped_after))

    def kernel(*refs):
        refs = list(refs)
        take = lambda count: [refs.pop(0) for _ in range(count)]
        ref = types.SimpleNamespace()
        held = vars(ref)
        for names in (names_in, names_out, names_scratch):
            held.update(zip(names, take(len(names))))
        bufs = [take(4) for _ in range(stage_count)]
        scatter, gather = Copies(*take(2)), Copies(*take(2))
        far_refs = {key: held[key] for key in (*late, *stored)}
        held.update(zip((*late, *stored), take(len(late) + len(stored))))
        (local,) = take(1)
        fetches, stores, count = [], [], []

        def local_copy(src, dst, kept):
            copy = pltpu.make_async_copy(src, dst, local.at[len(count)])
            copy.start()
            count.append(None)
            kept.append(copy)
            return copy

        for key in late:
            local_copy(far_refs[key], held[key], fetches)

        def after_work(at):
            for keys, stage in early:
                if stage == at:
                    for key in keys:
                        local_copy(held[key], far_refs[key], stores)

        x, y, z, core = place()
        others = neighbours() if gathers or scatters else group_neighbours()
        planes, queue = [], []
        for source, out in gathers:
            plane = Copies(*take(2))
            planes.append(plane)
            queue.append((gather_plane(plane, held[out]), (), True))
        for sources, out in scatters:
            (assembled,) = take(1)
            plane = Copies(*take(2))
            planes.append(plane)
            at, parts = 0, []
            for source in sources:
                columns = pl.ds(at, held[source].shape[-1])
                local_copy(held[source], assembled.at[:, :, columns], parts)
                at += held[source].shape[-1]
            steps = scatter_plane(plane, assembled, held[out], *take(7))
            queue.append((steps, parts, sources))
        stages = stages_of(ref, False)
        for stage, own in zip(stages, bufs):
            stage["bufs"] = own
        if swapped:
            swaps = Swaps(*take(2))
            greet_with_partner(others)
        else:
            greet(others)
        for sums in zeroed(ref):
            sums[...] = jnp.zeros_like(sums)
        for source, out in gathers:
            held[out][block_of(x, z)] = held[source][...]
        started, ended, ticks = [], [], [None] * (pace - 1)

        def tick():
            if not started:
                started.append(True)
                for _, parts, _ in queue:
                    for part in parts:
                        part.wait()
                for source, out in swapped:
                    swaps.copy(held[source], held[out])
            ticks.append(None)
            if len(ticks) % pace:
                return
            advance_planes()

        def advance_planes():
            while queue:
                try:
                    next(queue[0][0])
                    return
                except StopIteration:
                    queue.pop(0)
            if not ended:
                ended.append(True)
                for source, out in swapped_after:
                    swaps.copy(held[source], held[out])

        def before_work():
            if gathers and len(queue) == len(gathers) + len(scatters):
                drain(queue.pop(0)[0])
            for copy in fetches:
                copy.wait()
            fetches.clear()

        run_chain(scatter, gather, stages, tick, before_work, after_work)
        for steps, *_ in queue:
            drain(steps)
        queue.clear()
        advance_planes()
        for copies in (scatter, gather, *planes):
            copies.wait_sends()
        for copy in stores:
            copy.wait()
        if swapped:
            swaps.finish()

    results = pl.pallas_call(
        kernel,
        out_shape=tuple(shapes),
        in_specs=[HBM if key in (*late, *pieces) else VMEM for key in names_in],
        out_specs=tuple(HBM if key in stored else VMEM for key in names_out),
        scratch_shapes=scratch_shapes,
        compiler_params=params(number),
        name=name,
    )(*inputs.values())
    return dict(zip(names_out, results))


def sum_small(copies, small, out, got_x, got_z):
    x, y, z, core = place()
    own = core * 4 + y
    along_x = [device(x + step, y, z, core) for step in (1, 2, 3)]
    along_z = [device(x, y, z + step, core) for step in (1, 2, 3)]
    along_y = [device(x, y + step, z, core) for step in (1, 2, 3)]
    first = [copies.start(small, got_x.at[at], to) for at, to in enumerate(along_x)]
    yield
    for copy in first:
        copy.wait_recv()
    got_z[3] = small[...] + got_x[0] + got_x[1] + got_x[2]
    second = [copies.start(got_z.at[3], got_z.at[at], to) for at, to in enumerate(along_z)]
    yield
    for copy in second:
        copy.wait_recv()
    out[own] = got_z[3] + got_z[0] + got_z[1] + got_z[2]
    third = [copies.start(out.at[own], out.at[own], to) for to in along_y]
    yield
    for copy in third:
        copy.wait_recv()
    held = out.at[pl.ds(core * 4, 4)]
    copies.start(held, held, device(x, y, z, 1 - core)).wait_recv()


def end_kernel(*refs):
    refs = list(refs)
    take = lambda count: [refs.pop(0) for _ in range(count)]
    part, held, *pieces = take(5)
    layer_sums = [take(4), take(4)]
    rows_out, grads_out, small_out = take(3)
    grads, local = take(2)
    bufs, plane_bufs = take(4), take(7)
    rows_stage, grads_stage, small, got_x, got_z = take(5)
    swaps, group, plane, tiny = Swaps(*take(2)), Copies(*take(2)), Copies(*take(2)), Copies(*take(2))
    x, y, z, core = place()
    at, fetches = 0, []
    for number, piece in enumerate(pieces):
        columns = pl.ds(at, piece.shape[2])
        fetches.append(pltpu.make_async_copy(piece, grads.at[:, :, columns], local.at[number]))
        fetches[-1].start()
        at += piece.shape[2]
    small[...] = jnp.zeros_like(small)
    for base, (sums_one, sums_two, qkv_sums, in_sums) in zip((0, 8), layer_sums):
        third, hidden_width = qkv_sums.shape[1] // 3, in_sums.shape[1]
        small[base : base + 3] = sums_one[0:3]
        small[base + 3 : base + 6] = sums_two[0:3]
        small[base + 6 : base + 7, :third] = qkv_sums[0:1, :third]
        small[base + 6 : base + 7, third : 2 * third] = qkv_sums[0:1, 2 * third :]
        small[base + 6 : base + 7, 2 * third : 2 * third + hidden_width] = in_sums[0:1]
    greet_with_partner(
        neighbours()
        + [device(x + 2, y, z, core), device(x, y + 2, z, core), device(x, y, z + 2, core)]
    )
    tiny_steps = sum_small(tiny, small, small_out, got_x, got_z)
    plane_steps = scatter_plane(plane, grads, grads_stage, *plane_bufs)
    ticks = []

    def tick():
        ticks.append(None)
        if len(ticks) == 1:
            next(tiny_steps)
            for copy in fetches:
                copy.wait()
            next(plane_steps)
        elif len(ticks) == 2:
            next(tiny_steps)
        elif len(ticks) == 3:
            next(plane_steps)

    totals = scatter_all(group, part, bufs, tick)
    count = rows_stage.shape[0] // 2
    for at in (0, 1):
        rows = pl.ds(at * count, count)
        rows_stage[rows] = (held[rows] + totals[at]).astype(BF16)
    swaps.copy(rows_stage, rows_out)
    next(plane_steps)
    next(tiny_steps)
    next(plane_steps)
    drain(tiny_steps)
    drain(plane_steps)
    swaps.copy(grads_stage, grads_out)
    swaps.finish()
    group.wait_sends()
    plane.wait_sends()
    tiny.wait_sends()


def end(part, held, pieces, layer_sums):
    rows, width = held.shape
    kept, columns = pieces[0].shape[1], sum(piece.shape[2] for piece in pieces)
    shape = jax.ShapeDtypeStruct
    return pl.pallas_call(
        end_kernel,
        out_shape=(
            shape((rows, width), BF16),
            shape((kept, columns), BF16),
            shape((8, 16, width), F32),
        ),
        in_specs=[VMEM] * 2 + [HBM] * 3 + [VMEM] * 8,
        out_specs=(VMEM,) * 3,
        scratch_shapes=[pltpu.VMEM((16, kept, columns), BF16), pltpu.SemaphoreType.DMA((3,))]
        + scatter_scratch(rows, width)
        + scatter_plane_scratch(kept, columns)
        + [
            pltpu.VMEM((rows, width), BF16),
            pltpu.VMEM((kept, columns), BF16),
            pltpu.VMEM((16, width), F32),
            pltpu.VMEM((3, 16, width), F32),
            pltpu.VMEM((4, 16, width), F32),
        ]
        + sems(2)
        + sems(SCATTER_COPIES)
        + sems(PLANE_SCATTER_COPIES)
        + sems(10),
        compiler_params=params(1),
        name="end",
    )(part, held, *pieces, *layer_sums[0], *layer_sums[1])


def finish_kernel(
    small, zero, one, encoded, rows,
    encoded_out, rows_out, g_qkv, g_b_qv, g_out, g_b_out, g_in, g_b_in, g_down, g_b_down, g_gain, g_shift,
):
    third, hidden_width = g_out.shape[2], g_in.shape[2]
    cut = 4 * third
    encoded_out[...] = encoded[...]
    rows_out[...] = rows[...]
    for at, grads in enumerate((zero, one)):
        for which in range(3):
            columns = slice(which * third, (which + 1) * third)
            g_qkv[at, which] = grads[:, columns].astype(F32)
        g_out[at] = grads[:, 3 * third : cut].astype(F32)
        g_in[at] = grads[:, cut : cut + hidden_width].astype(F32)
        g_down[at] = grads[:, cut + hidden_width :].astype(F32)
        rows = jnp.sum(small[:, at * 8 : at * 8 + 8], axis=0)
        g_gain[at, 0:1], g_shift[at, 0:1], g_b_out[at : at + 1] = rows[0:1], rows[1:2], rows[2:3]
        g_gain[at, 1:2], g_shift[at, 1:2], g_b_down[at : at + 1] = rows[3:4], rows[4:5], rows[5:6]
        for block in range(8):
            row = small[block, at * 8 + 6 : at * 8 + 7]
            columns = slice(block * third, (block + 1) * third)
            g_b_qv[at, 0:1, columns] = row[:, :third]
            g_b_qv[at, 1:2, columns] = row[:, third : 2 * third]
            columns = slice(block * hidden_width, (block + 1) * hidden_width)
            g_b_in[at : at + 1, columns] = row[:, 2 * third : 2 * third + hidden_width]


def finish(small, zero, one, encoded, rows, third):
    kept, hidden_width = zero.shape[0], (zero.shape[1] - 4 * third) // 2
    width = small.shape[2]
    shapes = (
        (2, 3, kept, third),
        (2, 2, width),
        (2, kept, third),
        (2, width),
        (2, kept, hidden_width),
        (2, 8 * hidden_width),
        (2, kept, hidden_width),
        (2, width),
        (2, 2, width),
        (2, 2, width),
    )
    outs = [jax.ShapeDtypeStruct(encoded.shape, BF16)] * 2
    outs += [jax.ShapeDtypeStruct(shape, F32) for shape in shapes]
    return pl.pallas_call(
        finish_kernel,
        out_shape=tuple(outs),
        in_specs=[VMEM] * 5,
        out_specs=(VMEM,) * len(outs),
        compiler_params=pltpu.CompilerParams(vmem_limit_bytes=60 * 2**20),
        name="finish",
    )(small, zero, one, encoded, rows)


HEAD_SCALE = DH ** (-0.5)


def segment_parts(lengths, rows):
    def of(shape, dim):
        positions = lax.broadcasted_iota(jnp.int32, shape, dim)
        end, segments = 0, jnp.zeros(shape, jnp.int32)
        for at in range(4):
            end = end + lengths[0, at]
            segments += (positions >= end).astype(jnp.int32)
        return jnp.where(segments == 4, 4 + positions, segments)

    return of((rows, 1), 0), of((1, rows), 1)


def head_lanes(values, head):
    lanes = lax.broadcasted_iota(jnp.int32, values.shape, 1)
    return jnp.where((lanes >= head * DH) & (lanes < (head + 1) * DH), values, 0)


def pick_heads(parts):
    features = lax.broadcasted_iota(jnp.int32, parts[0].shape, 0)
    return jnp.where(features < DH, parts[0], parts[1])


CHUNK = 1024


def attend_kernel(layer, lengths, rows, weights, bias, qkv_out, context_out, lse_out, branch_out, v_turned, seg_row):
    total, width = rows.shape[0], context_out.shape[1]
    column, row = segment_parts(lengths, total)
    seg_row[...] = jnp.broadcast_to(row, seg_row.shape)

    def chunk(at):
        return pl.ds(pl.multiple_of(at * CHUNK, CHUNK), CHUNK)

    @pl.loop(0, total // CHUNK)
    def _(at):
        r = chunk(at)
        qkv = jnp.dot(rows[r], weights[:, : 3 * width], preferred_element_type=F32)
        qkv_out[r] = (qkv + bias[layer : layer + 1]).astype(BF16)

    keys = qkv_out[:, width : 2 * width]
    v_turned[...] = qkv_out[:, 2 * width :].astype(F32).T.astype(BF16)

    @pl.loop(0, total // CHUNK)
    def _(at):
        r = chunk(at)
        queries = qkv_out[r, :width].astype(F32) * HEAD_SCALE
        allowed = column == seg_row[0:1, r]
        parts = []
        for head in range(2):
            own = head_lanes(queries, head).astype(BF16)
            scores = lax.dot_general(keys, own, CONTRACT_LAST, preferred_element_type=F32)
            scores = jnp.where(allowed, scores, -1e30)
            peak = jnp.max(scores, axis=0, keepdims=True)
            raised = jnp.exp(scores - peak)
            total_row = jnp.sum(raised, axis=0, keepdims=True)
            probs = (raised * (1.0 / total_row)).astype(BF16)
            parts.append(jnp.dot(v_turned[...], probs, preferred_element_type=F32))
            lse_out[head : head + 1, r] = peak + jnp.log(total_row)
        context = pick_heads(parts).T.astype(BF16)
        context_out[r] = context
        branch = lax.dot_general(
            context, weights[:, 3 * width :], CONTRACT_LAST, preferred_element_type=F32
        )
        branch_out[r] = branch.astype(BF16)


def attend(layer, lengths, rows, weights, bias):
    total, width = rows.shape[0], weights.shape[1] // 4
    shape = jax.ShapeDtypeStruct
    return pl.pallas_call(
        functools.partial(attend_kernel, layer),
        out_shape=(
            shape((total, 3 * width), BF16),
            shape((total, width), BF16),
            shape((8, total), F32),
            shape((total, rows.shape[1]), BF16),
        ),
        in_specs=[pl.BlockSpec(memory_space=pltpu.SMEM)] + [VMEM] * 3,
        out_specs=(VMEM,) * 4,
        scratch_shapes=[pltpu.VMEM((width, total), BF16), pltpu.VMEM((8, total), jnp.int32)],
        compiler_params=pltpu.CompilerParams(vmem_limit_bytes=60 * 2**20),
        name="attend",
    )(lengths, rows, weights, bias)


def attend_back_kernel(
    lengths, grad_rows, rows, weights, qkv, context, lse,
    g_qkv, g_out, branch_out, sums_out,
    grad_context, grad_qkv, k_turned, k_sum, v_sum, seg_row,
):
    total, width = rows.shape[0], context.shape[1]
    column, row = segment_parts(lengths, total)
    seg_row[...] = jnp.broadcast_to(row, seg_row.shape)

    def chunk(at):
        return pl.ds(pl.multiple_of(at * CHUNK, CHUNK), CHUNK)

    @pl.loop(0, total // CHUNK)
    def _(at):
        r = chunk(at)
        grad_context[r] = jnp.dot(
            grad_rows[r], weights[:, 3 * width :], preferred_element_type=F32
        ).astype(BF16)

    keys, values = qkv[:, width : 2 * width], qkv[:, 2 * width :]
    k_turned[...] = keys.astype(F32).T.astype(BF16)
    k_sum[...] = jnp.zeros_like(k_sum)
    v_sum[...] = jnp.zeros_like(v_sum)

    @pl.loop(0, total // CHUNK)
    def _(at):
        r = chunk(at)
        queries = qkv[r, :width].astype(F32) * HEAD_SCALE
        grads = grad_context[r].astype(F32)
        allowed = column == seg_row[0:1, r]
        parts = []
        for head in range(2):
            own = head_lanes(queries, head).astype(BF16)
            own_grads = head_lanes(grads, head).astype(BF16)
            scores = lax.dot_general(keys, own, CONTRACT_LAST, preferred_element_type=F32)
            scores = jnp.where(allowed, scores, -1e30)
            probs = jnp.exp(scores - lse[head : head + 1, r])
            grad_probs = lax.dot_general(
                values, own_grads, CONTRACT_LAST, preferred_element_type=F32
            )
            v_sum[...] += jnp.dot(probs.astype(BF16), own_grads, preferred_element_type=F32)
            inner = jnp.sum(probs * grad_probs, axis=0, keepdims=True)
            grad_scores = (probs * (grad_probs - inner)).astype(BF16)
            k_sum[...] += jnp.dot(grad_scores, own, preferred_element_type=F32)
            parts.append(jnp.dot(k_turned[...], grad_scores, preferred_element_type=F32))
        grad_qkv[r, :width] = (pick_heads(parts).T * HEAD_SCALE).astype(BF16)

    grad_qkv[:, width : 2 * width] = k_sum[...].astype(BF16)
    grad_qkv[:, 2 * width :] = v_sum[...].astype(BF16)
    sums_out[...] = jnp.broadcast_to(
        jnp.sum(grad_qkv[...].astype(F32), axis=0, keepdims=True), sums_out.shape
    )

    @pl.loop(0, total // CHUNK)
    def _(at):
        r = chunk(at)
        branch = lax.dot_general(
            grad_qkv[r], weights[:, : 3 * width], CONTRACT_LAST, preferred_element_type=F32
        )
        branch_out[r] = branch.astype(BF16)

    @pl.loop(0, rows.shape[1] // CHUNK)
    def _(at):
        c = chunk(at)
        turned = lax.dot_general(
            grad_qkv[...], rows[:, c], CONTRACT_FIRST, preferred_element_type=F32
        )
        g_qkv[c] = turned.T.astype(BF16)
        turned = lax.dot_general(
            context[...], grad_rows[:, c], CONTRACT_FIRST, preferred_element_type=F32
        )
        g_out[c] = turned.T.astype(BF16)


def attend_back(lengths, grad_rows, rows, weights, qkv, context, lse):
    total, width = context.shape
    depth = rows.shape[1]
    shape = jax.ShapeDtypeStruct
    return pl.pallas_call(
        attend_back_kernel,
        out_shape=(
            shape((depth, 3 * width), BF16),
            shape((depth, width), BF16),
            shape((total, depth), BF16),
            shape((8, 3 * width), F32),
        ),
        in_specs=[pl.BlockSpec(memory_space=pltpu.SMEM)] + [VMEM] * 6,
        out_specs=(VMEM,) * 4,
        scratch_shapes=[
            pltpu.VMEM((total, width), BF16),
            pltpu.VMEM((total, 3 * width), BF16),
            pltpu.VMEM((width, total), BF16),
            pltpu.VMEM((total, width), F32),
            pltpu.VMEM((total, width), F32),
            pltpu.VMEM((8, total), jnp.int32),
        ],
        compiler_params=pltpu.CompilerParams(vmem_limit_bytes=60 * 2**20),
        name="attend_back",
    )(lengths, grad_rows, rows, weights, qkv, context, lse)


def shards(
    tokens,
    lengths,
    w_qkv,
    b_qv,
    w_out,
    b_out,
    w_in,
    b_in,
    w_down,
    b_down,
    ln_gain,
    ln_bias,
    cotangent,
):
    own_rows, width = tokens.shape
    total_rows = own_rows * 8
    layers, kept = w_qkv.shape[:2]
    col_width = w_qkv.shape[3]
    hidden_width = w_in.shape[2]

    (
        rows_zero, hidden, attention_zero, attention_shard, hidden_zero, hidden_one, lengths,
        norm_params, bias_in, bias_qkv,
    ) = start(
        tokens, w_qkv.transpose(0, 2, 1, 3), w_out.transpose(0, 2, 1), w_in,
        w_down.transpose(0, 2, 1), lengths, b_qv, b_out, b_in, b_down, ln_gain, ln_bias,
    )

    own_kind = ((own_rows, width), F32)
    sum_kind = ((8, width), F32)
    low_kind = ((own_rows, width), BF16)
    all_kind = ((8, own_rows, width), BF16)
    act_kind = ((8, own_rows, hidden_width), BF16)
    gelu_kind = ((8, own_rows, hidden_width), F32)
    in_sum_kind = ((8, hidden_width), F32)
    hidden_kind = ((16, kept, 2 * hidden_width), BF16)
    attention_kind = ((16, kept, 4 * col_width), BF16)
    grads_kind = ((kept, 4 * col_width + 2 * hidden_width), BF16)

    def attention(at, rows, full):
        rows, full = rows.reshape(total_rows, width), full.reshape(width, 4 * col_width)
        qkv, context, lse, branch = attend(at, lengths, rows, full, bias_qkv)
        return branch.reshape(all_kind[0]), (rows, full, qkv, context, lse)

    def attention_back(stored, rows):
        grad_rows = rows.reshape(total_rows, width)
        g_qkv, g_out, branch, sums = attend_back(lengths, grad_rows, *stored)
        pieces = (g_qkv.reshape(16, kept, -1), g_out.reshape(16, kept, -1))
        return branch.reshape(all_kind[0]), pieces, sums

    branch, stored_zero = attention(0, rows_zero, attention_zero)

    def zero_stages(ref, counting):
        if counting:
            return 2
        ref.layer = 0
        return [
            dict(
                part=ref.branch,
                rows=ref.mlp_input,
                between=forward_norm(ref, ref.held, 0, 0, ref.first_sum, ref.normed),
                work=hidden_forward(ref, hidden_width),
            ),
            dict(
                part=ref.branch_two,
                rows=ref.rows,
                between=forward_norm(ref, ref.normed, 0, 1, ref.second_sum, ref.hidden),
            ),
        ]

    zero = chain_call(
        2,
        "layer_zero",
        dict(
            branch=branch,
            held=hidden,
            params=norm_params,
            bias_in=bias_in,
            hidden_shard=hidden_zero,
            attention_shard=attention_shard,
            next_cotangent=cotangent,
        ),
        dict(
            first_sum=own_kind,
            second_sum=own_kind,
            hidden=own_kind,
            mlp_input=all_kind,
            pre_gelu=gelu_kind,
            act=act_kind,
            rows=all_kind,
            hidden_full=hidden_kind,
            attention_full=attention_kind,
            moved_cotangent=low_kind,
        ),
        dict(normed=own_kind, branch_two=all_kind),
        zero_stages,
        gathers=(("hidden_shard", "hidden_full"), ("attention_shard", "attention_full")),
        swapped=(("next_cotangent", "moved_cotangent"),),
        early=((("first_sum", "mlp_input", "pre_gelu", "act", "hidden_full"), 0),),
    )

    branch, stored_one = attention(1, zero["rows"], zero["attention_full"])

    def one_stages(ref, counting):
        if counting:
            return 3
        ref.layer = 1
        return [
            dict(
                part=ref.branch,
                rows=ref.mlp_input,
                between=forward_norm(ref, ref.held, 1, 0, ref.first_sum, ref.normed),
                work=hidden_forward(ref, hidden_width),
            ),
            dict(
                part=ref.branch_two,
                rows=ref.down_full,
                between=turn_norm(ref, ref.normed, 1, 1, ref.pulled, ref.sums_two),
                work=hidden_backward(ref, hidden_width),
            ),
            dict(
                part=ref.branch_three,
                rows=ref.rows,
                between=backward_norm(ref, ref.pulled, 1, 0, ref.first_sum, ref.grad_first, ref.sums_one),
                **hidden_grads(ref, ref.grads),
            ),
        ]

    one = chain_call(
        3,
        "layer_one",
        dict(
            branch=branch,
            held=zero["hidden"],
            params=norm_params,
            bias_in=bias_in,
            hidden_shard=hidden_one,
            cotangent=zero["moved_cotangent"],
        ),
        dict(
            encoded=low_kind,
            grad_first=own_kind,
            sums_one=sum_kind,
            sums_two=sum_kind,
            in_sums=in_sum_kind,
            rows=all_kind,
            grads=hidden_kind,
        ),
        dict(
            mlp_input=all_kind,
            act=act_kind,
            down_full=all_kind,
            pre_low=act_kind,
            first_sum=own_kind,
            normed=own_kind,
            pulled=own_kind,
            pre_gelu=gelu_kind,
            hidden_full=hidden_kind,
            branch_two=all_kind,
            branch_three=all_kind,
        ),
        one_stages,
        gathers=(("hidden_shard", "hidden_full"),),
        early=((("encoded",), 1),),
    )
    branch, pieces, qkv_sums_one = attention_back(stored_one, one["rows"])

    def back_stages(ref, counting):
        if counting:
            return 2
        return [
            dict(
                part=ref.branch,
                rows=ref.down_full,
                between=backward_norm(ref, ref.held, 0, 1, ref.second_sum, ref.pulled, ref.sums_two),
                work=hidden_backward(ref, hidden_width),
            ),
            dict(
                part=ref.branch_three,
                rows=ref.rows,
                between=backward_norm(ref, ref.pulled, 0, 0, ref.first_sum, ref.grad_first, ref.sums_one),
                **hidden_grads(ref, ref.grads),
            ),
        ]

    back = chain_call(
        4,
        "layer_back",
        dict(
            branch=branch,
            held=one["grad_first"],
            params=norm_params,
            first_sum=zero["first_sum"],
            second_sum=zero["second_sum"],
            pre_gelu=zero["pre_gelu"],
            hidden_full=zero["hidden_full"],
            mlp_input=zero["mlp_input"],
            act=zero["act"],
            grad_w_qkv=pieces[0],
            grad_w_out=pieces[1],
            grad_hidden=one["grads"],
            own_encoded=one["encoded"],
        ),
        dict(
            grad_first=own_kind,
            sums_one=sum_kind,
            sums_two=sum_kind,
            in_sums=in_sum_kind,
            rows=all_kind,
            moved_grads=grads_kind,
            grads=hidden_kind,
            encoded=low_kind,
        ),
        dict(later_grads=grads_kind, down_full=all_kind, pre_low=act_kind, pulled=own_kind, branch_three=all_kind),
        back_stages,
        scatters=((("grad_w_qkv", "grad_w_out", "grad_hidden"), "later_grads"),),
        swapped=(("own_encoded", "encoded"),),
        swapped_after=(("later_grads", "moved_grads"),),
        late=("pre_gelu", "hidden_full", "mlp_input", "act"),
        pace=2,
    )
    branch, pieces, qkv_sums_zero = attention_back(stored_zero, back["rows"])
    g_tokens, grads_zero, small = end(
        branch,
        back["grad_first"],
        (*pieces, back["grads"]),
        (
            (back["sums_one"], back["sums_two"], qkv_sums_zero, back["in_sums"]),
            (one["sums_one"], one["sums_two"], qkv_sums_one, one["in_sums"]),
        ),
    )
    (
        encoded, g_tokens, g_qkv, g_b_qv, g_out, g_b_out, g_in, g_b_in, g_down, g_b_down, g_gain, g_shift,
    ) = finish(small, grads_zero, back["moved_grads"], back["encoded"], g_tokens, col_width)
    return (
        encoded,
        g_tokens,
        g_qkv.transpose(0, 2, 1, 3),
        g_b_qv,
        g_out.transpose(0, 2, 1),
        g_b_out,
        g_in,
        g_b_in,
        g_down.transpose(0, 2, 1),
        g_b_down,
        g_gain,
        g_shift,
    )


def solution(mesh):
    placed = (
        P(("dp", "tensor"), None),
        P("dp", None),
        P(None, "dp", None, "tensor"),
        P(),
        P(None, "tensor", "dp"),
        P(),
        P(None, "dp", "tensor"),
        P(),
        P(None, "tensor", "dp"),
        P(),
        P(),
        P(),
        P(("dp", "tensor"), None),
    )
    return jax.shard_map(
        shards,
        mesh=mesh,
        in_specs=placed,
        out_specs=(
            P(("dp", "tensor"), None),
            P(("dp", "tensor"), None),
            P(None, "dp", None, "tensor"),
            P(),
            P(None, "tensor", "dp"),
            P(),
            P(None, "dp", "tensor"),
            P(),
            P(None, "tensor", "dp"),
            P(),
            P(),
            P(),
        ),
        check_vma=False,
    )
```
